256 devices in a mesh: dp: 32 (over y, z), proto: 8 (over x, core).
Axes of the slice: x: 4, y: 4, z: 8, core: 2. Of those that a mesh axis runs over, the one named last changes fastest.
Arguments:
- embed: bfloat16 [16384, 1024], P('dp'), may hold values from -3 to 3
- prototypes: bfloat16 [1024, 32768], P(None, 'proto'), may hold values from -2 to 2
- partner: int32 [16384], P('dp'), may hold values from 0 to 16383, as said below
Outputs:
- grad_embed: float32 [16384, 1024], P('dp', 'proto')
- grad_protos: float32 [1024, 32768], P('dp', 'proto')
- view_swapped_cost: float32 [16384], P('dp')
The draws below stay inside these ranges and needn't reach their ends.
Inputs may be any that keep to these rules, and one draw needn't show every extreme that they name: partner(partner(i)) = i and partner(i) != i; partner(i) lies in the same aligned block of 512 rows as i.
All inputs are finite; a program needn't handle non-finite values.
Results may differ from the reference program's by a relative error of at most 0.0015.
Values sent between devices are 32-bit elements; how exact they have to be, the bound alone decides.
No kernel may reach another device: no remote copies, remote signals or barrier semaphores. Data moves between devices by JAX's collectives and lax.ppermute only.
A program may use at most 128 MiB of HBM per device.

```python
import math
import jax
import jax.numpy as jnp
from jax import lax

D = 1024
PROTOS = 32768
ROWS_DEV = 512
SINK_ITERS = 3
ROWS = 16384


def families_count():
    return max(PROTOS // 512, 8)


def family_directions(key):
    return jax.random.normal(key, (D, families_count()), jnp.float32) * (1.0 / math.sqrt(D))


def spread(key, amount, lowest, highest):
    uniform_part = jax.random.uniform(key, (amount,), jnp.float32)
    return jnp.exp(math.log(lowest) + uniform_part * (math.log(highest) - math.log(lowest)))


def draw_prototypes(key, part):
    directions = family_directions(key)
    key = jax.random.fold_in(key, 2)
    own_key, member_key, scale_key = jax.random.split(key, 3)
    member = jax.random.randint(member_key, (PROTOS,), 0, families_count()).astype(jnp.int32)
    shared = jnp.take(directions, member, axis=1)
    own_part = jax.random.normal(own_key, (D, PROTOS), jnp.float32) * (1.0 / math.sqrt(D))
    scales = spread(scale_key, PROTOS, 0.5, 4.0)
    return jnp.clip((own_part + 0.6 * shared) * scales[None, :], -2.0, 2.0).astype(jnp.bfloat16)


def draw_embed(key, part):
    directions = family_directions(key)
    key = jax.random.fold_in(key, 1)
    crowd_key, pick_key, choose_key, jitter_key, scale_key = jax.random.split(key, 5)
    blocks = ROWS // ROWS_DEV
    steps_count = max(blocks - 1, 1)
    crowded = max(families_count() // 16, 1)
    block_of_row = jnp.arange(ROWS, dtype=jnp.int32) // ROWS_DEV
    crowd_roll = jax.random.randint(choose_key, (ROWS,), 0, steps_count).astype(jnp.int32)
    in_crowd = crowd_roll < block_of_row
    crowd_pick = jax.random.randint(crowd_key, (ROWS,), 0, crowded).astype(jnp.int32)
    any_pick = jax.random.randint(pick_key, (ROWS,), 0, families_count()).astype(jnp.int32)
    family = jnp.where(in_crowd, crowd_pick, any_pick)
    centres = jnp.take(directions, family, axis=1).T
    mixed_order = (block_of_row * 13 % blocks).astype(jnp.float32) / float(steps_count)
    jitter_width = 1.2 + 0.8 * mixed_order
    jitter = jax.random.normal(jitter_key, (ROWS, D), jnp.float32) * (1.0 / math.sqrt(D))
    scales = spread(scale_key, ROWS, 0.5, 4.0)
    values = (centres + jitter * jitter_width[:, None]) * scales[:, None]
    return jnp.clip(values, -3.0, 3.0).astype(jnp.bfloat16)


def draw_partner(key, part):
    key = jax.random.fold_in(key, 7)
    blocks = ROWS // ROWS_DEV
    orders = jax.vmap(lambda sub_key: jax.random.permutation(sub_key, ROWS_DEV))(jax.random.split(key, blocks))
    orders = orders.astype(jnp.int32)
    first_half = orders[:, 0::2]
    second_half = orders[:, 1::2]
    block_rows = jnp.arange(blocks, dtype=jnp.int32)[:, None]
    local_mate = jnp.zeros((blocks, ROWS_DEV), jnp.int32)
    local_mate = local_mate.at[block_rows, first_half].set(second_half)
    local_mate = local_mate.at[block_rows, second_half].set(first_half)
    offsets = jnp.arange(blocks, dtype=jnp.int32)[:, None] * ROWS_DEV
    return (local_mate + offsets).reshape(ROWS).astype(jnp.int32)


def setup_inputs(seed: int = 0) -> dict:
    arg_keys = jax.random.split(jax.random.key(seed), 4)
    embed = draw_embed(jax.random.fold_in(arg_keys[3], 71), 0)
    prototypes = draw_prototypes(jax.random.fold_in(arg_keys[3], 71), 0)
    partner = draw_partner(jax.random.fold_in(arg_keys[3], 71), 0)
    return dict(embed=embed, prototypes=prototypes, partner=partner)


code_eps = 0.05
sharpness_divisor = 0.1

def reference(embed, prototypes, partner):
    highest = lax.Precision.HIGHEST
    raw_embed = embed.astype(jnp.float32)
    embed_scale = lax.rsqrt(lax.optimization_barrier(jnp.sum(raw_embed * raw_embed, axis=1)) + 1e-06)
    unit_embed = (raw_embed * embed_scale[:, None]).astype(jnp.bfloat16)
    raw_protos = prototypes.astype(jnp.float32)
    proto_scale = lax.rsqrt(lax.optimization_barrier(jnp.sum(raw_protos * raw_protos, axis=0)) + 1e-06)
    unit_protos = (raw_protos * proto_scale[None, :]).astype(jnp.bfloat16)
    cluster_score_matrix = jnp.dot(unit_embed, unit_protos, preferred_element_type=jnp.float32)
    similarity_matrix = jnp.exp(cluster_score_matrix / code_eps)
    sample_factor = jnp.ones((ROWS,), jnp.float32)
    column_factor = jnp.ones((PROTOS,), jnp.float32)
    for sweep_index in range(SINK_ITERS):
        column_factor = 1.0 / jnp.dot(sample_factor, similarity_matrix, precision=highest)
        sample_factor = 1.0 / jnp.dot(similarity_matrix, column_factor, precision=highest)

    def block_step(running, block_index):
        first_row = (block_index * ROWS_DEV).astype(jnp.int32)
        tile_score_matrix = lax.dynamic_slice_in_dim(cluster_score_matrix, first_row, ROWS_DEV, 0)
        block_embed = lax.dynamic_slice_in_dim(unit_embed, first_row, ROWS_DEV, 0)
        companion_view_position = lax.dynamic_slice_in_dim(partner, first_row, ROWS_DEV, 0)
        balanced_assignments = jnp.take(similarity_matrix, companion_view_position, axis=0) * column_factor[None, :] * jnp.take(sample_factor, companion_view_position)[:, None]
        exponentiated_scores = jnp.exp(tile_score_matrix / sharpness_divisor)
        normalizer_total = lax.optimization_barrier(jnp.sum(exponentiated_scores, axis=1))
        mismatch_summand = lax.optimization_barrier(jnp.sum(balanced_assignments * tile_score_matrix, axis=1))
        view_swapped_cost = jnp.log(normalizer_total) - mismatch_summand / sharpness_divisor
        score_derivative = ((exponentiated_scores / normalizer_total[:, None] - balanced_assignments) / sharpness_divisor).astype(jnp.bfloat16)
        embed_term = lax.dot_general(score_derivative, unit_protos, (((1,), (1,)), ((), ())), preferred_element_type=jnp.float32)
        partial_grad = lax.dot_general(block_embed, score_derivative, (((0,), (0,)), ((), ())), preferred_element_type=jnp.float32)
        return (running + partial_grad, (embed_term, view_swapped_cost))
    block_ids = jnp.arange(ROWS // ROWS_DEV, dtype=jnp.int32)
    grad_protos, (embed_term, view_swapped_cost) = lax.scan(block_step, jnp.zeros((D, PROTOS), jnp.float32), block_ids)
    embed_term = embed_term.reshape(ROWS, D)
    view_swapped_cost = view_swapped_cost.reshape(ROWS)
    inner_sum = lax.optimization_barrier(jnp.sum(raw_embed * embed_term, axis=1))
    cubed = embed_scale * embed_scale * embed_scale
    grad_embed = embed_scale[:, None] * embed_term - (cubed * inner_sum)[:, None] * raw_embed
    return (grad_embed, grad_protos, view_swapped_cost)
```

```python
import functools

import jax
import jax.numpy as jnp
from jax import lax
from jax.experimental import pallas as pl
from jax.experimental.pallas import tpu as pltpu
from jax.sharding import PartitionSpec as P

SINK_ITERS = 3
NY, NZ, NX = 4, 8, 4
ROWS, COLS, D = 512, 4096, 1024
F32, BF16 = jnp.float32, jnp.bfloat16
MIB = 1 << 20


code_eps = 0.05
sharpness_divisor = 0.1


def dp_pairs(f):
    pairs = []
    for y in range(NY):
        for z in range(NZ):
            to_y, to_z = f(y, z)
            pairs.append((y * NZ + z, (to_y % NY) * NZ + to_z % NZ))
    return pairs


def proto_pairs(f):
    pairs = []
    for x in range(NX):
        for core in range(2):
            to_x, to_core = f(x, core)
            pairs.append((x * 2 + core, (to_x % NX) * 2 + to_core % 2))
    return pairs


def move_y(v, off):
    return lax.ppermute(v, "dp", dp_pairs(lambda y, z: (y + off, z)))


def move_z(v, off):
    return lax.ppermute(v, "dp", dp_pairs(lambda y, z: (y, z + off)))


def move_x(v, off):
    return lax.ppermute(v, "proto", proto_pairs(lambda x, c: (x + off, c)))


def move_core(v):
    return lax.ppermute(v, "proto", proto_pairs(lambda x, c: (x, c + 1)))


def sum_y(v):
    return (v + move_y(v, 2)) + (move_y(v, 1) + move_y(v, -1))


def sum_z(v):
    v = v + lax.ppermute(v, "dp", dp_pairs(lambda y, z: (y, z ^ 1)))
    return (v + move_z(v, 4)) + (move_z(v, 2) + move_z(v, -2))


def sum_x(v):
    return (v + move_x(v, 2)) + (move_x(v, 1) + move_x(v, -1))


def sum_core(v):
    return v + move_core(v)


def sum_dp(v):
    return sum_z(sum_y(v))


def sum_proto(v):
    return sum_x(sum_core(v))


def scores_kernel(embed_ref, protos_ref, affinity_ref, scores_ref, col_ref, unit_ref):
    @pl.when(pl.program_id(0) == 0)
    def _():
        raw = embed_ref[...].astype(F32)
        scale = lax.rsqrt(jnp.sum(raw * raw, axis=1, keepdims=True) + 1e-06)
        unit_ref[...] = (raw * scale).astype(BF16)

    raw = protos_ref[...].astype(F32)
    scale = lax.rsqrt(jnp.sum(raw * raw, axis=0, keepdims=True) + 1e-06)
    unit_protos = (raw * scale).astype(BF16)
    scores = jnp.dot(unit_ref[...], unit_protos, preferred_element_type=F32)
    affinity = jnp.exp(scores / code_eps)
    scores_ref[...] = scores
    width = scores.shape[1]
    at = pl.ds(pl.multiple_of(pl.program_id(0) * width, width), width)
    affinity_ref[:, at] = affinity
    col_ref[:, at] = jnp.sum(affinity, axis=0, keepdims=True)


def first_scores(embed, prototypes, block=512):
    return pl.pallas_call(
        scores_kernel,
        grid=(COLS // block,),
        in_specs=[
            pl.BlockSpec((ROWS, D), lambda j: (0, 0)),
            pl.BlockSpec((D, block), lambda j: (0, j)),
        ],
        out_specs=[
            pl.BlockSpec(memory_space=pltpu.VMEM),
            pl.BlockSpec((ROWS, block), lambda j: (0, j)),
            pl.BlockSpec(memory_space=pltpu.VMEM),
        ],
        out_shape=[
            pltpu.VMEM((ROWS, COLS), F32),
            jax.ShapeDtypeStruct((ROWS, COLS), F32),
            jax.ShapeDtypeStruct((1, COLS), F32),
        ],
        scratch_shapes=[pltpu.VMEM((ROWS, D), BF16)],
        compiler_params=pltpu.CompilerParams(vmem_limit_bytes=40 * MIB),
        cost_estimate=pl.CostEstimate(
            flops=2 * ROWS * COLS * D, bytes_accessed=18 * MIB, transcendentals=ROWS * COLS
        ),
        name="first_scores",
    )(embed, prototypes)


def row_kernel(affinity_ref, col_total_ref, row_ref):
    weight = 1.0 / col_total_ref[...]
    rows = 64
    parts = []
    for i in range(ROWS // rows):
        total = jnp.zeros((rows, 128), F32)
        for j in range(COLS // 128):
            total += affinity_ref[i * rows : (i + 1) * rows, j * 128 : (j + 1) * 128] * weight[
                :, j * 128 : (j + 1) * 128
            ]
        parts.append(total)
    row_ref[...] = jnp.sum(jnp.concatenate(parts, axis=0).T, axis=0, keepdims=True)


def row_sums(affinity, col_total):
    return pl.pallas_call(
        row_kernel,
        in_specs=[pl.BlockSpec(memory_space=pltpu.VMEM)] * 2,
        out_specs=pl.BlockSpec(memory_space=pltpu.VMEM),
        out_shape=jax.ShapeDtypeStruct((1, ROWS), F32),
        compiler_params=pltpu.CompilerParams(vmem_limit_bytes=24 * MIB),
        cost_estimate=pl.CostEstimate(
            flops=2 * ROWS * COLS, bytes_accessed=8 * MIB, transcendentals=0
        ),
        name="row_sums",
    )(pltpu.with_memory_space_constraint(affinity, pltpu.VMEM), col_total)


def col_kernel(affinity_ref, row_total_ref, col_ref, weight_ref):
    weight = 1.0 / row_total_ref[...]
    weight_ref[...] = jnp.broadcast_to(weight, (128, ROWS)).T
    for j in range(COLS // 128):
        col_ref[:, j * 128 : (j + 1) * 128] = jnp.sum(
            affinity_ref[:, j * 128 : (j + 1) * 128] * weight_ref[...], axis=0, keepdims=True
        )


def col_sums(affinity, row_total):
    return pl.pallas_call(
        col_kernel,
        in_specs=[pl.BlockSpec(memory_space=pltpu.VMEM)] * 2,
        out_specs=pl.BlockSpec(memory_space=pltpu.VMEM),
        out_shape=jax.ShapeDtypeStruct((1, COLS), F32),
        scratch_shapes=[pltpu.VMEM((ROWS, 128), F32)],
        compiler_params=pltpu.CompilerParams(vmem_limit_bytes=24 * MIB),
        cost_estimate=pl.CostEstimate(
            flops=2 * ROWS * COLS, bytes_accessed=8 * MIB, transcendentals=0
        ),
        name="col_sums",
    )(pltpu.with_memory_space_constraint(affinity, pltpu.VMEM), row_total)


def local(embed, prototypes, partner):
    affinity, scores, col_part = first_scores(embed, prototypes)
    col_total = row_total = row_part = None
    for sweep in range(SINK_ITERS):
        if sweep:
            col_part = col_sums(affinity, row_total)
        col_total = sum_dp(col_part)
        row_part = row_sums(affinity, col_total)
        row_total = sum_proto(row_part)

    raw_embed = embed.astype(F32)
    embed_scale = lax.rsqrt(jnp.sum(raw_embed * raw_embed, axis=1) + 1e-06)
    unit_embed = (raw_embed * embed_scale[:, None]).astype(BF16)
    raw_protos = prototypes.astype(F32)
    proto_scale = lax.rsqrt(jnp.sum(raw_protos * raw_protos, axis=0) + 1e-06)
    unit_protos = (raw_protos * proto_scale[None, :]).astype(BF16)
    mate = partner - lax.axis_index("dp") * ROWS
    column_factor = 1.0 / col_total
    sample_factor = 1.0 / row_total.reshape(ROWS)
    exponentiated = jnp.exp(scores / sharpness_divisor)
    targets = (
        jnp.take(affinity, mate, axis=0) * column_factor * jnp.take(sample_factor, mate)[:, None]
    )
    denominator, mismatch = lax.psum(
        (jnp.sum(exponentiated, axis=1), jnp.sum(targets * scores, axis=1)), "proto"
    )
    cost = jnp.log(denominator) - mismatch / sharpness_divisor
    grad_scores = (
        (exponentiated / denominator[:, None] - targets) / sharpness_divisor
    ).astype(BF16)
    grad_protos = lax.psum_scatter(
        lax.dot_general(
            unit_embed, grad_scores, (((0,), (0,)), ((), ())), preferred_element_type=F32
        ),
        "dp",
        scatter_dimension=0,
        tiled=True,
    )
    embed_term = lax.dot_general(
        grad_scores, unit_protos, (((1,), (1,)), ((), ())), preferred_element_type=F32
    )
    inner = jnp.sum(raw_embed * embed_term, axis=1)
    cubed = embed_scale * embed_scale * embed_scale
    grad_embed = lax.psum_scatter(
        embed_scale[:, None] * embed_term - (cubed * inner)[:, None] * raw_embed,
        "proto",
        scatter_dimension=1,
        tiled=True,
    )
    return (grad_embed, grad_protos, cost)


def solution(mesh):
    placed = (P("dp", None), P(None, "proto"), P("dp"))
    return jax.shard_map(
        local,
        mesh=mesh,
        in_specs=placed,
        out_specs=(P("dp", "proto"), P("dp", "proto"), P("dp")),
        check_vma=False,
    )
```

```python
import functools

import jax
import jax.numpy as jnp
from jax import lax
from jax.experimental import pallas as pl
from jax.experimental.pallas import tpu as pltpu
from jax.sharding import PartitionSpec as P

SINK_ITERS = 3
NY, NZ, NX = 4, 8, 4
ROWS, COLS, D = 512, 4096, 1024
WIDE, QUARTER, PAY = 2048, 1024, 264
F32, BF16 = jnp.float32, jnp.bfloat16
MIB = 1 << 20


code_eps = 0.05
sharpness_divisor = 0.1


def dp_pairs(f):
    pairs = []
    for y in range(NY):
        for z in range(NZ):
            to_y, to_z = f(y, z)
            pairs.append((y * NZ + z, (to_y % NY) * NZ + to_z % NZ))
    return pairs


def proto_pairs(f):
    pairs = []
    for x in range(NX):
        for core in range(2):
            to_x, to_core = f(x, core)
            pairs.append((x * 2 + core, (to_x % NX) * 2 + to_core % 2))
    return pairs


def move_y(v, off):
    return lax.ppermute(v, "dp", dp_pairs(lambda y, z: (y + off, z)))


def move_z(v, off):
    return lax.ppermute(v, "dp", dp_pairs(lambda y, z: (y, z + off)))


def move_x(v, off):
    return lax.ppermute(v, "proto", proto_pairs(lambda x, c: (x + off, c)))


def move_core(v):
    return lax.ppermute(v, "proto", proto_pairs(lambda x, c: (x, c + 1)))


def sum_y(v):
    return (v + move_y(v, 2)) + (move_y(v, 1) + move_y(v, -1))


def sum_z(v):
    v = v + lax.ppermute(v, "dp", dp_pairs(lambda y, z: (y, z ^ 1)))
    return (v + move_z(v, 4)) + (move_z(v, 2) + move_z(v, -2))


def sum_x(v):
    return (v + move_x(v, 2)) + (move_x(v, 1) + move_x(v, -1))


def sum_core(v):
    return v + move_core(v)


def sum_dp(v):
    return sum_z(sum_y(v))


def sum_proto(v):
    return sum_x(sum_core(v))


def in_vmem(v):
    return pltpu.with_memory_space_constraint(v, pltpu.VMEM)


VM = pl.BlockSpec(memory_space=pltpu.VMEM)


def params(mib):
    return pltpu.CompilerParams(vmem_limit_bytes=mib * MIB)


def cost(flops, mib, exps=0):
    return pl.CostEstimate(flops=flops, bytes_accessed=mib * MIB, transcendentals=exps)


def scores_kernel(
    place, embed_ref, mate_ref, protos_ref, exps_ref, scores_ref, col_ref, protos_out, unit_ref, pay_ref
):
    @pl.when(pl.program_id(0) == 0)
    def _():
        raw = embed_ref[...].astype(F32)
        scale = lax.rsqrt(jnp.sum(raw * raw, axis=1, keepdims=True) + 1e-06)
        unit_ref[...] = (raw * scale).astype(BF16)
        half = pl.ds(pl.multiple_of(place[3] * (ROWS // 2), ROWS // 2), ROWS // 2)
        pay_ref[: ROWS // 2, :] = unit_ref[half, :].astype(F32)
        pay_ref[ROWS // 2 :, :ROWS] = jnp.broadcast_to(mate_ref[...], (8, ROWS))
        pay_ref[ROWS // 2 :, ROWS:] = jnp.zeros((8, D - ROWS), F32)

    raw = protos_ref[...].astype(F32)
    scale = lax.rsqrt(jnp.sum(raw * raw, axis=0, keepdims=True) + 1e-06)
    unit_protos = (raw * scale).astype(BF16)
    protos_out[...] = unit_protos
    scores = jnp.dot(unit_ref[...], unit_protos, preferred_element_type=F32)
    exps = jnp.exp(scores * (1.0 / sharpness_divisor))
    scores_ref[...] = scores
    width = scores.shape[1]
    at = pl.ds(pl.multiple_of(pl.program_id(0) * width, width), width)
    exps_ref[:, at] = exps
    col_ref[:, at] = jnp.sum(exps * exps, axis=0, keepdims=True)


def first_scores(place, embed, mate, prototypes, block=512):
    return pl.pallas_call(
        scores_kernel,
        grid_spec=pltpu.PrefetchScalarGridSpec(
            num_scalar_prefetch=1,
            grid=(COLS // block,),
            in_specs=[
                pl.BlockSpec((ROWS, D), lambda j, p: (0, 0)),
                VM,
                pl.BlockSpec((D, block), lambda j, p: (0, j)),
            ],
            out_specs=[
                VM,
                pl.BlockSpec((ROWS, block), lambda j, p: (0, j)),
                VM,
                pl.BlockSpec((D, block), lambda j, p: (0, j)),
                VM,
                VM,
            ],
        ),
        out_shape=[
            pltpu.VMEM((ROWS, COLS), F32),
            jax.ShapeDtypeStruct((ROWS, COLS), F32),
            jax.ShapeDtypeStruct((1, COLS), F32),
            jax.ShapeDtypeStruct((D, COLS), BF16),
            pltpu.VMEM((ROWS, D), BF16),
            jax.ShapeDtypeStruct((PAY, D), F32),
        ],
        compiler_params=params(40),
        cost_estimate=cost(2 * ROWS * COLS * D, 26, ROWS * COLS),
        name="first_scores",
    )(place, embed, mate, prototypes)


def lanes_to_row(parts):
    return jnp.sum(jnp.concatenate(parts, axis=0).T, axis=0, keepdims=True)


def row_kernel(with_plain, exps_ref, col_total_ref, row_ref):
    weight = 1.0 / col_total_ref[...]
    rows = 64
    parts, plain_parts = [], []
    for i in range(ROWS // rows):
        total = jnp.zeros((rows, 128), F32)
        plain = jnp.zeros((rows, 128), F32)
        for j in range(COLS // 128):
            e = exps_ref[i * rows : (i + 1) * rows, j * 128 : (j + 1) * 128]
            total += (e * e) * weight[:, j * 128 : (j + 1) * 128]
            if with_plain:
                plain += e
        parts.append(total)
        plain_parts.append(plain)
    row_ref[0:1, :] = lanes_to_row(parts)
    if with_plain:
        row_ref[1:2, :] = lanes_to_row(plain_parts)


def row_sums(exps, col_total, with_plain):
    return pl.pallas_call(
        functools.partial(row_kernel, with_plain),
        in_specs=[VM, VM],
        out_specs=VM,
        out_shape=jax.ShapeDtypeStruct((2 if with_plain else 1, ROWS), F32),
        compiler_params=params(12),
        cost_estimate=cost(3 * ROWS * COLS, 1),
        name="row_sums",
    )(in_vmem(exps), col_total)


def mate_row_kernel(a0, a1, a2, a3, col_total_ref, row_ref):
    weight = 1.0 / col_total_ref[...]
    rows = 64
    parts = []
    for i in range(ROWS // rows):
        total = jnp.zeros((rows, 128), F32)
        for q, a in enumerate((a0, a1, a2, a3)):
            for j in range(QUARTER // 128):
                at = q * QUARTER + j * 128
                total += (
                    a[i * rows : (i + 1) * rows, j * 128 : (j + 1) * 128] * weight[:, at : at + 128]
                )
        parts.append(total)
    row_ref[...] = lanes_to_row(parts)


def mate_row_sums(mates, col_total):
    return pl.pallas_call(
        mate_row_kernel,
        in_specs=[VM] * 5,
        out_specs=VM,
        out_shape=jax.ShapeDtypeStruct((1, ROWS), F32),
        compiler_params=params(12),
        cost_estimate=cost(2 * ROWS * COLS, 1),
        name="mate_row_sums",
    )(*[in_vmem(m) for m in mates], col_total)


def col_kernel(exps_ref, row_total_ref, col_ref, weight_ref):
    weight = 1.0 / row_total_ref[0:1, :]
    weight_ref[...] = jnp.broadcast_to(weight, (128, ROWS)).T
    for j in range(COLS // 128):
        e = exps_ref[:, j * 128 : (j + 1) * 128]
        col_ref[:, j * 128 : (j + 1) * 128] = jnp.sum(
            (e * e) * weight_ref[...], axis=0, keepdims=True
        )


def col_sums(exps, row_total):
    return pl.pallas_call(
        col_kernel,
        in_specs=[VM, VM],
        out_specs=VM,
        out_shape=jax.ShapeDtypeStruct((1, COLS), F32),
        scratch_shapes=[pltpu.VMEM((ROWS, 128), F32)],
        compiler_params=params(12),
        cost_estimate=cost(3 * ROWS * COLS, 1),
        name="col_sums",
    )(in_vmem(exps), row_total)


def mate_rows(x, mate):
    pick = (lax.broadcasted_iota(jnp.int32, (ROWS, ROWS), 0).astype(F32) == mate).astype(BF16)
    return jnp.dot(pick, x, preferred_element_type=F32).astype(BF16)


def block_out(place, x, mate, protos_ref, exps_ref, mates_ref, turned_ref, turn):
    protos = protos_ref[...]
    exps_ref[...] = jnp.exp(
        jnp.dot(x, protos, preferred_element_type=F32) * (1.0 / sharpness_divisor)
    )
    xm = mate_rows(x, mate)
    mates_ref[...] = jnp.exp(jnp.dot(xm, protos, preferred_element_type=F32) * (1.0 / code_eps))
    turn[...] = x.astype(F32).T
    for o in range(NZ):
        for p in range(NY):
            to = lax.rem(place[0] + p, NY) * NZ + lax.rem(place[1] + o, NZ)
            rows = turn[pl.ds(pl.multiple_of(to * 32, 32), 32), :]
            at = o * 128 + p * 32
            turned_ref[at : at + 32, :] = rows.astype(BF16)
    return xm


def own_block_kernel(
    place, unit_ref, mate_ref, protos_ref, exps_ref, mates_ref, turned_ref, xm_ref, turn
):
    xm_ref[...] = block_out(
        place, unit_ref[...], mate_ref[...], protos_ref, exps_ref, mates_ref, turned_ref, turn
    )


def far_block_kernel(
    place, same_ref, other_ref, protos_ref, exps_ref, mates_ref, turned_ref, turn, held
):
    half = ROWS // 2
    core = place[3]
    held[pl.ds(pl.multiple_of(core * half, half), half), :] = same_ref[:half, :].astype(BF16)
    held[pl.ds(pl.multiple_of((1 - core) * half, half), half), :] = other_ref[:half, :].astype(BF16)
    block_out(
        place,
        held[...],
        same_ref[half : half + 1, :ROWS],
        protos_ref,
        exps_ref,
        mates_ref,
        turned_ref,
        turn,
    )


def block_call(place, a, b, protos, own):
    shapes = [
        pltpu.VMEM((ROWS, QUARTER), F32),
        pltpu.VMEM((ROWS, QUARTER), F32),
        pltpu.VMEM((D, ROWS), BF16),
    ]
    scratch = [pltpu.VMEM((D, ROWS), F32)]
    if own:
        shapes.append(pltpu.VMEM((ROWS, D), BF16))
    else:
        scratch.append(pltpu.VMEM((ROWS, D), BF16))
    return pl.pallas_call(
        own_block_kernel if own else far_block_kernel,
        grid_spec=pltpu.PrefetchScalarGridSpec(
            num_scalar_prefetch=1,
            grid=(1,),
            in_specs=[VM, VM, pl.BlockSpec((D, QUARTER), lambda i, p: (0, p[0]))],
            out_specs=[VM] * len(shapes),
            scratch_shapes=scratch,
        ),
        out_shape=shapes,
        compiler_params=params(24),
        cost_estimate=cost(4 * ROWS * QUARTER * D, 4, 2 * ROWS * QUARTER),
        name="own_block" if own else "far_block",
    )(place, in_vmem(a) if own else a, b, protos)


def mate_piece_kernel(xm_ref, protos_ref, mates_ref):
    mates_ref[...] = jnp.exp(
        jnp.dot(xm_ref[...], protos_ref[...], preferred_element_type=F32) * (1.0 / code_eps)
    )


def mate_piece(xm, protos, q):
    return pl.pallas_call(
        mate_piece_kernel,
        grid=(1,),
        in_specs=[VM, pl.BlockSpec((D, QUARTER), lambda i: (0, q))],
        out_specs=VM,
        out_shape=pltpu.VMEM((ROWS, QUARTER), F32),
        compiler_params=params(16),
        cost_estimate=cost(2 * ROWS * QUARTER * D, 2, ROWS * QUARTER),
        name="mate_piece",
    )(in_vmem(xm), protos)


def down(row):
    return jnp.broadcast_to(row, (128, ROWS)).T


def embed_grad_kernel(
    place,
    exps_ref,
    a0,
    a1,
    a2,
    a3,
    col_total_ref,
    row_total_ref,
    plain_ref,
    embed_ref,
    scores_ref,
    protos_ref,
    mine_ref,
    other_ref,
    soft,
    hard,
    match,
    grads,
    total,
):
    step = pl.program_id(0)

    @pl.when(step == 0)
    def _():
        soft[...] = down((1.0 / sharpness_divisor) / plain_ref[...])
        hard[...] = down(1.0 / row_total_ref[...])
        match[...] = jnp.zeros_like(match)
        total[...] = jnp.zeros_like(total)

    for q, mates in enumerate((a0, a1, a2, a3)):

        @pl.when(step == q)
        def _():
            for j in range(QUARTER // 128):
                lanes = slice(j * 128, (j + 1) * 128)
                at = slice(q * QUARTER + j * 128, q * QUARTER + (j + 1) * 128)
                targets = mates[:, lanes] * (1.0 / col_total_ref[:, at]) * hard[...]
                match[...] += targets * scores_ref[:, lanes]
                grads[:, lanes] = (
                    exps_ref[:, at] * soft[...] - targets * (1.0 / sharpness_divisor)
                ).astype(BF16)

    total[...] += lax.dot_general(
        grads[...], protos_ref[...], (((1,), (1,)), ((), ())), preferred_element_type=F32
    )

    @pl.when(step == COLS // QUARTER - 1)
    def _():
        raw = embed_ref[...].astype(F32)
        term = total[...]
        scale = lax.rsqrt(jnp.sum(raw * raw, axis=1, keepdims=True) + 1e-06)
        inner = jnp.sum(raw * term, axis=1, keepdims=True)
        total[...] = scale * term - (scale * scale * scale * inner) * raw
        matched = jnp.sum(match[...].T, axis=0, keepdims=True)
        for o in range(NX):
            to = lax.rem(place[2] + o, NX) * 2
            for core, ref in ((place[3], mine_ref), (1 - place[3], other_ref)):
                at = pl.ds(pl.multiple_of((to + core) * 128, 128), 128)
                ref[o, :ROWS, :] = total[:, at]
                ref[o, ROWS:, :] = jnp.zeros((8, 128), F32)
                for t in range(ROWS // 128):
                    ref[o, ROWS + t : ROWS + t + 1, :] = matched[:, t * 128 : (t + 1) * 128]


def embed_grad(place, exps, mates, col_total, row_total, plain, embed, scores, protos):
    out = jax.ShapeDtypeStruct((NX, ROWS + 8, 128), F32)
    return pl.pallas_call(
        embed_grad_kernel,
        grid_spec=pltpu.PrefetchScalarGridSpec(
            num_scalar_prefetch=1,
            grid=(COLS // QUARTER,),
            in_specs=[VM] * 9
            + [
                pl.BlockSpec((ROWS, QUARTER), lambda j, p: (0, j)),
                pl.BlockSpec((D, QUARTER), lambda j, p: (0, j)),
            ],
            out_specs=[VM, VM],
            scratch_shapes=[
                pltpu.VMEM((ROWS, 128), F32),
                pltpu.VMEM((ROWS, 128), F32),
                pltpu.VMEM((ROWS, 128), F32),
                pltpu.VMEM((ROWS, QUARTER), BF16),
                pltpu.VMEM((ROWS, D), F32),
            ],
        ),
        out_shape=[out, out],
        compiler_params=params(24),
        cost_estimate=cost(2 * ROWS * COLS * D, 18),
        name="embed_grad",
    )(
        place,
        in_vmem(exps),
        *[in_vmem(m) for m in mates],
        col_total,
        row_total,
        plain,
        embed,
        scores,
        protos,
    )


def first_chunk_kernel(place, *refs):
    exps, mates, scals = refs[0:4], refs[4:8], refs[8:12]
    turned, col_total_ref = refs[12:16], refs[16]
    grads, chunk_a, chunk_b = refs[17:20]
    at = pl.ds(pl.multiple_of(place[0] * QUARTER, QUARTER), QUARTER)
    weight = (1.0 / sharpness_divisor) / col_total_ref[:, at]
    total = None
    for b in range(NY):
        soft = down((1.0 / sharpness_divisor) / scals[b][1:2, :])
        hard = down(1.0 / scals[b][0:1, :])
        for j in range(QUARTER // 128):
            lanes = slice(j * 128, (j + 1) * 128)
            grads[b * ROWS : (b + 1) * ROWS, lanes] = (
                exps[b][:, lanes] * soft - mates[b][:, lanes] * weight[:, lanes] * hard
            ).astype(BF16)
        part = jnp.dot(
            turned[b][4 * 128 : 5 * 128, :],
            grads[b * ROWS : (b + 1) * ROWS, :],
            preferred_element_type=F32,
        )
        total = part if total is None else total + part
    chunk_a[...] = total[:, : QUARTER // 2]
    chunk_b[...] = total[:, QUARTER // 2 :]


def first_chunk(place, exps, mates, scals, turned, col_total):
    half = jax.ShapeDtypeStruct((128, QUARTER // 2), F32)
    return pl.pallas_call(
        first_chunk_kernel,
        in_specs=[pl.BlockSpec(memory_space=pltpu.SMEM)] + [VM] * 17,
        out_specs=[VM] * 3,
        out_shape=[pltpu.VMEM((WIDE, QUARTER), BF16), half, half],
        compiler_params=params(20),
        cost_estimate=cost(2 * 128 * WIDE * QUARTER + 6 * WIDE * QUARTER, 2),
        name="first_chunk",
    )(
        place,
        *[in_vmem(v) for v in exps],
        *[in_vmem(v) for v in mates],
        *scals,
        *[in_vmem(v) for v in turned],
        col_total,
    )


def chunks_kernel(offsets, t0, t1, t2, t3, grads, *outs):
    for o, out in zip(offsets, outs):
        total = None
        for b, turned in enumerate((t0, t1, t2, t3)):
            part = jnp.dot(
                turned[o * 128 : (o + 1) * 128, :],
                grads[b * ROWS : (b + 1) * ROWS, :],
                preferred_element_type=F32,
            )
            total = part if total is None else total + part
        out[...] = total


def chunks(turned, grads, offsets):
    return pl.pallas_call(
        functools.partial(chunks_kernel, offsets),
        in_specs=[VM] * 5,
        out_specs=[VM] * len(offsets),
        out_shape=[jax.ShapeDtypeStruct((128, QUARTER), F32)] * len(offsets),
        compiler_params=params(20),
        cost_estimate=cost(2 * 128 * WIDE * QUARTER * len(offsets), 1),
        name="chunks",
    )(*[in_vmem(v) for v in turned], in_vmem(grads))


def gather_kernel(place, r0, r1, r2, r3, out_ref):
    for o, ref in enumerate((r0, r1, r2, r3)):
        quarter = lax.rem(place[0] + NY - o, NY)
        out_ref[:, pl.ds(pl.multiple_of(quarter * QUARTER, QUARTER), QUARTER)] = ref[...]


def gather_quarters(place, quarters):
    return pl.pallas_call(
        gather_kernel,
        in_specs=[pl.BlockSpec(memory_space=pltpu.SMEM)] + [VM] * 4,
        out_specs=VM,
        out_shape=jax.ShapeDtypeStruct((32, COLS), F32),
        compiler_params=params(8),
        cost_estimate=cost(0, 1),
        name="gather_quarters",
    )(place, *quarters)


def local(embed, prototypes, partner):
    dp, proto = lax.axis_index("dp"), lax.axis_index("proto")
    place = jnp.stack([dp // NZ, dp % NZ, proto // 2, proto % 2]).astype(jnp.int32)
    mate = (partner - dp * ROWS).astype(F32).reshape(1, ROWS)
    exps, scores, col_part, protos, unit, pay = first_scores(place, embed, mate, prototypes)

    from_left, from_right = move_y(pay, 1), move_y(pay, -1)
    far = jnp.concatenate([move_y(from_left[:128], 1), move_y(from_right[128:], -1)], axis=0)
    same = [from_left, far, from_right]

    col_total = sum_dp(col_part)
    row_total = sum_proto(row_sums(exps, col_total, True))
    plain = row_total[1:2]
    blocks = [block_call(place, unit, mate, protos, True)]
    xm = blocks[0][3]
    mates = [mate_piece(xm, protos, q) for q in range(NY)]
    for sweep in range(1, SINK_ITERS):
        col_total = sum_dp(col_sums(exps, row_total))
        if sweep + 1 < SINK_ITERS:
            row_total = sum_proto(row_sums(exps, col_total, False))
    blocks += [block_call(place, v, move_core(v), protos, False) for v in same]
    row_total = sum_proto(mate_row_sums(mates, col_total))

    scal = jnp.concatenate([row_total, plain], axis=0)
    scals = [scal, move_y(scal, 1), move_y(scal, 2), move_y(scal, -1)]

    mine, other = embed_grad(
        place, exps, mates, col_total, row_total, plain, embed, scores, protos
    )

    turned = [b[2] for b in blocks]
    grads, up, back = first_chunk(
        place, [b[0] for b in blocks], [b[1] for b in blocks], scals, turned, col_total
    )
    half = QUARTER // 2
    up, back = move_z(up, 1), move_z(back, -1)
    c3, c5 = chunks(turned, grads, (3, 5))
    up = jnp.concatenate([c3[:, :half] + up, c3[:, half:]], axis=1)
    back = jnp.concatenate([c5[:, :half], c5[:, half:] + back], axis=1)
    up, back = move_z(up, 1), move_z(back, -1)
    c2, c6 = chunks(turned, grads, (2, 6))
    up, back = move_z(up + c2, 1), move_z(back + c6, -1)
    c1, c7 = chunks(turned, grads, (1, 7))
    up, back = move_z(up + c1, 1), move_z(back + c7, -1)
    (c0,) = chunks(turned, grads, (0,))
    done = c0 + up + back
    grad_protos = gather_quarters(
        place, [done[:32]] + [move_y(done[32 * o : 32 * o + 32], o) for o in (1, 2, 3)]
    )

    shares = mine + move_core(other)
    share = (shares[0] + move_x(shares[2], 2)) + (move_x(shares[1], 1) + move_x(shares[3], -1))
    matched = share[ROWS : ROWS + ROWS // 128].reshape(ROWS)
    view_swapped_cost = jnp.log(plain.reshape(ROWS)) - matched / sharpness_divisor
    return (share[:ROWS], grad_protos, view_swapped_cost)


def solution(mesh):
    placed = (P("dp", None), P(None, "proto"), P("dp"))
    return jax.shard_map(
        local,
        mesh=mesh,
        in_specs=placed,
        out_specs=(P("dp", "proto"), P("dp", "proto"), P("dp")),
        check_vma=False,
    )
```

```python
import functools

import jax
import jax.numpy as jnp
from jax import lax
from jax.experimental import pallas as pl
from jax.experimental.pallas import tpu as pltpu
from jax.sharding import PartitionSpec as P

NY, NZ, NX = 4, 8, 4
ROWS, COLS, D = 512, 4096, 1024
WIDE, QUARTER, PAY = 2048, 1024, 264
F32, BF16 = jnp.float32, jnp.bfloat16
MIB = 1 << 20


code_eps = 0.05
sharpness_divisor = 0.1


def dp_pairs(f):
    pairs = []
    for y in range(NY):
        for z in range(NZ):
            to_y, to_z = f(y, z)
            pairs.append((y * NZ + z, (to_y % NY) * NZ + to_z % NZ))
    return pairs


def proto_pairs(f):
    pairs = []
    for x in range(NX):
        for core in range(2):
            to_x, to_core = f(x, core)
            pairs.append((x * 2 + core, (to_x % NX) * 2 + to_core % 2))
    return pairs


def move_y(v, off):
    return lax.ppermute(v, "dp", dp_pairs(lambda y, z: (y + off, z)))


def move_z(v, off):
    return lax.ppermute(v, "dp", dp_pairs(lambda y, z: (y, z + off)))


def move_x(v, off):
    return lax.ppermute(v, "proto", proto_pairs(lambda x, c: (x + off, c)))


def move_core(v):
    return lax.ppermute(v, "proto", proto_pairs(lambda x, c: (x, c + 1)))


def sum_y(v):
    return (v + move_y(v, 2)) + (move_y(v, 1) + move_y(v, -1))


def sum_z(v):
    before, after = move_z(v, 1), move_z(v, -1)
    two = v + after
    three = before + two
    return three + (move_z(three, -3) + move_z(two, 3))


def sum_x(v):
    return (v + move_x(v, 2)) + (move_x(v, 1) + move_x(v, -1))


def sum_core(v):
    return v + move_core(v)


def sum_dp(v):
    return sum_z(sum_y(v))


def sum_proto(v):
    return sum_x(sum_core(v))


def in_vmem(v):
    return pltpu.with_memory_space_constraint(v, pltpu.VMEM)


def in_hbm(v):
    return pltpu.with_memory_space_constraint(v, pltpu.HBM)


VM = pl.BlockSpec(memory_space=pltpu.VMEM)
ANY = pl.BlockSpec(memory_space=pl.ANY)


def params(mib):
    return pltpu.CompilerParams(vmem_limit_bytes=mib * MIB)


def cost(flops, mib, exps=0):
    return pl.CostEstimate(flops=flops, bytes_accessed=mib * MIB, transcendentals=exps)


def scores_kernel(
    place, embed_ref, mate_ref, protos_ref, exps_ref, scores_ref, col_ref, protos_out, unit_ref, pay_ref
):
    @pl.when(pl.program_id(0) == 0)
    def _():
        raw = embed_ref[...].astype(F32)
        scale = lax.rsqrt(jnp.sum(raw * raw, axis=1, keepdims=True) + 1e-06)
        unit_ref[...] = (raw * scale).astype(BF16)
        half = pl.ds(pl.multiple_of(place[3] * (ROWS // 2), ROWS // 2), ROWS // 2)
        pay_ref[: ROWS // 2, :] = unit_ref[half, :].astype(F32)
        pay_ref[ROWS // 2 :, :ROWS] = jnp.broadcast_to(mate_ref[...], (8, ROWS))
        pay_ref[ROWS // 2 :, ROWS:] = jnp.zeros((8, D - ROWS), F32)

    raw = protos_ref[...].astype(F32)
    scale = lax.rsqrt(jnp.sum(raw * raw, axis=0, keepdims=True) + 1e-06)
    unit_protos = (raw * scale).astype(BF16)
    protos_out[...] = unit_protos
    scores = jnp.dot(unit_ref[...], unit_protos, preferred_element_type=F32)
    exps = jnp.exp(scores * (1.0 / sharpness_divisor))
    scores_ref[...] = scores
    width = scores.shape[1]
    at = pl.ds(pl.multiple_of(pl.program_id(0) * width, width), width)
    exps_ref[:, at] = exps
    col_ref[:, at] = jnp.sum(exps * exps, axis=0, keepdims=True)


def first_scores(place, embed, mate, prototypes, block=512):
    return pl.pallas_call(
        scores_kernel,
        grid_spec=pltpu.PrefetchScalarGridSpec(
            num_scalar_prefetch=1,
            grid=(COLS // block,),
            in_specs=[
                pl.BlockSpec((ROWS, D), lambda j, p: (0, 0)),
                VM,
                pl.BlockSpec((D, block), lambda j, p: (0, j)),
            ],
            out_specs=[
                VM,
                pl.BlockSpec((ROWS, block), lambda j, p: (0, j)),
                VM,
                pl.BlockSpec((D, block), lambda j, p: (0, j)),
                VM,
                VM,
            ],
        ),
        out_shape=[
            pltpu.VMEM((ROWS, COLS), F32),
            jax.ShapeDtypeStruct((ROWS, COLS), F32),
            jax.ShapeDtypeStruct((1, COLS), F32),
            jax.ShapeDtypeStruct((D, COLS), BF16),
            pltpu.VMEM((ROWS, D), BF16),
            jax.ShapeDtypeStruct((PAY, D), F32),
        ],
        compiler_params=params(40),
        cost_estimate=cost(2 * ROWS * COLS * D, 26, ROWS * COLS),
        name="first_scores",
    )(place, embed, mate, prototypes)


def lanes_to_row(parts):
    return jnp.sum(jnp.concatenate(parts, axis=0).T, axis=0, keepdims=True)


def row_kernel(with_plain, exps_ref, col_total_ref, *refs):
    row_ref = refs[-1]
    weight = 1.0 / col_total_ref[...]
    rows = 64
    parts, plain_parts = [], []
    for i in range(ROWS // rows):
        total = jnp.zeros((rows, 128), F32)
        plain = jnp.zeros((rows, 128), F32)
        for j in range(COLS // 128):
            e = exps_ref[i * rows : (i + 1) * rows, j * 128 : (j + 1) * 128]
            total += (e * e) * weight[:, j * 128 : (j + 1) * 128]
            if with_plain:
                plain += e
        parts.append(total)
        plain_parts.append(plain)
    row_ref[0:1, :] = lanes_to_row(parts)
    if with_plain:
        row_ref[1:2, :] = lanes_to_row(plain_parts)


def row_sums(exps, col_total, with_plain, after):
    return pl.pallas_call(
        functools.partial(row_kernel, with_plain),
        in_specs=[VM, VM] + [ANY] * len(after),
        out_specs=VM,
        out_shape=jax.ShapeDtypeStruct((2 if with_plain else 1, ROWS), F32),
        compiler_params=params(6),
        cost_estimate=cost(3 * ROWS * COLS, 1),
        name="row_sums",
    )(in_vmem(exps), col_total, *after)


def mate_row_kernel(a0, a1, a2, a3, col_total_ref, *refs):
    row_ref = refs[-1]
    weight = 1.0 / col_total_ref[...]
    rows = 64
    parts = []
    for i in range(ROWS // rows):
        total = jnp.zeros((rows, 128), F32)
        for q, a in enumerate((a0, a1, a2, a3)):
            for j in range(QUARTER // 128):
                at = q * QUARTER + j * 128
                total += (
                    a[i * rows : (i + 1) * rows, j * 128 : (j + 1) * 128] * weight[:, at : at + 128]
                )
        parts.append(total)
    row_ref[...] = lanes_to_row(parts)


def mate_row_sums(mates, col_total, after):
    return pl.pallas_call(
        mate_row_kernel,
        in_specs=[VM] * 5 + [ANY] * len(after),
        out_specs=VM,
        out_shape=jax.ShapeDtypeStruct((1, ROWS), F32),
        compiler_params=params(6),
        cost_estimate=cost(2 * ROWS * COLS, 1),
        name="mate_row_sums",
    )(*[in_vmem(m) for m in mates], col_total, *after)


def col_kernel(exps_ref, row_total_ref, *refs):
    col_ref, weight_ref = refs[-2:]
    weight = 1.0 / row_total_ref[0:1, :]
    weight_ref[...] = jnp.broadcast_to(weight, (128, ROWS)).T
    for j in range(COLS // 128):
        e = exps_ref[:, j * 128 : (j + 1) * 128]
        col_ref[:, j * 128 : (j + 1) * 128] = jnp.sum(
            (e * e) * weight_ref[...], axis=0, keepdims=True
        )


def col_sums(exps, row_total, early, after):
    return pl.pallas_call(
        col_kernel,
        in_specs=[VM, VM] + [VM] * len(early) + [ANY] * len(after),
        out_specs=VM,
        out_shape=jax.ShapeDtypeStruct((1, COLS), F32),
        scratch_shapes=[pltpu.VMEM((ROWS, 128), F32)],
        compiler_params=params(6),
        cost_estimate=cost(3 * ROWS * COLS, 1),
        name="col_sums",
    )(in_vmem(exps), row_total, *[in_vmem(v) for v in early], *after)


def mate_rows(x, mate):
    pick = (lax.broadcasted_iota(jnp.int32, (ROWS, ROWS), 0).astype(F32) == mate).astype(BF16)
    return jnp.dot(pick, x, preferred_element_type=F32).astype(BF16)


def block_out(place, x, mate, protos_ref, exps_ref, mates_ref, turned_ref, turn):
    protos = protos_ref[...]
    exps_ref[...] = jnp.exp(
        jnp.dot(x, protos, preferred_element_type=F32) * (1.0 / sharpness_divisor)
    )
    xm = mate_rows(x, mate)
    mates_ref[...] = jnp.exp(jnp.dot(xm, protos, preferred_element_type=F32) * (1.0 / code_eps))
    turn[...] = x.astype(F32).T
    for o in range(NZ):
        for p in range(NY):
            to = lax.rem(place[0] + p, NY) * NZ + lax.rem(place[1] + o, NZ)
            rows = turn[pl.ds(pl.multiple_of(to * 32, 32), 32), :]
            at = o * 128 + p * 32
            turned_ref[at : at + 32, :] = rows.astype(BF16)
    return xm


def own_block_kernel(
    place, unit_ref, mate_ref, protos_ref, exps_ref, mates_ref, turned_ref, xm_ref, turn
):
    xm_ref[...] = block_out(
        place, unit_ref[...], mate_ref[...], protos_ref, exps_ref, mates_ref, turned_ref, turn
    )


def far_block_kernel(
    place, same_ref, other_ref, protos_ref, exps_ref, mates_ref, turned_ref, flag_ref, turn, held
):
    flag_ref[...] = jnp.zeros_like(flag_ref)
    half = ROWS // 2
    core = place[3]
    held[pl.ds(pl.multiple_of(core * half, half), half), :] = same_ref[:half, :].astype(BF16)
    held[pl.ds(pl.multiple_of((1 - core) * half, half), half), :] = other_ref[:half, :].astype(BF16)
    block_out(
        place,
        held[...],
        same_ref[half : half + 1, :ROWS],
        protos_ref,
        exps_ref,
        mates_ref,
        turned_ref,
        turn,
    )


def block_call(place, a, b, protos, own):
    shapes = [
        pltpu.VMEM((ROWS, QUARTER), F32),
        pltpu.VMEM((ROWS, QUARTER), F32),
        pltpu.VMEM((D, ROWS), BF16),
    ]
    scratch = [pltpu.VMEM((D, ROWS), F32)]
    if own:
        shapes.append(pltpu.VMEM((ROWS, D), BF16))
    else:
        shapes.append(jax.ShapeDtypeStruct((1, 128), F32))
        scratch.append(pltpu.VMEM((ROWS, D), BF16))
    return pl.pallas_call(
        own_block_kernel if own else far_block_kernel,
        grid_spec=pltpu.PrefetchScalarGridSpec(
            num_scalar_prefetch=1,
            grid=(1,),
            in_specs=[VM, VM, pl.BlockSpec((D, QUARTER), lambda i, p: (0, p[0]))],
            out_specs=[VM] * len(shapes),
            scratch_shapes=scratch,
        ),
        out_shape=shapes,
        compiler_params=params(14),
        cost_estimate=cost(4 * ROWS * QUARTER * D, 4, 2 * ROWS * QUARTER),
        name="own_block" if own else "far_block",
    )(place, in_vmem(a) if own else a, b, in_hbm(protos))


def mate_piece_kernel(xm_ref, protos_ref, mates_ref):
    mates_ref[...] = jnp.exp(
        jnp.dot(xm_ref[...], protos_ref[...], preferred_element_type=F32) * (1.0 / code_eps)
    )


def mate_piece(xm, protos, q):
    return pl.pallas_call(
        mate_piece_kernel,
        grid=(1,),
        in_specs=[VM, pl.BlockSpec((D, QUARTER), lambda i: (0, q))],
        out_specs=VM,
        out_shape=pltpu.VMEM((ROWS, QUARTER), F32),
        compiler_params=params(16),
        cost_estimate=cost(2 * ROWS * QUARTER * D, 2, ROWS * QUARTER),
        name="mate_piece",
    )(in_vmem(xm), in_hbm(protos))


def down(row):
    return jnp.broadcast_to(row, (128, ROWS)).T


def embed_grad_kernel(part, place, *refs):
    refs = refs[2:]
    if part == 0:
        m0, m1, col_total_ref, row_total_ref, plain_ref, scores_ref, protos_ref = refs[:7]
        total, match, soft, hard, grads = refs[7:]
    else:
        m0, m1, col_total_ref, row_total_ref, plain_ref = refs[:5]
        total_in, match_in, embed_ref, scores_ref, protos_ref = refs[5:10]
        mine_ref, other_ref, total, match, soft, hard, grads = refs[10:]
    step = pl.program_id(0)

    @pl.when(step == 0)
    def _():
        soft[...] = down((1.0 / sharpness_divisor) / plain_ref[...])
        hard[...] = down(1.0 / row_total_ref[...])
        match[...] = jnp.zeros_like(match) if part == 0 else match_in[...]
        total[...] = jnp.zeros_like(total) if part == 0 else total_in[...]

    for q, mates in enumerate((m0, m1)):

        @pl.when(step == q)
        def _():
            for j in range(QUARTER // 128):
                lanes = slice(j * 128, (j + 1) * 128)
                first = (2 * part + q) * QUARTER + j * 128
                weight = 1.0 / col_total_ref[:, first : first + 128]
                targets = mates[:, lanes] * weight * hard[...]
                scores = scores_ref[:, lanes]
                match[...] += targets * scores
                grads[:, lanes] = (
                    jnp.exp(scores * (1.0 / sharpness_divisor)) * soft[...]
                    - targets * (1.0 / sharpness_divisor)
                ).astype(BF16)

    total[...] += lax.dot_general(
        grads[...], protos_ref[...], (((1,), (1,)), ((), ())), preferred_element_type=F32
    )

    if part == 1:

        @pl.when(step == 1)
        def _():
            raw = embed_ref[...].astype(F32)
            term = total[...]
            scale = lax.rsqrt(jnp.sum(raw * raw, axis=1, keepdims=True) + 1e-06)
            inner = jnp.sum(raw * term, axis=1, keepdims=True)
            total[...] = scale * term - (scale * scale * scale * inner) * raw
            matched = jnp.sum(match[...].T, axis=0, keepdims=True)
            for o in range(NX):
                to = lax.rem(place[2] + o, NX) * 2
                for core, ref in ((place[3], mine_ref), (1 - place[3], other_ref)):
                    at = pl.ds(pl.multiple_of((to + core) * 128, 128), 128)
                    ref[o, :ROWS, :] = total[:, at]
                    ref[o, ROWS:, :] = jnp.zeros((8, 128), F32)
                    for t in range(ROWS // 128):
                        ref[o, ROWS + t : ROWS + t + 1, :] = matched[:, t * 128 : (t + 1) * 128]


def embed_grad(part, place, after, mates, col_total, row_total, plain, more, scores, protos):
    column = pltpu.VMEM((ROWS, 128), F32)
    sums = [pltpu.VMEM((ROWS, D), F32), column]
    scratch = [column, column, pltpu.VMEM((ROWS, QUARTER), BF16)]
    if part == 0:
        shapes = sums
    else:
        shapes = [jax.ShapeDtypeStruct((NX, ROWS + 8, 128), F32)] * 2
        scratch = sums + scratch
        more = [in_vmem(more[0]), in_vmem(more[1]), more[2]]
    return pl.pallas_call(
        functools.partial(embed_grad_kernel, part),
        grid_spec=pltpu.PrefetchScalarGridSpec(
            num_scalar_prefetch=1,
            grid=(2,),
            in_specs=[ANY] * 2
            + [VM] * (5 + len(more))
            + [
                pl.BlockSpec((ROWS, QUARTER), lambda j, p: (0, 2 * part + j)),
                pl.BlockSpec((D, QUARTER), lambda j, p: (0, 2 * part + j)),
            ],
            out_specs=[VM, VM],
            scratch_shapes=scratch,
        ),
        out_shape=shapes,
        compiler_params=params(18),
        cost_estimate=cost(ROWS * COLS * D, 9, ROWS * COLS // 2),
        name="embed_grad",
    )(
        place,
        *after,
        *[in_vmem(m) for m in mates],
        col_total,
        row_total,
        plain,
        *more,
        in_hbm(scores),
        in_hbm(protos),
    )


def first_chunk_kernel(place, *refs):
    exps, mates, scals = refs[0:4], refs[4:8], refs[8:12]
    turned, col_total_ref = refs[12:16], refs[16]
    grads, chunk_a, chunk_b = refs[17:20]
    at = pl.ds(pl.multiple_of(place[0] * QUARTER, QUARTER), QUARTER)
    weight = (1.0 / sharpness_divisor) / col_total_ref[:, at]
    total = None
    for b in range(NY):
        soft = down((1.0 / sharpness_divisor) / scals[b][1:2, :])
        hard = down(1.0 / scals[b][0:1, :])
        for j in range(QUARTER // 128):
            lanes = slice(j * 128, (j + 1) * 128)
            grads[b * ROWS : (b + 1) * ROWS, lanes] = (
                exps[b][:, lanes] * soft - mates[b][:, lanes] * weight[:, lanes] * hard
            ).astype(BF16)
        part = jnp.dot(
            turned[b][4 * 128 : 5 * 128, :],
            grads[b * ROWS : (b + 1) * ROWS, :],
            preferred_element_type=F32,
        )
        total = part if total is None else total + part
    chunk_a[...] = total[:, : QUARTER // 2]
    chunk_b[...] = total[:, QUARTER // 2 :]


def first_chunk(place, exps, mates, scals, turned, col_total):
    half = jax.ShapeDtypeStruct((128, QUARTER // 2), F32)
    return pl.pallas_call(
        first_chunk_kernel,
        in_specs=[pl.BlockSpec(memory_space=pltpu.SMEM)] + [VM] * 17,
        out_specs=[VM] * 3,
        out_shape=[pltpu.VMEM((WIDE, QUARTER), BF16), half, half],
        compiler_params=params(12),
        cost_estimate=cost(2 * 128 * WIDE * QUARTER + 6 * WIDE * QUARTER, 2),
        name="first_chunk",
    )(
        place,
        *[in_vmem(v) for v in exps],
        *[in_vmem(v) for v in mates],
        *scals,
        *[in_vmem(v) for v in turned],
        col_total,
    )


def chunks_kernel(offsets, t0, t1, t2, t3, grads, *outs):
    for o, out in zip(offsets, outs):
        total = None
        for b, turned in enumerate((t0, t1, t2, t3)):
            part = jnp.dot(
                turned[o * 128 : (o + 1) * 128, :],
                grads[b * ROWS : (b + 1) * ROWS, :],
                preferred_element_type=F32,
            )
            total = part if total is None else total + part
        out[...] = total


def chunks(turned, grads, offsets):
    return pl.pallas_call(
        functools.partial(chunks_kernel, offsets),
        in_specs=[VM] * 5,
        out_specs=[VM] * len(offsets),
        out_shape=[jax.ShapeDtypeStruct((128, QUARTER), F32)] * len(offsets),
        compiler_params=params(10),
        cost_estimate=cost(2 * 128 * WIDE * QUARTER * len(offsets), 1),
        name="chunks",
    )(*[in_vmem(v) for v in turned], in_vmem(grads))


def gather_kernel(place, r0, r1, r2, r3, out_ref):
    for o, ref in enumerate((r0, r1, r2, r3)):
        quarter = lax.rem(place[0] + NY - o, NY)
        out_ref[:, pl.ds(pl.multiple_of(quarter * QUARTER, QUARTER), QUARTER)] = ref[...]


def gather_quarters(place, quarters):
    return pl.pallas_call(
        gather_kernel,
        in_specs=[pl.BlockSpec(memory_space=pltpu.SMEM)] + [VM] * 4,
        out_specs=VM,
        out_shape=jax.ShapeDtypeStruct((32, COLS), F32),
        compiler_params=params(8),
        cost_estimate=cost(0, 1),
        name="gather_quarters",
    )(place, *quarters)


def local(embed, prototypes, partner):
    dp, proto = lax.axis_index("dp"), lax.axis_index("proto")
    place = jnp.stack([dp // NZ, dp % NZ, proto // 2, proto % 2]).astype(jnp.int32)
    mate = (partner - dp * ROWS).astype(F32).reshape(1, ROWS)
    exps, scores, col_part, protos, unit, pay = first_scores(place, embed, mate, prototypes)

    from_left, from_right = move_y(pay, 1), move_y(pay, -1)
    far = jnp.concatenate([move_y(from_left[:128], 1), move_y(from_right[128:], -1)], axis=0)
    same = [from_left, far, from_right]

    col_total = sum_dp(col_part)
    row_total = sum_proto(row_sums(exps, col_total, True, [from_left, from_right]))
    plain = row_total[1:2]
    blocks = [block_call(place, unit, mate, protos, True)]
    xm = blocks[0][3]
    mates = [mate_piece(xm, protos, q) for q in range(NY)]
    crossed = [move_core(v) for v in same]
    blocks += [block_call(place, v, w, protos, False) for v, w in zip(same, crossed)]

    col_total = sum_dp(col_sums(exps, row_total, [], []))
    row_total = sum_proto(row_sums(exps, col_total, False, [far]))
    col_total = sum_dp(col_sums(exps, row_total, mates, crossed))
    row_total = sum_proto(mate_row_sums(mates, col_total, [b[3] for b in blocks[1:]]))

    scal = jnp.concatenate([row_total, plain], axis=0)
    scals = [scal, move_y(scal, 1), move_y(scal, 2), move_y(scal, -1)]

    turned = [b[2] for b in blocks]
    grads, up, back = first_chunk(
        place, [b[0] for b in blocks], [b[1] for b in blocks], scals, turned, col_total
    )
    half = QUARTER // 2
    up, back = move_z(up, 1), move_z(back, -1)
    c3, c5 = chunks(turned, grads, (3, 5))
    sums = embed_grad(
        0, place, (up, back), mates[:2], col_total, row_total, plain, [], scores, protos
    )
    up = jnp.concatenate([c3[:, :half] + up, c3[:, half:]], axis=1)
    back = jnp.concatenate([c5[:, :half], c5[:, half:] + back], axis=1)
    up, back = move_z(up, 1), move_z(back, -1)
    c2, c6 = chunks(turned, grads, (2, 6))
    mine, other = embed_grad(
        1,
        place,
        (up, back),
        mates[2:],
        col_total,
        row_total,
        plain,
        [*sums, embed],
        scores,
        protos,
    )
    up, back = move_z(up + c2, 1), move_z(back + c6, -1)
    c1, c7 = chunks(turned, grads, (1, 7))
    up, back = move_z(up + c1, 1), move_z(back + c7, -1)
    (c0,) = chunks(turned, grads, (0,))
    done = c0 + up + back
    grad_protos = gather_quarters(
        place, [done[:32]] + [move_y(done[32 * o : 32 * o + 32], o) for o in (1, 2, 3)]
    )

    shares = mine + move_core(other)
    share = (shares[0] + move_x(shares[2], 2)) + (move_x(shares[1], 1) + move_x(shares[3], -1))
    matched = share[ROWS : ROWS + ROWS // 128].reshape(ROWS)
    view_swapped_cost = jnp.log(plain.reshape(ROWS)) - matched / sharpness_divisor
    return (share[:ROWS], grad_protos, view_swapped_cost)


def solution(mesh):
    placed = (P("dp", None), P(None, "proto"), P("dp"))
    return jax.shard_map(
        local,
        mesh=mesh,
        in_specs=placed,
        out_specs=(P("dp", "proto"), P("dp", "proto"), P("dp")),
        check_vma=False,
    )
```

```python
import functools

import jax
import jax.numpy as jnp
from jax import lax
from jax.experimental import pallas as pl
from jax.experimental.pallas import tpu as pltpu
from jax.sharding import PartitionSpec as P

NY, NZ, NX = 4, 8, 4
ROWS, COLS, D = 512, 4096, 1024
WIDE, QUARTER, PAY = 2048, 1024, 264
F32, BF16 = jnp.float32, jnp.bfloat16
MIB = 1 << 20


code_eps = 0.05
sharpness_divisor = 0.1


def dp_pairs(f):
    pairs = []
    for y in range(NY):
        for z in range(NZ):
            to_y, to_z = f(y, z)
            pairs.append((y * NZ + z, (to_y % NY) * NZ + to_z % NZ))
    return pairs


def proto_pairs(f):
    pairs = []
    for x in range(NX):
        for core in range(2):
            to_x, to_core = f(x, core)
            pairs.append((x * 2 + core, (to_x % NX) * 2 + to_core % 2))
    return pairs


def move_y(v, off):
    return lax.ppermute(v, "dp", dp_pairs(lambda y, z: (y + off, z)))


def move_z(v, off):
    return lax.ppermute(v, "dp", dp_pairs(lambda y, z: (y, z + off)))


def move_x(v, off):
    return lax.ppermute(v, "proto", proto_pairs(lambda x, c: (x + off, c)))


def move_core(v):
    return lax.ppermute(v, "proto", proto_pairs(lambda x, c: (x, c + 1)))


def sum_y(v, after=()):
    terms = [v, move_y(v, 2), move_y(v, 1), move_y(v, -1)]
    if after:
        return add(terms, after)
    return (terms[0] + terms[1]) + (terms[2] + terms[3])


def sum_z(v):
    before, after = move_z(v, 1), move_z(v, -1)
    two = v + after
    three = before + two
    return three + (move_z(three, -3) + move_z(two, 3))


def sum_x(v):
    return (v + move_x(v, 2)) + (move_x(v, 1) + move_x(v, -1))


def sum_core(v):
    return v + move_core(v)


def sum_dp(v, after=()):
    return sum_z(sum_y(v, after))


def sum_proto(v):
    return sum_x(sum_core(v))


def in_vmem(v):
    return pltpu.with_memory_space_constraint(v, pltpu.VMEM)


def in_hbm(v):
    return pltpu.with_memory_space_constraint(v, pltpu.HBM)


VM = pl.BlockSpec(memory_space=pltpu.VMEM)
ANY = pl.BlockSpec(memory_space=pl.ANY)


def params(mib):
    return pltpu.CompilerParams(vmem_limit_bytes=mib * MIB)


def cost(flops, mib, exps=0):
    return pl.CostEstimate(flops=flops, bytes_accessed=mib * MIB, transcendentals=exps)


def unit_kernel(place, embed_ref, mate_ref, unit_ref, pay_ref):
    raw = embed_ref[...].astype(F32)
    scale = lax.rsqrt(jnp.sum(raw * raw, axis=1, keepdims=True) + 1e-06)
    unit_ref[...] = (raw * scale).astype(BF16)
    half = pl.ds(pl.multiple_of(place[3] * (ROWS // 2), ROWS // 2), ROWS // 2)
    pay_ref[: ROWS // 2, :] = unit_ref[half, :].astype(F32)
    pay_ref[ROWS // 2 :, :ROWS] = jnp.broadcast_to(mate_ref[...], (8, ROWS))
    pay_ref[ROWS // 2 :, ROWS:] = jnp.zeros((8, D - ROWS), F32)


def unit_rows(place, embed, mate):
    return pl.pallas_call(
        unit_kernel,
        in_specs=[pl.BlockSpec(memory_space=pltpu.SMEM), VM, VM],
        out_specs=[VM, VM],
        out_shape=[pltpu.VMEM((ROWS, D), BF16), jax.ShapeDtypeStruct((PAY, D), F32)],
        compiler_params=params(12),
        cost_estimate=cost(4 * ROWS * D, 3),
        name="unit_rows",
    )(place, embed, mate)


def scores_kernel(unit_ref, protos_ref, exps_ref, scores_ref, col_ref, protos_out):
    raw = protos_ref[...].astype(F32)
    scale = lax.rsqrt(jnp.sum(raw * raw, axis=0, keepdims=True) + 1e-06)
    unit_protos = (raw * scale).astype(BF16)
    scores = jnp.dot(unit_ref[...], unit_protos, preferred_element_type=F32)
    exps = jnp.exp(scores * (1.0 / sharpness_divisor))
    scores_ref[...] = scores
    width = scores.shape[1]
    at = pl.ds(pl.multiple_of(pl.program_id(0) * width, width), width)
    protos_out[:, at] = unit_protos
    exps_ref[:, at] = exps
    col_ref[:, at] = jnp.sum(exps * exps, axis=0, keepdims=True)


def first_scores(unit, prototypes, block=512):
    return pl.pallas_call(
        scores_kernel,
        grid=(COLS // block,),
        in_specs=[VM, pl.BlockSpec((D, block), lambda j: (0, j))],
        out_specs=[VM, pl.BlockSpec((ROWS, block), lambda j: (0, j)), VM, VM],
        out_shape=[
            pltpu.VMEM((ROWS, COLS), F32),
            pltpu.HBM((ROWS, COLS), F32),
            jax.ShapeDtypeStruct((1, COLS), F32),
            pltpu.VMEM((D, COLS), BF16),
        ],
        compiler_params=params(20),
        cost_estimate=cost(2 * ROWS * COLS * D, 16, ROWS * COLS),
        name="first_scores",
    )(in_vmem(unit), in_hbm(prototypes))


def add_kernel(n, *refs):
    total = refs[0][...]
    for ref in refs[1:n]:
        total += ref[...]
    refs[-1][...] = total


def add(terms, after):
    return pl.pallas_call(
        functools.partial(add_kernel, len(terms)),
        in_specs=[VM] * len(terms) + [ANY] * len(after),
        out_specs=VM,
        out_shape=jax.ShapeDtypeStruct(terms[0].shape, F32),
        compiler_params=params(6),
        cost_estimate=cost(terms[0].size * len(terms), 1),
        name="add",
    )(*terms, *after)


def lanes_to_row(parts):
    return jnp.sum(jnp.concatenate(parts, axis=0).T, axis=0, keepdims=True)


def row_kernel(with_plain, exps_ref, col_total_ref, *refs):
    row_ref = refs[-1]
    weight = 1.0 / col_total_ref[...]
    rows = 64
    parts, plain_parts = [], []
    for i in range(ROWS // rows):
        total = jnp.zeros((rows, 128), F32)
        plain = jnp.zeros((rows, 128), F32)
        for j in range(COLS // 128):
            e = exps_ref[i * rows : (i + 1) * rows, j * 128 : (j + 1) * 128]
            total += (e * e) * weight[:, j * 128 : (j + 1) * 128]
            if with_plain:
                plain += e
        parts.append(total)
        plain_parts.append(plain)
    row_ref[0:1, :] = lanes_to_row(parts)
    if with_plain:
        row_ref[1:2, :] = lanes_to_row(plain_parts)


def row_sums(exps, col_total, with_plain, after):
    return pl.pallas_call(
        functools.partial(row_kernel, with_plain),
        in_specs=[VM, VM] + [ANY] * len(after),
        out_specs=VM,
        out_shape=jax.ShapeDtypeStruct((2 if with_plain else 1, ROWS), F32),
        compiler_params=params(6),
        cost_estimate=cost(3 * ROWS * COLS, 1),
        name="row_sums",
    )(in_vmem(exps), col_total, *after)


def mate_row_kernel(a0, a1, a2, a3, col_total_ref, *refs):
    row_ref = refs[-1]
    weight = 1.0 / col_total_ref[...]
    rows = 64
    parts = []
    for i in range(ROWS // rows):
        total = jnp.zeros((rows, 128), F32)
        for q, a in enumerate((a0, a1, a2, a3)):
            for j in range(QUARTER // 128):
                at = q * QUARTER + j * 128
                total += (
                    a[i * rows : (i + 1) * rows, j * 128 : (j + 1) * 128] * weight[:, at : at + 128]
                )
        parts.append(total)
    row_ref[...] = lanes_to_row(parts)


def mate_row_sums(mates, col_total, after):
    return pl.pallas_call(
        mate_row_kernel,
        in_specs=[VM] * 5 + [ANY] * len(after),
        out_specs=VM,
        out_shape=jax.ShapeDtypeStruct((1, ROWS), F32),
        compiler_params=params(6),
        cost_estimate=cost(2 * ROWS * COLS, 1),
        name="mate_row_sums",
    )(*[in_vmem(m) for m in mates], col_total, *after)


def col_kernel(exps_ref, row_total_ref, *refs):
    col_ref, weight_ref = refs[-2:]
    weight = 1.0 / row_total_ref[0:1, :]
    weight_ref[...] = jnp.broadcast_to(weight, (128, ROWS)).T
    for j in range(COLS // 128):
        e = exps_ref[:, j * 128 : (j + 1) * 128]
        col_ref[:, j * 128 : (j + 1) * 128] = jnp.sum(
            (e * e) * weight_ref[...], axis=0, keepdims=True
        )


def col_sums(exps, row_total, early, after):
    return pl.pallas_call(
        col_kernel,
        in_specs=[VM, VM] + [VM] * len(early) + [ANY] * len(after),
        out_specs=VM,
        out_shape=jax.ShapeDtypeStruct((1, COLS), F32),
        scratch_shapes=[pltpu.VMEM((ROWS, 128), F32)],
        compiler_params=params(6),
        cost_estimate=cost(3 * ROWS * COLS, 1),
        name="col_sums",
    )(in_vmem(exps), row_total, *[in_vmem(v) for v in early], *after)


def mate_rows(x, mate):
    pick = (lax.broadcasted_iota(jnp.int32, (ROWS, ROWS), 0).astype(F32) == mate).astype(BF16)
    return jnp.dot(pick, x, preferred_element_type=F32).astype(BF16)


def block_out(place, x, mate, protos_ref, exps_ref, mates_ref, turned_ref, turn):
    xm = mate_rows(x, mate)
    for j in range(0, QUARTER, 256):
        at = pl.ds(pl.multiple_of(place[0] * QUARTER + j, 256), 256)
        protos = protos_ref[:, at]
        exps_ref[:, j : j + 256] = jnp.exp(
            jnp.dot(x, protos, preferred_element_type=F32) * (1.0 / sharpness_divisor)
        )
        mates_ref[:, j : j + 256] = jnp.exp(
            jnp.dot(xm, protos, preferred_element_type=F32) * (1.0 / code_eps)
        )
    turn[...] = x.astype(F32).T
    for o in range(NZ):
        for p in range(NY):
            to = lax.rem(place[0] + p, NY) * NZ + lax.rem(place[1] + o, NZ)
            rows = turn[pl.ds(pl.multiple_of(to * 32, 32), 32), :]
            at = o * 128 + p * 32
            turned_ref[at : at + 32, :] = rows.astype(BF16)
    return xm


def own_block_kernel(
    place, unit_ref, mate_ref, protos_ref, exps_ref, mates_ref, turned_ref, xm_ref, turn
):
    xm_ref[...] = block_out(
        place, unit_ref[...], mate_ref[...], protos_ref, exps_ref, mates_ref, turned_ref, turn
    )


def far_block_kernel(
    place, same_ref, other_ref, protos_ref, exps_ref, mates_ref, turned_ref, flag_ref, turn, held
):
    flag_ref[...] = jnp.zeros_like(flag_ref)
    half = ROWS // 2
    core = place[3]
    held[pl.ds(pl.multiple_of(core * half, half), half), :] = same_ref[:half, :].astype(BF16)
    held[pl.ds(pl.multiple_of((1 - core) * half, half), half), :] = other_ref[:half, :].astype(BF16)
    block_out(
        place,
        held[...],
        same_ref[half : half + 1, :ROWS],
        protos_ref,
        exps_ref,
        mates_ref,
        turned_ref,
        turn,
    )


def block_call(place, a, b, protos, own):
    shapes = [
        pltpu.VMEM((ROWS, QUARTER), F32),
        pltpu.VMEM((ROWS, QUARTER), F32),
        pltpu.VMEM((D, ROWS), BF16),
    ]
    scratch = [pltpu.VMEM((D, ROWS), F32)]
    if own:
        shapes.append(pltpu.VMEM((ROWS, D), BF16))
    else:
        shapes.append(jax.ShapeDtypeStruct((1, 128), F32))
        scratch.append(pltpu.VMEM((ROWS, D), BF16))
    return pl.pallas_call(
        own_block_kernel if own else far_block_kernel,
        in_specs=[pl.BlockSpec(memory_space=pltpu.SMEM), VM, VM, VM],
        out_specs=[VM] * len(shapes),
        scratch_shapes=scratch,
        out_shape=shapes,
        compiler_params=params(9),
        cost_estimate=cost(4 * ROWS * QUARTER * D, 4, 2 * ROWS * QUARTER),
        name="own_block" if own else "far_block",
    )(place, in_vmem(a) if own else a, b, in_vmem(protos))


def mate_piece_kernel(q, xm_ref, protos_ref, mates_ref):
    for j in range(0, QUARTER, 256):
        protos = protos_ref[:, q * QUARTER + j : q * QUARTER + j + 256]
        mates_ref[:, j : j + 256] = jnp.exp(
            jnp.dot(xm_ref[...], protos, preferred_element_type=F32) * (1.0 / code_eps)
        )


def mate_piece(xm, protos, q):
    return pl.pallas_call(
        functools.partial(mate_piece_kernel, q),
        in_specs=[VM, VM],
        out_specs=VM,
        out_shape=pltpu.VMEM((ROWS, QUARTER), F32),
        compiler_params=params(6),
        cost_estimate=cost(2 * ROWS * QUARTER * D, 2, ROWS * QUARTER),
        name="mate_piece",
    )(in_vmem(xm), in_vmem(protos))


def down(row):
    return jnp.broadcast_to(row, (128, ROWS)).T


def embed_grad_kernel(place, *refs):
    mates, refs = refs[2:6], refs[6:]
    col_total_ref, row_total_ref, plain_ref, protos_ref, embed_ref, scores_ref = refs[:6]
    mine, other = refs[6 : 6 + NX], refs[6 + NX : 6 + 2 * NX]
    total, match, soft, hard, grads = refs[6 + 2 * NX :]
    soft[...] = down((1.0 / sharpness_divisor) / plain_ref[...])
    hard[...] = down(1.0 / row_total_ref[...])
    match[...] = jnp.zeros_like(match)
    width = 512
    for t in range(COLS // width):
        for j in range(width // 128):
            first = t * width + j * 128
            inside = first % QUARTER
            weight = 1.0 / col_total_ref[:, first : first + 128]
            targets = mates[first // QUARTER][:, inside : inside + 128] * weight * hard[...]
            scores = scores_ref[:, first : first + 128]
            match[...] += targets * scores
            grads[t % 2, :, j * 128 : (j + 1) * 128] = (
                jnp.exp(scores * (1.0 / sharpness_divisor)) * soft[...]
                - targets * (1.0 / sharpness_divisor)
            ).astype(BF16)
        part = lax.dot_general(
            grads[t % 2],
            protos_ref[:, t * width : (t + 1) * width],
            (((1,), (1,)), ((), ())),
            preferred_element_type=F32,
        )
        if t == 0:
            total[...] = part
        else:
            total[...] += part

    raw = embed_ref[...].astype(F32)
    term = total[...]
    scale = lax.rsqrt(jnp.sum(raw * raw, axis=1, keepdims=True) + 1e-06)
    inner = jnp.sum(raw * term, axis=1, keepdims=True)
    total[...] = scale * term - (scale * scale * scale * inner) * raw
    matched = jnp.sum(match[...].T, axis=0, keepdims=True)
    for o in range(NX):
        to = lax.rem(place[2] + o, NX) * 2
        for core, ref in ((place[3], mine[o]), (1 - place[3], other[o])):
            at = pl.ds(pl.multiple_of((to + core) * 128, 128), 128)
            ref[:ROWS, :] = total[:, at]
            ref[ROWS:, :] = jnp.zeros((8, 128), F32)
            for t in range(ROWS // 128):
                ref[ROWS + t : ROWS + t + 1, :] = matched[:, t * 128 : (t + 1) * 128]


def embed_grad(place, after, mates, col_total, row_total, plain, protos, embed, scores):
    column = pltpu.VMEM((ROWS, 128), F32)
    return pl.pallas_call(
        embed_grad_kernel,
        in_specs=[pl.BlockSpec(memory_space=pltpu.SMEM)] + [ANY] * 2 + [VM] * 10,
        out_specs=[VM] * (2 * NX),
        scratch_shapes=[
            pltpu.VMEM((ROWS, D), F32),
            column,
            column,
            column,
            pltpu.VMEM((2, ROWS, 512), BF16),
        ],
        out_shape=[jax.ShapeDtypeStruct((ROWS + 8, 128), F32)] * (2 * NX),
        compiler_params=params(12),
        cost_estimate=cost(ROWS * COLS * D // 4, 1, ROWS * COLS // 8),
        name="embed_grad",
    )(
        place,
        *after,
        *[in_vmem(m) for m in mates],
        col_total,
        row_total,
        plain,
        in_vmem(protos),
        embed,
        in_vmem(scores),
    )


def first_chunk_kernel(place, *refs):
    exps, mates, scals = refs[0:4], refs[4:8], refs[8:12]
    turned, col_total_ref = refs[12:16], refs[16]
    grads, chunk_a, chunk_b = refs[17:20]
    at = pl.ds(pl.multiple_of(place[0] * QUARTER, QUARTER), QUARTER)
    weight = (1.0 / sharpness_divisor) / col_total_ref[:, at]
    total = None
    for b in range(NY):
        soft = down((1.0 / sharpness_divisor) / scals[b][1:2, :])
        hard = down(1.0 / scals[b][0:1, :])
        for j in range(QUARTER // 128):
            lanes = slice(j * 128, (j + 1) * 128)
            grads[b * ROWS : (b + 1) * ROWS, lanes] = (
                exps[b][:, lanes] * soft - mates[b][:, lanes] * weight[:, lanes] * hard
            ).astype(BF16)
        part = jnp.dot(
            turned[b][4 * 128 : 5 * 128, :],
            grads[b * ROWS : (b + 1) * ROWS, :],
            preferred_element_type=F32,
        )
        total = part if total is None else total + part
    chunk_a[...] = total[:, : QUARTER // 2]
    chunk_b[...] = total[:, QUARTER // 2 :]


def first_chunk(place, exps, mates, scals, turned, col_total):
    half = jax.ShapeDtypeStruct((128, QUARTER // 2), F32)
    return pl.pallas_call(
        first_chunk_kernel,
        in_specs=[pl.BlockSpec(memory_space=pltpu.SMEM)] + [VM] * 17,
        out_specs=[VM] * 3,
        out_shape=[pltpu.VMEM((WIDE, QUARTER), BF16), half, half],
        compiler_params=params(6),
        cost_estimate=cost(2 * 128 * WIDE * QUARTER + 6 * WIDE * QUARTER, 2),
        name="first_chunk",
    )(
        place,
        *[in_vmem(v) for v in exps],
        *[in_vmem(v) for v in mates],
        *scals,
        *[in_vmem(v) for v in turned],
        col_total,
    )


def chunks_kernel(offsets, t0, t1, t2, t3, grads, *outs):
    for o, out in zip(offsets, outs[-len(offsets) :]):
        total = None
        for b, turned in enumerate((t0, t1, t2, t3)):
            part = jnp.dot(
                turned[o * 128 : (o + 1) * 128, :],
                grads[b * ROWS : (b + 1) * ROWS, :],
                preferred_element_type=F32,
            )
            total = part if total is None else total + part
        out[...] = total


def chunks(turned, grads, offsets):
    return pl.pallas_call(
        functools.partial(chunks_kernel, offsets),
        in_specs=[VM] * 5,
        out_specs=[VM] * len(offsets),
        out_shape=[jax.ShapeDtypeStruct((128, QUARTER), F32)] * len(offsets),
        compiler_params=params(5),
        cost_estimate=cost(2 * 128 * WIDE * QUARTER * len(offsets) // 4, 1),
        name="chunks",
    )(*[in_vmem(v) for v in turned], in_vmem(grads))


def gather_kernel(place, r0, r1, r2, r3, out_ref):
    for o, ref in enumerate((r0, r1, r2, r3)):
        quarter = lax.rem(place[0] + NY - o, NY)
        out_ref[:, pl.ds(pl.multiple_of(quarter * QUARTER, QUARTER), QUARTER)] = ref[...]


def gather_quarters(place, quarters):
    return pl.pallas_call(
        gather_kernel,
        in_specs=[pl.BlockSpec(memory_space=pltpu.SMEM)] + [VM] * 4,
        out_specs=VM,
        out_shape=jax.ShapeDtypeStruct((32, COLS), F32),
        compiler_params=params(8),
        cost_estimate=cost(0, 1),
        name="gather_quarters",
    )(place, *quarters)


def local(embed, prototypes, partner):
    dp, proto = lax.axis_index("dp"), lax.axis_index("proto")
    place = jnp.stack([dp // NZ, dp % NZ, proto // 2, proto % 2]).astype(jnp.int32)
    mate = (partner - dp * ROWS).astype(F32).reshape(1, ROWS)
    unit, pay = unit_rows(place, embed, mate)
    exps, scores, col_part, protos = first_scores(unit, prototypes)

    from_left, from_right = move_y(pay, 1), move_y(pay, -1)
    far = jnp.concatenate([move_y(from_left[:128], 1), move_y(from_right[128:], -1)], axis=0)
    same = [from_left, far, from_right]

    col_total = sum_dp(col_part, [from_left, from_right])
    row_total = sum_proto(row_sums(exps, col_total, True, [far]))
    plain = row_total[1:2]
    crossed = [move_core(v) for v in same]
    blocks = [block_call(place, unit, mate, protos, True)]
    blocks += [block_call(place, v, w, protos, False) for v, w in zip(same, crossed)]
    xm = blocks[0][3]
    mates = [mate_piece(xm, protos, q) for q in range(NY)]

    col_total = sum_dp(col_sums(exps, row_total, [], crossed))
    row_total = sum_proto(row_sums(exps, col_total, False, [b[3] for b in blocks[1:]]))
    col_total = sum_dp(col_sums(exps, row_total, [], []))
    row_total = sum_proto(mate_row_sums(mates, col_total, []))

    scal = jnp.concatenate([row_total, plain], axis=0)
    scals = [scal, move_y(scal, 1), move_y(scal, 2), move_y(scal, -1)]

    turned = [b[2] for b in blocks]
    grads, up, back = first_chunk(
        place, [b[0] for b in blocks], [b[1] for b in blocks], scals, turned, col_total
    )
    half = QUARTER // 2
    up, back = move_z(up, 1), move_z(back, -1)
    c3, c5 = chunks(turned, grads, (3, 5))
    parts = embed_grad(
        place, (up, back), mates, col_total, row_total, plain, protos, embed, scores
    )
    up = jnp.concatenate([c3[:, :half] + up, c3[:, half:]], axis=1)
    back = jnp.concatenate([c5[:, :half], c5[:, half:] + back], axis=1)
    up, back = move_z(up, 1), move_z(back, -1)
    c2, c6 = chunks(turned, grads, (2, 6))
    up, back = add([up, c2], parts[:1]), add([back, c6], parts[:1])
    up, back = move_z(up, 1), move_z(back, -1)
    c1, c7 = chunks(turned, grads, (1, 7))
    up, back = add([up, c1], []), add([back, c7], [])
    shares = [parts[o] + move_core(parts[NX + o]) for o in range(NX)]
    moved = [move_x(shares[o], o) for o in (1, 2, 3)]
    up, back = move_z(up, 1), move_z(back, -1)
    (c0,) = chunks(turned, grads, (0,))
    done = add([c0, up, back], shares)
    grad_protos = gather_quarters(
        place, [done[:32]] + [move_y(done[32 * o : 32 * o + 32], o) for o in (1, 2, 3)]
    )

    share = (shares[0] + moved[1]) + (moved[0] + moved[2])
    matched = share[ROWS : ROWS + ROWS // 128].reshape(ROWS)
    view_swapped_cost = jnp.log(plain.reshape(ROWS)) - matched / sharpness_divisor
    return (share[:ROWS], grad_protos, view_swapped_cost)


def solution(mesh):
    placed = (P("dp", None), P(None, "proto"), P("dp"))
    return jax.shard_map(
        local,
        mesh=mesh,
        in_specs=placed,
        out_specs=(P("dp", "proto"), P("dp", "proto"), P("dp")),
        check_vma=False,
    )
```

```python
import functools

import jax
import jax.numpy as jnp
from jax import lax
from jax.experimental import pallas as pl
from jax.experimental.pallas import tpu as pltpu
from jax.sharding import PartitionSpec as P

NY, NZ, NX = 4, 8, 4
ROWS, COLS, D = 512, 4096, 1024
WIDE, QUARTER, PAY = 2048, 1024, 264
F32, BF16 = jnp.float32, jnp.bfloat16
MIB = 1 << 20


code_eps = 0.05
sharpness_divisor = 0.1


def dp_pairs(f):
    pairs = []
    for y in range(NY):
        for z in range(NZ):
            to_y, to_z = f(y, z)
            pairs.append((y * NZ + z, (to_y % NY) * NZ + to_z % NZ))
    return pairs


def proto_pairs(f):
    pairs = []
    for x in range(NX):
        for core in range(2):
            to_x, to_core = f(x, core)
            pairs.append((x * 2 + core, (to_x % NX) * 2 + to_core % 2))
    return pairs


def move_y(v, off):
    return lax.ppermute(v, "dp", dp_pairs(lambda y, z: (y + off, z)))


def move_z(v, off):
    return lax.ppermute(v, "dp", dp_pairs(lambda y, z: (y, z + off)))


def move_x(v, off):
    return lax.ppermute(v, "proto", proto_pairs(lambda x, c: (x + off, c)))


def move_core(v):
    return lax.ppermute(v, "proto", proto_pairs(lambda x, c: (x, c + 1)))


def sum_y(v):
    return (v + move_y(v, 2)) + (move_y(v, 1) + move_y(v, -1))


def sum_z(v, after=()):
    left, right = move_z(v, 1), move_z(v, -1)
    two = v + right
    three = left + two
    terms = [three, move_z(three, -3), move_z(two, 3)]
    if after:
        return add(terms, after)
    return terms[0] + (terms[1] + terms[2])


def sum_x(v):
    return (v + move_x(v, 2)) + (move_x(v, 1) + move_x(v, -1))


def sum_core(v):
    return v + move_core(v)


def sum_dp(v, after=()):
    return sum_y(sum_z(v, after))


def sum_proto(v):
    return sum_x(sum_core(v))


def in_vmem(v):
    return pltpu.with_memory_space_constraint(v, pltpu.VMEM)


def in_hbm(v):
    return pltpu.with_memory_space_constraint(v, pltpu.HBM)


VM = pl.BlockSpec(memory_space=pltpu.VMEM)
ANY = pl.BlockSpec(memory_space=pl.ANY)


def params(mib):
    return pltpu.CompilerParams(vmem_limit_bytes=mib * MIB)


def cost(flops, mib, exps=0):
    return pl.CostEstimate(flops=flops, bytes_accessed=mib * MIB, transcendentals=exps)


def unit_kernel(place, embed_ref, mate_ref, unit_ref, pay_ref):
    raw = embed_ref[...].astype(F32)
    scale = lax.rsqrt(jnp.sum(raw * raw, axis=1, keepdims=True) + 1e-06)
    unit_ref[...] = (raw * scale).astype(BF16)
    half = pl.ds(pl.multiple_of(place[3] * (ROWS // 2), ROWS // 2), ROWS // 2)
    pay_ref[: ROWS // 2, :] = unit_ref[half, :].astype(F32)
    pay_ref[ROWS // 2 :, :ROWS] = jnp.broadcast_to(mate_ref[...], (8, ROWS))
    pay_ref[ROWS // 2 :, ROWS:] = jnp.zeros((8, D - ROWS), F32)


def unit_rows(place, embed, mate):
    return pl.pallas_call(
        unit_kernel,
        in_specs=[pl.BlockSpec(memory_space=pltpu.SMEM), VM, VM],
        out_specs=[VM, VM],
        out_shape=[pltpu.VMEM((ROWS, D), BF16), jax.ShapeDtypeStruct((PAY, D), F32)],
        compiler_params=params(12),
        cost_estimate=cost(4 * ROWS * D, 3),
        name="unit_rows",
    )(place, embed, mate)


def scores_kernel(unit_ref, protos_ref, exps_ref, scores_ref, col_ref, protos_out):
    raw = protos_ref[...].astype(F32)
    scale = lax.rsqrt(jnp.sum(raw * raw, axis=0, keepdims=True) + 1e-06)
    unit_protos = (raw * scale).astype(BF16)
    scores = jnp.dot(unit_ref[...], unit_protos, preferred_element_type=F32)
    exps = jnp.exp(scores * (1.0 / sharpness_divisor))
    scores_ref[...] = scores
    width = scores.shape[1]
    at = pl.ds(pl.multiple_of(pl.program_id(0) * width, width), width)
    protos_out[:, at] = unit_protos
    exps_ref[:, at] = exps
    col_ref[:, at] = jnp.sum(exps * exps, axis=0, keepdims=True)


def first_scores(unit, prototypes, block=512):
    return pl.pallas_call(
        scores_kernel,
        grid=(COLS // block,),
        in_specs=[VM, pl.BlockSpec((D, block), lambda j: (0, j))],
        out_specs=[VM, pl.BlockSpec((ROWS, block), lambda j: (0, j)), VM, VM],
        out_shape=[
            pltpu.VMEM((ROWS, COLS), F32),
            pltpu.HBM((ROWS, COLS), F32),
            jax.ShapeDtypeStruct((1, COLS), F32),
            pltpu.VMEM((D, COLS), BF16),
        ],
        compiler_params=params(20),
        cost_estimate=cost(2 * ROWS * COLS * D, 16, ROWS * COLS),
        name="first_scores",
    )(in_vmem(unit), in_hbm(prototypes))


def add_kernel(n, *refs):
    total = refs[0][...]
    for ref in refs[1:n]:
        total += ref[...]
    refs[-1][...] = total


def add(terms, after, held=()):
    return pl.pallas_call(
        functools.partial(add_kernel, len(terms)),
        in_specs=[VM] * (len(terms) + len(held)) + [ANY] * len(after),
        out_specs=VM,
        out_shape=jax.ShapeDtypeStruct(terms[0].shape, F32),
        compiler_params=params(6),
        cost_estimate=cost(terms[0].size * len(terms), 1),
        name="add",
    )(*terms, *[in_vmem(v) for v in held], *after)


def hold_kernel(n, *refs):
    for i in range(n):
        refs[i - n][...] = refs[i][...]


def hold(values, after):
    return pl.pallas_call(
        functools.partial(hold_kernel, len(values)),
        in_specs=[VM] * len(values) + [ANY] * len(after),
        out_specs=[VM] * len(values),
        out_shape=[jax.ShapeDtypeStruct(v.shape, F32) for v in values],
        compiler_params=params(6),
        cost_estimate=cost(0, 1),
        name="hold",
    )(*values, *after)


def hop_kernel(left_ref, right_ref, *refs):
    low_ref, high_ref = refs[-2:]
    low_ref[...] = left_ref[:128, :]
    high_ref[...] = right_ref[128:, :]


def second_hop(left, right, after):
    return pl.pallas_call(
        hop_kernel,
        in_specs=[VM, VM] + [ANY] * len(after),
        out_specs=[VM, VM],
        out_shape=[
            jax.ShapeDtypeStruct((128, D), F32),
            jax.ShapeDtypeStruct((PAY - 128, D), F32),
        ],
        compiler_params=params(8),
        cost_estimate=cost(ROWS * D, 2),
        name="second_hop",
    )(left, right, *after)


def lanes_to_row(parts):
    return jnp.sum(jnp.concatenate(parts, axis=0).T, axis=0, keepdims=True)


def row_kernel(with_plain, exps_ref, col_total_ref, *refs):
    row_ref = refs[-1]
    weight = 1.0 / col_total_ref[...]
    rows = 64
    parts, plain_parts = [], []
    for i in range(ROWS // rows):
        total = jnp.zeros((rows, 128), F32)
        plain = jnp.zeros((rows, 128), F32)
        for j in range(COLS // 128):
            e = exps_ref[i * rows : (i + 1) * rows, j * 128 : (j + 1) * 128]
            total += (e * e) * weight[:, j * 128 : (j + 1) * 128]
            if with_plain:
                plain += e
        parts.append(total)
        plain_parts.append(plain)
    row_ref[0:1, :] = lanes_to_row(parts)
    if with_plain:
        row_ref[1:2, :] = lanes_to_row(plain_parts)


def row_sums(exps, col_total, with_plain, after):
    return pl.pallas_call(
        functools.partial(row_kernel, with_plain),
        in_specs=[VM, VM] + [ANY] * len(after),
        out_specs=VM,
        out_shape=jax.ShapeDtypeStruct((2 if with_plain else 1, ROWS), F32),
        compiler_params=params(6),
        cost_estimate=cost(3 * ROWS * COLS, 1),
        name="row_sums",
    )(in_vmem(exps), col_total, *after)


def mate_row_kernel(a0, a1, a2, a3, col_total_ref, *refs):
    row_ref = refs[-1]
    weight = 1.0 / col_total_ref[...]
    rows = 64
    parts = []
    for i in range(ROWS // rows):
        total = jnp.zeros((rows, 128), F32)
        for q, a in enumerate((a0, a1, a2, a3)):
            for j in range(QUARTER // 128):
                at = q * QUARTER + j * 128
                total += (
                    a[i * rows : (i + 1) * rows, j * 128 : (j + 1) * 128] * weight[:, at : at + 128]
                )
        parts.append(total)
    row_ref[...] = lanes_to_row(parts)


def mate_row_sums(mates, col_total, after):
    return pl.pallas_call(
        mate_row_kernel,
        in_specs=[VM] * 5 + [ANY] * len(after),
        out_specs=VM,
        out_shape=jax.ShapeDtypeStruct((1, ROWS), F32),
        compiler_params=params(6),
        cost_estimate=cost(2 * ROWS * COLS, 1),
        name="mate_row_sums",
    )(*[in_vmem(m) for m in mates], col_total, *after)


def col_kernel(exps_ref, row_total_ref, *refs):
    col_ref, weight_ref = refs[-2:]
    weight = 1.0 / row_total_ref[0:1, :]
    weight_ref[...] = jnp.broadcast_to(weight, (128, ROWS)).T
    for j in range(COLS // 128):
        e = exps_ref[:, j * 128 : (j + 1) * 128]
        col_ref[:, j * 128 : (j + 1) * 128] = jnp.sum(
            (e * e) * weight_ref[...], axis=0, keepdims=True
        )


def col_sums(exps, row_total, early, after):
    return pl.pallas_call(
        col_kernel,
        in_specs=[VM, VM] + [VM] * len(early) + [ANY] * len(after),
        out_specs=VM,
        out_shape=jax.ShapeDtypeStruct((1, COLS), F32),
        scratch_shapes=[pltpu.VMEM((ROWS, 128), F32)],
        compiler_params=params(6),
        cost_estimate=cost(3 * ROWS * COLS, 1),
        name="col_sums",
    )(in_vmem(exps), row_total, *[in_vmem(v) for v in early], *after)


def mate_rows(x, mate):
    pick = (lax.broadcasted_iota(jnp.int32, (ROWS, ROWS), 0).astype(F32) == mate).astype(BF16)
    return jnp.dot(pick, x, preferred_element_type=F32).astype(BF16)


def block_out(place, x, mate, protos_ref, exps_ref, mates_ref, turned_ref, turn):
    xm = mate_rows(x, mate)
    for j in range(0, QUARTER, 256):
        at = pl.ds(pl.multiple_of(place[0] * QUARTER + j, 256), 256)
        protos = protos_ref[:, at]
        exps_ref[:, j : j + 256] = jnp.exp(
            jnp.dot(x, protos, preferred_element_type=F32) * (1.0 / sharpness_divisor)
        )
        mates_ref[:, j : j + 256] = jnp.exp(
            jnp.dot(xm, protos, preferred_element_type=F32) * (1.0 / code_eps)
        )
    turn[...] = x.astype(F32).T
    for o in range(NZ):
        for p in range(NY):
            to = lax.rem(place[0] + p, NY) * NZ + lax.rem(place[1] + o, NZ)
            rows = turn[pl.ds(pl.multiple_of(to * 32, 32), 32), :]
            at = o * 128 + p * 32
            turned_ref[at : at + 32, :] = rows.astype(BF16)
    return xm


def own_block_kernel(
    place, unit_ref, mate_ref, protos_ref, exps_ref, mates_ref, turned_ref, xm_ref, turn
):
    xm_ref[...] = block_out(
        place, unit_ref[...], mate_ref[...], protos_ref, exps_ref, mates_ref, turned_ref, turn
    )


def far_block_kernel(
    place, same_ref, other_ref, protos_ref, exps_ref, mates_ref, turned_ref, flag_ref, turn, held
):
    flag_ref[...] = jnp.zeros_like(flag_ref)
    half = ROWS // 2
    core = place[3]
    held[pl.ds(pl.multiple_of(core * half, half), half), :] = same_ref[:half, :].astype(BF16)
    held[pl.ds(pl.multiple_of((1 - core) * half, half), half), :] = other_ref[:half, :].astype(BF16)
    block_out(
        place,
        held[...],
        same_ref[half : half + 1, :ROWS],
        protos_ref,
        exps_ref,
        mates_ref,
        turned_ref,
        turn,
    )


def block_call(place, a, b, protos, own):
    shapes = [
        pltpu.VMEM((ROWS, QUARTER), F32),
        pltpu.VMEM((ROWS, QUARTER), F32),
        pltpu.VMEM((D, ROWS), BF16),
    ]
    scratch = [pltpu.VMEM((D, ROWS), F32)]
    if own:
        shapes.append(pltpu.VMEM((ROWS, D), BF16))
    else:
        shapes.append(jax.ShapeDtypeStruct((1, 128), F32))
        scratch.append(pltpu.VMEM((ROWS, D), BF16))
    return pl.pallas_call(
        own_block_kernel if own else far_block_kernel,
        in_specs=[pl.BlockSpec(memory_space=pltpu.SMEM), VM, VM, VM],
        out_specs=[VM] * len(shapes),
        scratch_shapes=scratch,
        out_shape=shapes,
        compiler_params=params(9),
        cost_estimate=cost(4 * ROWS * QUARTER * D, 4, 2 * ROWS * QUARTER),
        name="own_block" if own else "far_block",
    )(place, in_vmem(a) if own else a, b, in_vmem(protos))


def mate_piece_kernel(q, xm_ref, protos_ref, mates_ref):
    for j in range(0, QUARTER, 256):
        protos = protos_ref[:, q * QUARTER + j : q * QUARTER + j + 256]
        mates_ref[:, j : j + 256] = jnp.exp(
            jnp.dot(xm_ref[...], protos, preferred_element_type=F32) * (1.0 / code_eps)
        )


def mate_piece(xm, protos, q):
    return pl.pallas_call(
        functools.partial(mate_piece_kernel, q),
        in_specs=[VM, VM],
        out_specs=VM,
        out_shape=pltpu.VMEM((ROWS, QUARTER), F32),
        compiler_params=params(6),
        cost_estimate=cost(2 * ROWS * QUARTER * D, 2, ROWS * QUARTER),
        name="mate_piece",
    )(in_vmem(xm), in_vmem(protos))


def down(row):
    return jnp.broadcast_to(row, (128, ROWS)).T


def embed_grad_kernel(part, place, *refs):
    mates, refs = refs[2:4], refs[4:]
    col_total_ref, row_total_ref, plain_ref, protos_ref, scores_ref = refs[:5]
    if part == 0:
        total, match, soft, hard, grads = refs[5:]
        match[...] = jnp.zeros_like(match)
    else:
        total_in, match_in, embed_ref = refs[5:8]
        mine, other = refs[8 : 8 + NX], refs[8 + NX : 8 + 2 * NX]
        total, match, soft, hard, grads = refs[8 + 2 * NX :]
        match[...] = match_in[...]
    soft[...] = down((1.0 / sharpness_divisor) / plain_ref[...])
    hard[...] = down(1.0 / row_total_ref[...])
    width = 512
    for t in range(COLS // 2 // width):
        for j in range(width // 128):
            first = t * width + j * 128
            at = part * (COLS // 2) + first
            inside = first % QUARTER
            weight = 1.0 / col_total_ref[:, at : at + 128]
            targets = mates[first // QUARTER][:, inside : inside + 128] * weight * hard[...]
            scores = scores_ref[:, at : at + 128]
            match[...] += targets * scores
            grads[t % 2, :, j * 128 : (j + 1) * 128] = (
                jnp.exp(scores * (1.0 / sharpness_divisor)) * soft[...]
                - targets * (1.0 / sharpness_divisor)
            ).astype(BF16)
        at = part * (COLS // 2) + t * width
        term = lax.dot_general(
            grads[t % 2],
            protos_ref[:, at : at + width],
            (((1,), (1,)), ((), ())),
            preferred_element_type=F32,
        )
        if t > 0:
            total[...] += term
        elif part == 0:
            total[...] = term
        else:
            total[...] = total_in[...] + term

    if part == 1:
        raw = embed_ref[...].astype(F32)
        term = total[...]
        scale = lax.rsqrt(jnp.sum(raw * raw, axis=1, keepdims=True) + 1e-06)
        inner = jnp.sum(raw * term, axis=1, keepdims=True)
        total[...] = scale * term - (scale * scale * scale * inner) * raw
        matched = jnp.sum(match[...].T, axis=0, keepdims=True)
        for o in range(NX):
            to = lax.rem(place[2] + o, NX) * 2
            for core, ref in ((place[3], mine[o]), (1 - place[3], other[o])):
                at = pl.ds(pl.multiple_of((to + core) * 128, 128), 128)
                ref[:ROWS, :] = total[:, at]
                ref[ROWS:, :] = jnp.zeros((8, 128), F32)
                for t in range(ROWS // 128):
                    ref[ROWS + t : ROWS + t + 1, :] = matched[:, t * 128 : (t + 1) * 128]


def embed_grad(part, place, after, mates, vectors, protos, scores, more):
    column = pltpu.VMEM((ROWS, 128), F32)
    sums = [pltpu.VMEM((ROWS, D), F32), column]
    scratch = [column, column, pltpu.VMEM((2, ROWS, 512), BF16)]
    if part == 0:
        shapes = sums
    else:
        shapes = [jax.ShapeDtypeStruct((ROWS + 8, 128), F32)] * (2 * NX)
        scratch = sums + scratch
        more = [in_vmem(more[0]), in_vmem(more[1]), more[2]]
    return pl.pallas_call(
        functools.partial(embed_grad_kernel, part),
        in_specs=[pl.BlockSpec(memory_space=pltpu.SMEM)] + [ANY] * 2 + [VM] * (7 + len(more)),
        out_specs=[VM] * len(shapes),
        scratch_shapes=scratch,
        out_shape=shapes,
        compiler_params=params(12),
        cost_estimate=cost(ROWS * COLS * D // 8, 1, ROWS * COLS // 16),
        name="embed_grad",
    )(
        place,
        *after,
        *[in_vmem(m) for m in mates],
        *vectors,
        in_vmem(protos),
        in_vmem(scores),
        *more,
    )


def first_chunk_kernel(place, *refs):
    exps, mates, scals = refs[0:4], refs[4:8], refs[8:12]
    turned, col_total_ref = refs[12:16], refs[16]
    grads, chunk_a, chunk_b = refs[17:20]
    at = pl.ds(pl.multiple_of(place[0] * QUARTER, QUARTER), QUARTER)
    weight = (1.0 / sharpness_divisor) / col_total_ref[:, at]
    total = None
    for b in range(NY):
        soft = down((1.0 / sharpness_divisor) / scals[b][1:2, :])
        hard = down(1.0 / scals[b][0:1, :])
        for j in range(QUARTER // 128):
            lanes = slice(j * 128, (j + 1) * 128)
            grads[b * ROWS : (b + 1) * ROWS, lanes] = (
                exps[b][:, lanes] * soft - mates[b][:, lanes] * weight[:, lanes] * hard
            ).astype(BF16)
        part = jnp.dot(
            turned[b][4 * 128 : 5 * 128, :],
            grads[b * ROWS : (b + 1) * ROWS, :],
            preferred_element_type=F32,
        )
        total = part if total is None else total + part
    chunk_a[...] = total[:, : QUARTER // 2]
    chunk_b[...] = total[:, QUARTER // 2 :]


def first_chunk(place, exps, mates, scals, turned, col_total):
    half = jax.ShapeDtypeStruct((128, QUARTER // 2), F32)
    return pl.pallas_call(
        first_chunk_kernel,
        in_specs=[pl.BlockSpec(memory_space=pltpu.SMEM)] + [VM] * 17,
        out_specs=[VM] * 3,
        out_shape=[pltpu.VMEM((WIDE, QUARTER), BF16), half, half],
        compiler_params=params(6),
        cost_estimate=cost(2 * 128 * WIDE * QUARTER + 6 * WIDE * QUARTER, 2),
        name="first_chunk",
    )(
        place,
        *[in_vmem(v) for v in exps],
        *[in_vmem(v) for v in mates],
        *scals,
        *[in_vmem(v) for v in turned],
        col_total,
    )


def chunks_kernel(offsets, t0, t1, t2, t3, grads, *outs):
    for i, o in enumerate(offsets):
        total = None
        for b, turned in enumerate((t0, t1, t2, t3)):
            part = jnp.dot(
                turned[o * 128 : (o + 1) * 128, :],
                grads[b * ROWS : (b + 1) * ROWS, :],
                preferred_element_type=F32,
            )
            total = part if total is None else total + part
        outs[2 * i][...] = total[:, : QUARTER // 2]
        outs[2 * i + 1][...] = total[:, QUARTER // 2 :]


def chunks(turned, grads, offsets):
    return pl.pallas_call(
        functools.partial(chunks_kernel, offsets),
        in_specs=[VM] * 5,
        out_specs=[VM] * (2 * len(offsets)),
        out_shape=[jax.ShapeDtypeStruct((128, QUARTER // 2), F32)] * (2 * len(offsets)),
        compiler_params=params(5),
        cost_estimate=cost(2 * 128 * WIDE * QUARTER * len(offsets) // 4, 1),
        name="chunks",
    )(*[in_vmem(v) for v in turned], in_vmem(grads))


def last_add_kernel(*refs):
    half = QUARTER // 2
    for h in range(2):
        total = (refs[3 * h][...] + refs[3 * h + 1][...]) + refs[3 * h + 2][...]
        for o in range(NY):
            refs[-NY + o][:, h * half : (h + 1) * half] = total[o * 32 : (o + 1) * 32, :]


def last_add(terms, after):
    return pl.pallas_call(
        last_add_kernel,
        in_specs=[VM] * 6 + [ANY] * len(after),
        out_specs=[VM] * NY,
        out_shape=[jax.ShapeDtypeStruct((32, QUARTER), F32)] * NY,
        compiler_params=params(5),
        cost_estimate=cost(3 * 128 * QUARTER, 1),
        name="last_add",
    )(*terms, *after)


def gather_kernel(place, r0, r1, r2, r3, out_ref):
    for o, ref in enumerate((r0, r1, r2, r3)):
        quarter = lax.rem(place[0] + NY - o, NY)
        out_ref[:, pl.ds(pl.multiple_of(quarter * QUARTER, QUARTER), QUARTER)] = ref[...]


def gather_quarters(place, quarters):
    return pl.pallas_call(
        gather_kernel,
        in_specs=[pl.BlockSpec(memory_space=pltpu.SMEM)] + [VM] * 4,
        out_specs=VM,
        out_shape=jax.ShapeDtypeStruct((32, COLS), F32),
        compiler_params=params(8),
        cost_estimate=cost(0, 1),
        name="gather_quarters",
    )(place, *quarters)


def local(embed, prototypes, partner):
    dp, proto = lax.axis_index("dp"), lax.axis_index("proto")
    place = jnp.stack([dp // NZ, dp % NZ, proto // 2, proto % 2]).astype(jnp.int32)
    mate = (partner - dp * ROWS).astype(F32).reshape(1, ROWS)
    unit, pay = unit_rows(place, embed, mate)
    exps, scores, col_part, protos = first_scores(unit, prototypes)

    from_left, from_right = move_y(pay, 1), move_y(pay, -1)

    col_total = sum_dp(col_part, [from_left, from_right])
    low, high = second_hop(from_left, from_right, [col_total])
    far = jnp.concatenate([move_y(low, 1), move_y(high, -1)], axis=0)
    same = [from_left, far, from_right]
    crossed = [move_core(v) for v in same]
    row_total = sum_proto(row_sums(exps, col_total, True, []))
    plain = row_total[1:2]
    blocks = [block_call(place, unit, mate, protos, True)]
    blocks += [block_call(place, v, w, protos, False) for v, w in zip(same, crossed)]
    xm = blocks[0][3]
    mates = [mate_piece(xm, protos, q) for q in range(NY)]

    col_total = sum_dp(col_sums(exps, row_total, [], []), [far])
    row_total = sum_proto(row_sums(exps, col_total, False, [crossed[0], crossed[2]]))
    col_total = sum_dp(col_sums(exps, row_total, mates, [crossed[1]]))
    row_total = sum_proto(mate_row_sums(mates, col_total, [b[3] for b in blocks[1:]]))

    scal = jnp.concatenate([row_total, plain], axis=0)
    scals = [scal, move_y(scal, 1), move_y(scal, 2), move_y(scal, -1)]

    turned = [b[2] for b in blocks]
    grads, up, back = first_chunk(
        place, [b[0] for b in blocks], [b[1] for b in blocks], scals, turned, col_total
    )
    vectors = (col_total, row_total, plain)
    up0, back1 = move_z(up, 1), move_z(back, -1)
    c30, c31, c50, c51 = chunks(turned, grads, (3, 5))
    up1, back0 = move_z(c31, 1), move_z(c50, -1)
    up0, back1 = c30 + up0, c51 + back1
    sums = embed_grad(0, place, (up0, back1), mates[:2], vectors, protos, scores, [])
    up0, back1 = move_z(up0, 1), move_z(back1, -1)
    c20, c21, c60, c61 = chunks(turned, grads, (2, 6))
    up1, back0 = add([c21, up1], [], sums[1:]), add([c60, back0], [], sums[1:])
    parts = embed_grad(
        1, place, (up1, back0), mates[2:], vectors, protos, scores, [*sums, embed]
    )
    up1, back0 = move_z(up1, 1), move_z(back0, -1)
    up0, back1 = move_z(c20 + up0, 1), move_z(c61 + back1, -1)
    c10, c11, c70, c71 = chunks(turned, grads, (1, 7))
    up1, back0 = c11 + up1, c70 + back0
    others = hold(parts[NX:], [up1, back0])
    up1, back0 = move_z(up1, 1), move_z(back0, -1)
    up0, back1 = move_z(c10 + up0, 1), move_z(c71 + back1, -1)
    shares = [parts[o] + move_core(others[o]) for o in range(NX)]
    moved = [move_x(shares[o], o) for o in (1, 2, 3)]
    c00, c01 = chunks(turned, grads, (0,))
    done = last_add([c00, up0, back0, c01, up1, back1], shares)
    grad_protos = gather_quarters(
        place, [done[0]] + [move_y(done[o], o) for o in (1, 2, 3)]
    )

    share = (shares[0] + moved[1]) + (moved[0] + moved[2])
    matched = share[ROWS : ROWS + ROWS // 128].reshape(ROWS)
    view_swapped_cost = jnp.log(plain.reshape(ROWS)) - matched / sharpness_divisor
    return (share[:ROWS], grad_protos, view_swapped_cost)


def solution(mesh):
    placed = (P("dp", None), P(None, "proto"), P("dp"))
    return jax.shard_map(
        local,
        mesh=mesh,
        in_specs=placed,
        out_specs=(P("dp", "proto"), P("dp", "proto"), P("dp")),
        check_vma=False,
    )
```

```python
import functools

import jax
import jax.numpy as jnp
from jax import lax
from jax.experimental import pallas as pl
from jax.experimental.pallas import tpu as pltpu
from jax.sharding import PartitionSpec as P

NY, NZ, NX = 4, 8, 4
ROWS, COLS, D = 512, 4096, 1024
WIDE, QUARTER, PAY = 2048, 1024, 264
F32, BF16 = jnp.float32, jnp.bfloat16
MIB = 1 << 20


code_eps = 0.05
sharpness_divisor = 0.1


def dp_pairs(f):
    pairs = []
    for y in range(NY):
        for z in range(NZ):
            to_y, to_z = f(y, z)
            pairs.append((y * NZ + z, (to_y % NY) * NZ + to_z % NZ))
    return pairs


def proto_pairs(f):
    pairs = []
    for x in range(NX):
        for core in range(2):
            to_x, to_core = f(x, core)
            pairs.append((x * 2 + core, (to_x % NX) * 2 + to_core % 2))
    return pairs


def move_y(v, off):
    return lax.ppermute(v, "dp", dp_pairs(lambda y, z: (y + off, z)))


def move_z(v, off):
    return lax.ppermute(v, "dp", dp_pairs(lambda y, z: (y, z + off)))


def move_x(v, off):
    return lax.ppermute(v, "proto", proto_pairs(lambda x, c: (x + off, c)))


def move_core(v):
    return lax.ppermute(v, "proto", proto_pairs(lambda x, c: (x, c + 1)))


def sum_y(v):
    return (v + move_y(v, 2)) + (move_y(v, 1) + move_y(v, -1))


def sum_z(v, after=(), early=()):
    left, right = move_z(v, 1), move_z(v, -1)
    two = add([v, right], early) if early else v + right
    three = left + two
    terms = [three, move_z(three, -3), move_z(two, 3)]
    if after:
        return add(terms, after)
    return terms[0] + (terms[1] + terms[2])


def sum_x(v):
    return (v + move_x(v, 2)) + (move_x(v, 1) + move_x(v, -1))


def sum_core(v):
    return v + move_core(v)


def sum_dp(v, after=(), early=()):
    return sum_y(sum_z(v, after, early))


def sum_proto(v):
    return sum_x(sum_core(v))


def in_vmem(v):
    return pltpu.with_memory_space_constraint(v, pltpu.VMEM)


def in_hbm(v):
    return pltpu.with_memory_space_constraint(v, pltpu.HBM)


VM = pl.BlockSpec(memory_space=pltpu.VMEM)
ANY = pl.BlockSpec(memory_space=pl.ANY)


def params(mib):
    return pltpu.CompilerParams(vmem_limit_bytes=mib * MIB)


def cost(flops, mib, exps=0):
    return pl.CostEstimate(flops=flops, bytes_accessed=mib * MIB, transcendentals=exps)


def unit_kernel(place, embed_ref, mate_ref, unit_ref, pay_ref):
    raw = embed_ref[...].astype(F32)
    scale = lax.rsqrt(jnp.sum(raw * raw, axis=1, keepdims=True) + 1e-06)
    unit_ref[...] = (raw * scale).astype(BF16)
    half = pl.ds(pl.multiple_of(place[3] * (ROWS // 2), ROWS // 2), ROWS // 2)
    pay_ref[: ROWS // 2, :] = unit_ref[half, :].astype(F32)
    pay_ref[ROWS // 2 :, :ROWS] = jnp.broadcast_to(mate_ref[...], (8, ROWS))
    pay_ref[ROWS // 2 :, ROWS:] = jnp.zeros((8, D - ROWS), F32)


def unit_rows(place, embed, mate):
    return pl.pallas_call(
        unit_kernel,
        in_specs=[pl.BlockSpec(memory_space=pltpu.SMEM), VM, VM],
        out_specs=[VM, VM],
        out_shape=[pltpu.VMEM((ROWS, D), BF16), jax.ShapeDtypeStruct((PAY, D), F32)],
        compiler_params=params(12),
        cost_estimate=cost(4 * ROWS * D, 3),
        name="unit_rows",
    )(place, embed, mate)


def scores_kernel(unit_ref, protos_ref, exps_ref, scores_ref, col_ref, protos_out):
    raw = protos_ref[...].astype(F32)
    scale = lax.rsqrt(jnp.sum(raw * raw, axis=0, keepdims=True) + 1e-06)
    unit_protos = (raw * scale).astype(BF16)
    scores = jnp.dot(unit_ref[...], unit_protos, preferred_element_type=F32)
    exps = jnp.exp(scores * (1.0 / sharpness_divisor))
    scores_ref[...] = scores
    width = scores.shape[1]
    at = pl.ds(pl.multiple_of(pl.program_id(0) * width, width), width)
    protos_out[:, at] = unit_protos
    exps_ref[:, at] = exps
    col_ref[:, at] = jnp.sum(exps * exps, axis=0, keepdims=True)


def first_scores(unit, prototypes, block=512):
    return pl.pallas_call(
        scores_kernel,
        grid=(COLS // block,),
        in_specs=[VM, pl.BlockSpec((D, block), lambda j: (0, j))],
        out_specs=[VM, pl.BlockSpec((ROWS, block), lambda j: (0, j)), VM, VM],
        out_shape=[
            pltpu.VMEM((ROWS, COLS), F32),
            pltpu.HBM((ROWS, COLS), F32),
            jax.ShapeDtypeStruct((1, COLS), F32),
            pltpu.VMEM((D, COLS), BF16),
        ],
        compiler_params=params(20),
        cost_estimate=cost(2 * ROWS * COLS * D, 16, ROWS * COLS),
        name="first_scores",
    )(in_vmem(unit), in_hbm(prototypes))


def add_kernel(n, *refs):
    total = refs[0][...]
    for ref in refs[1:n]:
        total += ref[...]
    refs[-1][...] = total


def add(terms, after):
    return pl.pallas_call(
        functools.partial(add_kernel, len(terms)),
        in_specs=[VM] * len(terms) + [ANY] * len(after),
        out_specs=VM,
        out_shape=jax.ShapeDtypeStruct(terms[0].shape, F32),
        compiler_params=params(6),
        cost_estimate=cost(terms[0].size * len(terms), 1),
        name="add",
    )(*terms, *after)


def hop_kernel(left_ref, right_ref, *refs):
    low_ref, high_ref = refs[-2:]
    low_ref[...] = left_ref[:128, :]
    high_ref[...] = right_ref[128:, :]


def second_hop(left, right, after):
    return pl.pallas_call(
        hop_kernel,
        in_specs=[VM, VM] + [ANY] * len(after),
        out_specs=[VM, VM],
        out_shape=[
            jax.ShapeDtypeStruct((128, D), F32),
            jax.ShapeDtypeStruct((PAY - 128, D), F32),
        ],
        compiler_params=params(8),
        cost_estimate=cost(ROWS * D, 2),
        name="second_hop",
    )(left, right, *after)


def lanes_to_row(parts):
    return jnp.sum(jnp.concatenate(parts, axis=0).T, axis=0, keepdims=True)


def row_kernel(with_plain, exps_ref, col_total_ref, *refs):
    row_ref = refs[-1]
    weight = 1.0 / col_total_ref[...]
    rows = 64
    parts, plain_parts = [], []
    for i in range(ROWS // rows):
        total = jnp.zeros((rows, 128), F32)
        plain = jnp.zeros((rows, 128), F32)
        for j in range(COLS // 128):
            e = exps_ref[i * rows : (i + 1) * rows, j * 128 : (j + 1) * 128]
            total += (e * e) * weight[:, j * 128 : (j + 1) * 128]
            if with_plain:
                plain += e
        parts.append(total)
        plain_parts.append(plain)
    row_ref[0:1, :] = lanes_to_row(parts)
    if with_plain:
        row_ref[1:2, :] = lanes_to_row(plain_parts)


def row_sums(exps, col_total, with_plain, after):
    return pl.pallas_call(
        functools.partial(row_kernel, with_plain),
        in_specs=[VM, VM] + [ANY] * len(after),
        out_specs=VM,
        out_shape=jax.ShapeDtypeStruct((2 if with_plain else 1, ROWS), F32),
        compiler_params=params(6),
        cost_estimate=cost(3 * ROWS * COLS, 1),
        name="row_sums",
    )(in_vmem(exps), col_total, *after)


def mate_row_kernel(a0, a1, a2, a3, col_total_ref, *refs):
    row_ref = refs[-1]
    weight = 1.0 / col_total_ref[...]
    rows = 64
    parts = []
    for i in range(ROWS // rows):
        total = jnp.zeros((rows, 128), F32)
        for q, a in enumerate((a0, a1, a2, a3)):
            for j in range(QUARTER // 128):
                at = q * QUARTER + j * 128
                total += (
                    a[i * rows : (i + 1) * rows, j * 128 : (j + 1) * 128] * weight[:, at : at + 128]
                )
        parts.append(total)
    row_ref[...] = lanes_to_row(parts)


def mate_row_sums(mates, col_total, after):
    return pl.pallas_call(
        mate_row_kernel,
        in_specs=[VM] * 5 + [ANY] * len(after),
        out_specs=VM,
        out_shape=jax.ShapeDtypeStruct((1, ROWS), F32),
        compiler_params=params(6),
        cost_estimate=cost(2 * ROWS * COLS, 1),
        name="mate_row_sums",
    )(*[in_vmem(m) for m in mates], col_total, *after)


def col_kernel(exps_ref, row_total_ref, *refs):
    col_ref, weight_ref = refs[-2:]
    weight = 1.0 / row_total_ref[0:1, :]
    weight_ref[...] = jnp.broadcast_to(weight, (128, ROWS)).T
    for j in range(COLS // 128):
        e = exps_ref[:, j * 128 : (j + 1) * 128]
        col_ref[:, j * 128 : (j + 1) * 128] = jnp.sum(
            (e * e) * weight_ref[...], axis=0, keepdims=True
        )


def col_sums(exps, row_total, early, after):
    return pl.pallas_call(
        col_kernel,
        in_specs=[VM, VM] + [VM] * len(early) + [ANY] * len(after),
        out_specs=VM,
        out_shape=jax.ShapeDtypeStruct((1, COLS), F32),
        scratch_shapes=[pltpu.VMEM((ROWS, 128), F32)],
        compiler_params=params(6),
        cost_estimate=cost(3 * ROWS * COLS, 1),
        name="col_sums",
    )(in_vmem(exps), row_total, *[in_vmem(v) for v in early], *after)


def mate_rows(x, mate):
    pick = (lax.broadcasted_iota(jnp.int32, (ROWS, ROWS), 0).astype(F32) == mate).astype(BF16)
    return jnp.dot(pick, x, preferred_element_type=F32).astype(BF16)


def block_out(place, x, mate, protos_ref, exps_ref, mates_ref, turned_ref, turn):
    xm = mate_rows(x, mate)
    for j in range(0, QUARTER, 256):
        at = pl.ds(pl.multiple_of(place[0] * QUARTER + j, 256), 256)
        protos = protos_ref[:, at]
        exps_ref[:, j : j + 256] = jnp.exp(
            jnp.dot(x, protos, preferred_element_type=F32) * (1.0 / sharpness_divisor)
        )
        mates_ref[:, j : j + 256] = jnp.exp(
            jnp.dot(xm, protos, preferred_element_type=F32) * (1.0 / code_eps)
        )
    turn[...] = x.astype(F32).T
    for o in range(NZ):
        for p in range(NY):
            to = lax.rem(place[0] + p, NY) * NZ + lax.rem(place[1] + o, NZ)
            rows = turn[pl.ds(pl.multiple_of(to * 32, 32), 32), :]
            at = o * 128 + p * 32
            turned_ref[at : at + 32, :] = rows.astype(BF16)
    return xm


def own_block_kernel(
    place, unit_ref, mate_ref, protos_ref, exps_ref, mates_ref, turned_ref, xm_ref, turn
):
    xm_ref[...] = block_out(
        place, unit_ref[...], mate_ref[...], protos_ref, exps_ref, mates_ref, turned_ref, turn
    )


def far_block_kernel(
    place, same_ref, other_ref, protos_ref, exps_ref, mates_ref, turned_ref, flag_ref, turn, held
):
    flag_ref[...] = jnp.zeros_like(flag_ref)
    half = ROWS // 2
    core = place[3]
    held[pl.ds(pl.multiple_of(core * half, half), half), :] = same_ref[:half, :].astype(BF16)
    held[pl.ds(pl.multiple_of((1 - core) * half, half), half), :] = other_ref[:half, :].astype(BF16)
    block_out(
        place,
        held[...],
        same_ref[half : half + 1, :ROWS],
        protos_ref,
        exps_ref,
        mates_ref,
        turned_ref,
        turn,
    )


def block_call(place, a, b, protos, own):
    shapes = [
        pltpu.VMEM((ROWS, QUARTER), F32),
        pltpu.VMEM((ROWS, QUARTER), F32),
        pltpu.VMEM((D, ROWS), BF16),
    ]
    scratch = [pltpu.VMEM((D, ROWS), F32)]
    if own:
        shapes.append(pltpu.VMEM((ROWS, D), BF16))
    else:
        shapes.append(jax.ShapeDtypeStruct((1, 128), F32))
        scratch.append(pltpu.VMEM((ROWS, D), BF16))
    return pl.pallas_call(
        own_block_kernel if own else far_block_kernel,
        in_specs=[pl.BlockSpec(memory_space=pltpu.SMEM), VM, VM, VM],
        out_specs=[VM] * len(shapes),
        scratch_shapes=scratch,
        out_shape=shapes,
        compiler_params=params(9),
        cost_estimate=cost(4 * ROWS * QUARTER * D, 4, 2 * ROWS * QUARTER),
        name="own_block" if own else "far_block",
    )(place, in_vmem(a) if own else a, b, in_vmem(protos))


def mate_piece_kernel(q, xm_ref, protos_ref, mates_ref):
    for j in range(0, QUARTER, 256):
        protos = protos_ref[:, q * QUARTER + j : q * QUARTER + j + 256]
        mates_ref[:, j : j + 256] = jnp.exp(
            jnp.dot(xm_ref[...], protos, preferred_element_type=F32) * (1.0 / code_eps)
        )


def mate_piece(xm, protos, q):
    return pl.pallas_call(
        functools.partial(mate_piece_kernel, q),
        in_specs=[VM, VM],
        out_specs=VM,
        out_shape=pltpu.VMEM((ROWS, QUARTER), F32),
        compiler_params=params(6),
        cost_estimate=cost(2 * ROWS * QUARTER * D, 2, ROWS * QUARTER),
        name="mate_piece",
    )(in_vmem(xm), in_vmem(protos))


def down(row):
    return jnp.broadcast_to(row, (128, ROWS)).T


def embed_grad_kernel(place, *refs):
    mates, refs = refs[2:6], refs[6:]
    col_total_ref, row_total_ref, plain_ref, protos_ref, embed_ref, scores_ref = refs[:6]
    mine, other = refs[6 : 6 + NX], refs[6 + NX : 6 + 2 * NX]
    total, match, soft, hard, grads = refs[6 + 2 * NX :]
    soft[...] = down((1.0 / sharpness_divisor) / plain_ref[...])
    hard[...] = down(1.0 / row_total_ref[...])
    match[...] = jnp.zeros_like(match)
    width = 512
    for t in range(COLS // width):
        for j in range(width // 128):
            first = t * width + j * 128
            inside = first % QUARTER
            weight = 1.0 / col_total_ref[:, first : first + 128]
            targets = mates[first // QUARTER][:, inside : inside + 128] * weight * hard[...]
            scores = scores_ref[:, first : first + 128]
            match[...] += targets * scores
            grads[t % 2, :, j * 128 : (j + 1) * 128] = (
                jnp.exp(scores * (1.0 / sharpness_divisor)) * soft[...]
                - targets * (1.0 / sharpness_divisor)
            ).astype(BF16)
        part = lax.dot_general(
            grads[t % 2],
            protos_ref[:, t * width : (t + 1) * width],
            (((1,), (1,)), ((), ())),
            preferred_element_type=F32,
        )
        if t == 0:
            total[...] = part
        else:
            total[...] += part

    raw = embed_ref[...].astype(F32)
    term = total[...]
    scale = lax.rsqrt(jnp.sum(raw * raw, axis=1, keepdims=True) + 1e-06)
    inner = jnp.sum(raw * term, axis=1, keepdims=True)
    total[...] = scale * term - (scale * scale * scale * inner) * raw
    matched = jnp.sum(match[...].T, axis=0, keepdims=True)
    for o in range(NX):
        to = lax.rem(place[2] + o, NX) * 2
        for core, ref in ((place[3], mine[o]), (1 - place[3], other[o])):
            at = pl.ds(pl.multiple_of((to + core) * 128, 128), 128)
            ref[:ROWS, :] = total[:, at]
            ref[ROWS:, :] = jnp.zeros((8, 128), F32)
            for t in range(ROWS // 128):
                ref[ROWS + t : ROWS + t + 1, :] = matched[:, t * 128 : (t + 1) * 128]


def embed_grad(place, after, mates, col_total, row_total, plain, protos, embed, scores):
    column = pltpu.VMEM((ROWS, 128), F32)
    return pl.pallas_call(
        embed_grad_kernel,
        in_specs=[pl.BlockSpec(memory_space=pltpu.SMEM)] + [ANY] * 2 + [VM] * 10,
        out_specs=[VM] * (2 * NX),
        scratch_shapes=[
            pltpu.VMEM((ROWS, D), F32),
            column,
            column,
            column,
            pltpu.VMEM((2, ROWS, 512), BF16),
        ],
        out_shape=[jax.ShapeDtypeStruct((ROWS + 8, 128), F32)] * (2 * NX),
        compiler_params=params(12),
        cost_estimate=cost(ROWS * COLS * D // 4, 1, ROWS * COLS // 8),
        name="embed_grad",
    )(
        place,
        *after,
        *[in_vmem(m) for m in mates],
        col_total,
        row_total,
        plain,
        in_vmem(protos),
        embed,
        in_vmem(scores),
    )


def first_chunk_kernel(place, *refs):
    exps, mates, scals = refs[0:4], refs[4:8], refs[8:12]
    turned, col_total_ref = refs[12:16], refs[16]
    grads, chunk_a, chunk_b = refs[17:20]
    at = pl.ds(pl.multiple_of(place[0] * QUARTER, QUARTER), QUARTER)
    weight = (1.0 / sharpness_divisor) / col_total_ref[:, at]
    total = None
    for b in range(NY):
        soft = down((1.0 / sharpness_divisor) / scals[b][1:2, :])
        hard = down(1.0 / scals[b][0:1, :])
        for j in range(QUARTER // 128):
            lanes = slice(j * 128, (j + 1) * 128)
            grads[b * ROWS : (b + 1) * ROWS, lanes] = (
                exps[b][:, lanes] * soft - mates[b][:, lanes] * weight[:, lanes] * hard
            ).astype(BF16)
        part = jnp.dot(
            turned[b][4 * 128 : 5 * 128, :],
            grads[b * ROWS : (b + 1) * ROWS, :],
            preferred_element_type=F32,
        )
        total = part if total is None else total + part
    chunk_a[...] = total[:, : QUARTER // 2]
    chunk_b[...] = total[:, QUARTER // 2 :]


def first_chunk(place, exps, mates, scals, turned, col_total):
    half = jax.ShapeDtypeStruct((128, QUARTER // 2), F32)
    return pl.pallas_call(
        first_chunk_kernel,
        in_specs=[pl.BlockSpec(memory_space=pltpu.SMEM)] + [VM] * 17,
        out_specs=[VM] * 3,
        out_shape=[pltpu.VMEM((WIDE, QUARTER), BF16), half, half],
        compiler_params=params(6),
        cost_estimate=cost(2 * 128 * WIDE * QUARTER + 6 * WIDE * QUARTER, 2),
        name="first_chunk",
    )(
        place,
        *[in_vmem(v) for v in exps],
        *[in_vmem(v) for v in mates],
        *scals,
        *[in_vmem(v) for v in turned],
        col_total,
    )


def chunks_kernel(offsets, t0, t1, t2, t3, grads, *outs):
    for o, out in zip(offsets, outs[-len(offsets) :]):
        total = None
        for b, turned in enumerate((t0, t1, t2, t3)):
            part = jnp.dot(
                turned[o * 128 : (o + 1) * 128, :],
                grads[b * ROWS : (b + 1) * ROWS, :],
                preferred_element_type=F32,
            )
            total = part if total is None else total + part
        out[...] = total


def chunks(turned, grads, offsets):
    return pl.pallas_call(
        functools.partial(chunks_kernel, offsets),
        in_specs=[VM] * 5,
        out_specs=[VM] * len(offsets),
        out_shape=[jax.ShapeDtypeStruct((128, QUARTER), F32)] * len(offsets),
        compiler_params=params(5),
        cost_estimate=cost(2 * 128 * WIDE * QUARTER * len(offsets) // 4, 1),
        name="chunks",
    )(*[in_vmem(v) for v in turned], in_vmem(grads))


def gather_kernel(place, r0, r1, r2, r3, out_ref):
    for o, ref in enumerate((r0, r1, r2, r3)):
        quarter = lax.rem(place[0] + NY - o, NY)
        out_ref[:, pl.ds(pl.multiple_of(quarter * QUARTER, QUARTER), QUARTER)] = ref[...]


def gather_quarters(place, quarters):
    return pl.pallas_call(
        gather_kernel,
        in_specs=[pl.BlockSpec(memory_space=pltpu.SMEM)] + [VM] * 4,
        out_specs=VM,
        out_shape=jax.ShapeDtypeStruct((32, COLS), F32),
        compiler_params=params(8),
        cost_estimate=cost(0, 1),
        name="gather_quarters",
    )(place, *quarters)


def finish_kernel(s0, s1, s2, s3, plain_ref, grad_ref, cost_ref):
    share = (s0[...] + s2[...]) + (s1[...] + s3[...])
    grad_ref[...] = share[:ROWS, :]
    for t in range(ROWS // 128):
        lanes = slice(t * 128, (t + 1) * 128)
        matched = share[ROWS + t : ROWS + t + 1, :]
        cost_ref[:, lanes] = jnp.log(plain_ref[:, lanes]) - matched * (1.0 / sharpness_divisor)


def finish_ordered(s0, s1, s2, s3, plain, after):
    def kernel(a, b, c, d, e, unread, grad_ref, cost_ref):
        finish_kernel(a, b, c, d, e, grad_ref, cost_ref)

    return pl.pallas_call(
        kernel,
        in_specs=[VM] * 5 + [ANY],
        out_specs=[VM, VM],
        out_shape=[
            jax.ShapeDtypeStruct((ROWS, 128), F32),
            jax.ShapeDtypeStruct((1, ROWS), F32),
        ],
        compiler_params=params(6),
        cost_estimate=cost(4 * ROWS * 128, 1),
        name="finish",
    )(s0, s1, s2, s3, plain, after)


def local(embed, prototypes, partner):
    dp, proto = lax.axis_index("dp"), lax.axis_index("proto")
    place = jnp.stack([dp // NZ, dp % NZ, proto // 2, proto % 2]).astype(jnp.int32)
    mate = (partner - dp * ROWS).astype(F32).reshape(1, ROWS)
    unit, pay = unit_rows(place, embed, mate)
    exps, scores, col_part, protos = first_scores(unit, prototypes)

    from_left, from_right = move_y(pay, 1), move_y(pay, -1)

    col_total = sum_dp(col_part, [from_left, from_right])
    low, high = second_hop(from_left, from_right, [col_total])
    far = jnp.concatenate([move_y(low, 1), move_y(high, -1)], axis=0)
    same = [from_left, far, from_right]
    crossed = [move_core(v) for v in same]
    row_total = sum_proto(row_sums(exps, col_total, True, []))
    plain = row_total[1:2]
    blocks = [block_call(place, unit, mate, protos, True)]
    blocks += [block_call(place, v, w, protos, False) for v, w in zip(same, crossed)]
    xm = blocks[0][3]
    mates = [mate_piece(xm, protos, q) for q in range(NY)]

    col_total = sum_dp(col_sums(exps, row_total, [], []), [], [far])
    row_total = sum_proto(row_sums(exps, col_total, False, [crossed[0], crossed[2]]))
    col_total = sum_dp(col_sums(exps, row_total, mates, []))
    row_total = sum_proto(mate_row_sums(mates, col_total, [b[3] for b in blocks[1:]]))

    scal = jnp.concatenate([row_total, plain], axis=0)
    scals = [scal, move_y(scal, 1), move_y(scal, 2), move_y(scal, -1)]

    turned = [b[2] for b in blocks]
    grads, up, back = first_chunk(
        place, [b[0] for b in blocks], [b[1] for b in blocks], scals, turned, col_total
    )
    half = QUARTER // 2
    up, back = move_z(up, 1), move_z(back, -1)
    c3, c5 = chunks(turned, grads, (3, 5))
    parts = embed_grad(
        place, (up, back), mates, col_total, row_total, plain, protos, embed, scores
    )
    up = jnp.concatenate([c3[:, :half] + up, c3[:, half:]], axis=1)
    back = jnp.concatenate([c5[:, :half], c5[:, half:] + back], axis=1)
    up, back = move_z(up, 1), move_z(back, -1)
    c2, c6 = chunks(turned, grads, (2, 6))
    up, back = add([up, c2], parts[:1]), add([back, c6], parts[:1])
    up, back = move_z(up, 1), move_z(back, -1)
    c1, c7 = chunks(turned, grads, (1, 7))
    up, back = up + c1, back + c7
    up, back = move_z(up, 1), move_z(back, -1)
    shares = [parts[o] + move_core(parts[NX + o]) for o in range(NX)]
    moved = [move_x(shares[o], o) for o in (1, 2, 3)]
    (c0,) = chunks(turned, grads, (0,))
    done = add([c0, up, back], shares)
    quarters = [done[:32]] + [move_y(done[32 * o : 32 * o + 32], o) for o in (1, 2, 3)]
    grad_protos = gather_quarters(place, quarters)

    grad_embed, view_swapped_cost = finish_ordered(shares[0], *moved, plain, quarters[2])
    return (grad_embed, grad_protos, view_swapped_cost.reshape(ROWS))


def solution(mesh):
    placed = (P("dp", None), P(None, "proto"), P("dp"))
    return jax.shard_map(
        local,
        mesh=mesh,
        in_specs=placed,
        out_specs=(P("dp", "proto"), P("dp", "proto"), P("dp")),
        check_vma=False,
    )
```

```python
import functools

import jax
import jax.numpy as jnp
from jax import lax
from jax.experimental import pallas as pl
from jax.experimental.pallas import tpu as pltpu
from jax.sharding import PartitionSpec as P

NY, NZ, NX = 4, 8, 4
ROWS, COLS, D = 512, 4096, 1024
WIDE, QUARTER, PAY = 2048, 1024, 264
F32, BF16 = jnp.float32, jnp.bfloat16
MIB = 1 << 20


code_eps = 0.05
sharpness_divisor = 0.1


def dp_pairs(f):
    pairs = []
    for y in range(NY):
        for z in range(NZ):
            to_y, to_z = f(y, z)
            pairs.append((y * NZ + z, (to_y % NY) * NZ + to_z % NZ))
    return pairs


def proto_pairs(f):
    pairs = []
    for x in range(NX):
        for core in range(2):
            to_x, to_core = f(x, core)
            pairs.append((x * 2 + core, (to_x % NX) * 2 + to_core % 2))
    return pairs


def move_y(v, off):
    return lax.ppermute(v, "dp", dp_pairs(lambda y, z: (y + off, z)))


def move_z(v, off):
    return lax.ppermute(v, "dp", dp_pairs(lambda y, z: (y, z + off)))


def move_x(v, off):
    return lax.ppermute(v, "proto", proto_pairs(lambda x, c: (x + off, c)))


def move_core(v):
    return lax.ppermute(v, "proto", proto_pairs(lambda x, c: (x, c + 1)))


def sum_y(v):
    return (v + move_y(v, 2)) + (move_y(v, 1) + move_y(v, -1))


def sum_z(v, after=(), early=()):
    left, right = move_z(v, 1), move_z(v, -1)
    two = add([v, right], early) if early else v + right
    three = left + two
    terms = [three, move_z(three, -3), move_z(two, 3)]
    if after:
        return add(terms, after)
    return terms[0] + (terms[1] + terms[2])


def sum_x(v):
    return (v + move_x(v, 2)) + (move_x(v, 1) + move_x(v, -1))


def sum_core(v):
    return v + move_core(v)


def sum_dp(v, after=(), early=()):
    return sum_y(sum_z(v, after, early))


def sum_proto(v):
    return sum_x(sum_core(v))


def in_vmem(v):
    return pltpu.with_memory_space_constraint(v, pltpu.VMEM)


def in_hbm(v):
    return pltpu.with_memory_space_constraint(v, pltpu.HBM)


VM = pl.BlockSpec(memory_space=pltpu.VMEM)
ANY = pl.BlockSpec(memory_space=pl.ANY)


def params(mib):
    return pltpu.CompilerParams(vmem_limit_bytes=mib * MIB)


def cost(flops, mib, exps=0):
    return pl.CostEstimate(flops=flops, bytes_accessed=mib * MIB, transcendentals=exps)


def unit_kernel(place, embed_ref, mate_ref, unit_ref, pay_ref):
    raw = embed_ref[...].astype(F32)
    scale = lax.rsqrt(jnp.sum(raw * raw, axis=1, keepdims=True) + 1e-06)
    unit_ref[...] = (raw * scale).astype(BF16)
    half = pl.ds(pl.multiple_of(place[3] * (ROWS // 2), ROWS // 2), ROWS // 2)
    pay_ref[: ROWS // 2, :] = unit_ref[half, :].astype(F32)
    pay_ref[ROWS // 2 :, :ROWS] = jnp.broadcast_to(mate_ref[...], (8, ROWS))
    pay_ref[ROWS // 2 :, ROWS:] = jnp.zeros((8, D - ROWS), F32)


def unit_rows(place, embed, mate):
    return pl.pallas_call(
        unit_kernel,
        in_specs=[pl.BlockSpec(memory_space=pltpu.SMEM), VM, VM],
        out_specs=[VM, VM],
        out_shape=[pltpu.VMEM((ROWS, D), BF16), jax.ShapeDtypeStruct((PAY, D), F32)],
        compiler_params=params(12),
        cost_estimate=cost(4 * ROWS * D, 3),
        name="unit_rows",
    )(place, embed, mate)


def scores_kernel(unit_ref, protos_ref, exps_ref, col_ref, protos_out):
    raw = protos_ref[...].astype(F32)
    scale = lax.rsqrt(jnp.sum(raw * raw, axis=0, keepdims=True) + 1e-06)
    unit_protos = (raw * scale).astype(BF16)
    scores = jnp.dot(unit_ref[...], unit_protos, preferred_element_type=F32)
    exps = jnp.exp(scores * (1.0 / sharpness_divisor))
    width = scores.shape[1]
    at = pl.ds(pl.multiple_of(pl.program_id(0) * width, width), width)
    protos_out[:, at] = unit_protos
    exps_ref[:, at] = exps
    col_ref[:, at] = jnp.sum(exps * exps, axis=0, keepdims=True)


def first_scores(unit, prototypes, block=1024):
    return pl.pallas_call(
        scores_kernel,
        grid=(COLS // block,),
        in_specs=[VM, pl.BlockSpec((D, block), lambda j: (0, j))],
        out_specs=[VM, VM, VM],
        out_shape=[
            pltpu.VMEM((ROWS, COLS), F32),
            jax.ShapeDtypeStruct((1, COLS), F32),
            pltpu.VMEM((D, COLS), BF16),
        ],
        compiler_params=params(24),
        cost_estimate=cost(2 * ROWS * COLS * D, 8, ROWS * COLS),
        name="first_scores",
    )(in_vmem(unit), in_hbm(prototypes))


def add_kernel(n, *refs):
    total = refs[0][...]
    for ref in refs[1:n]:
        total += ref[...]
    refs[-1][...] = total


def add(terms, after):
    return pl.pallas_call(
        functools.partial(add_kernel, len(terms)),
        in_specs=[VM] * len(terms) + [ANY] * len(after),
        out_specs=VM,
        out_shape=jax.ShapeDtypeStruct(terms[0].shape, F32),
        compiler_params=params(6),
        cost_estimate=cost(terms[0].size * len(terms), 1),
        name="add",
    )(*terms, *after)


def hop_kernel(left_ref, right_ref, *refs):
    low_ref, high_ref = refs[-2:]
    low_ref[...] = left_ref[:128, :]
    high_ref[...] = right_ref[128:, :]


def second_hop(left, right, after):
    return pl.pallas_call(
        hop_kernel,
        in_specs=[VM, VM] + [ANY] * len(after),
        out_specs=[VM, VM],
        out_shape=[
            jax.ShapeDtypeStruct((128, D), F32),
            jax.ShapeDtypeStruct((PAY - 128, D), F32),
        ],
        compiler_params=params(8),
        cost_estimate=cost(ROWS * D, 2),
        name="second_hop",
    )(left, right, *after)


def lanes_to_row(parts):
    return jnp.sum(jnp.concatenate(parts, axis=0).T, axis=0, keepdims=True)


def row_kernel(with_plain, exps_ref, col_total_ref, *refs):
    row_ref = refs[-1]
    weight = 1.0 / col_total_ref[...]
    rows = 64
    parts, plain_parts = [], []
    for i in range(ROWS // rows):
        total = jnp.zeros((rows, 128), F32)
        plain = jnp.zeros((rows, 128), F32)
        for j in range(COLS // 128):
            e = exps_ref[i * rows : (i + 1) * rows, j * 128 : (j + 1) * 128]
            total += (e * e) * weight[:, j * 128 : (j + 1) * 128]
            if with_plain:
                plain += e
        parts.append(total)
        plain_parts.append(plain)
    row_ref[0:1, :] = lanes_to_row(parts)
    if with_plain:
        row_ref[1:2, :] = lanes_to_row(plain_parts)


def row_sums(exps, col_total, with_plain, after):
    return pl.pallas_call(
        functools.partial(row_kernel, with_plain),
        in_specs=[VM, VM] + [ANY] * len(after),
        out_specs=VM,
        out_shape=jax.ShapeDtypeStruct((2 if with_plain else 1, ROWS), F32),
        compiler_params=params(6),
        cost_estimate=cost(3 * ROWS * COLS, 1),
        name="row_sums",
    )(in_vmem(exps), col_total, *after)


def mate_row_kernel(a0, a1, a2, a3, col_total_ref, *refs):
    row_ref = refs[-1]
    weight = 1.0 / col_total_ref[...]
    rows = 64
    parts = []
    for i in range(ROWS // rows):
        total = jnp.zeros((rows, 128), F32)
        for q, a in enumerate((a0, a1, a2, a3)):
            for j in range(QUARTER // 128):
                at = q * QUARTER + j * 128
                total += (
                    a[i * rows : (i + 1) * rows, j * 128 : (j + 1) * 128] * weight[:, at : at + 128]
                )
        parts.append(total)
    row_ref[...] = lanes_to_row(parts)


def mate_row_sums(mates, col_total, after):
    return pl.pallas_call(
        mate_row_kernel,
        in_specs=[VM] * 5 + [ANY] * len(after),
        out_specs=VM,
        out_shape=jax.ShapeDtypeStruct((1, ROWS), F32),
        compiler_params=params(6),
        cost_estimate=cost(2 * ROWS * COLS, 1),
        name="mate_row_sums",
    )(*[in_vmem(m) for m in mates], col_total, *after)


def col_kernel(exps_ref, row_total_ref, *refs):
    col_ref, weight_ref = refs[-2:]
    weight = 1.0 / row_total_ref[0:1, :]
    weight_ref[...] = jnp.broadcast_to(weight, (128, ROWS)).T
    for j in range(COLS // 128):
        e = exps_ref[:, j * 128 : (j + 1) * 128]
        col_ref[:, j * 128 : (j + 1) * 128] = jnp.sum(
            (e * e) * weight_ref[...], axis=0, keepdims=True
        )


def col_sums(exps, row_total, early, after):
    return pl.pallas_call(
        col_kernel,
        in_specs=[VM, VM] + [VM] * len(early) + [ANY] * len(after),
        out_specs=VM,
        out_shape=jax.ShapeDtypeStruct((1, COLS), F32),
        scratch_shapes=[pltpu.VMEM((ROWS, 128), F32)],
        compiler_params=params(6),
        cost_estimate=cost(3 * ROWS * COLS, 1),
        name="col_sums",
    )(in_vmem(exps), row_total, *[in_vmem(v) for v in early], *after)


def mate_rows(x, mate):
    pick = (lax.broadcasted_iota(jnp.int32, (ROWS, ROWS), 0).astype(F32) == mate).astype(BF16)
    return jnp.dot(pick, x, preferred_element_type=F32).astype(BF16)


def turn_rows(place, x, turned_ref, turn):
    turn[...] = x.T
    for o in range(NZ):
        for p in range(NY):
            to = lax.rem(place[0] + p, NY) * NZ + lax.rem(place[1] + o, NZ)
            at = o * 128 + p * 32
            turned_ref[at : at + 32, :] = turn[pl.ds(pl.multiple_of(to * 32, 32), 32), :]


def own_block_kernel(place, unit_ref, mate_ref, turned_ref, xm_ref, turn):
    xm_ref[...] = mate_rows(unit_ref[...], mate_ref[...])
    turn_rows(place, unit_ref[...], turned_ref, turn)


def own_block(place, unit, mate):
    return pl.pallas_call(
        own_block_kernel,
        in_specs=[pl.BlockSpec(memory_space=pltpu.SMEM), VM, VM],
        out_specs=[VM, VM],
        scratch_shapes=[pltpu.VMEM((D, ROWS), BF16)],
        out_shape=[pltpu.VMEM((D, ROWS), BF16), pltpu.VMEM((ROWS, D), BF16)],
        compiler_params=params(7),
        cost_estimate=cost(2 * ROWS * ROWS * D, 4),
        name="own_block",
    )(place, in_vmem(unit), mate)


def far_block_kernel(
    place, same_ref, other_ref, protos_ref, exps_ref, mates_ref, turned_ref, flag_ref, turn, held
):
    flag_ref[...] = jnp.zeros_like(flag_ref)
    half = ROWS // 2
    core = place[3]
    held[pl.ds(pl.multiple_of(core * half, half), half), :] = same_ref[:half, :].astype(BF16)
    held[pl.ds(pl.multiple_of((1 - core) * half, half), half), :] = other_ref[:half, :].astype(BF16)
    x = held[...]
    xm = mate_rows(x, same_ref[half : half + 1, :ROWS])
    for j in range(0, QUARTER, 256):
        at = pl.ds(pl.multiple_of(place[0] * QUARTER + j, 256), 256)
        protos = protos_ref[:, at]
        exps_ref[:, j : j + 256] = jnp.exp(
            jnp.dot(x, protos, preferred_element_type=F32) * (1.0 / sharpness_divisor)
        )
        mates_ref[:, j : j + 256] = jnp.exp(
            jnp.dot(xm, protos, preferred_element_type=F32) * (1.0 / code_eps)
        )
    turn_rows(place, x, turned_ref, turn)


def far_block(place, same, other, protos):
    return pl.pallas_call(
        far_block_kernel,
        in_specs=[pl.BlockSpec(memory_space=pltpu.SMEM), VM, VM, VM],
        out_specs=[VM] * 4,
        scratch_shapes=[pltpu.VMEM((D, ROWS), BF16), pltpu.VMEM((ROWS, D), BF16)],
        out_shape=[
            pltpu.VMEM((ROWS, QUARTER), F32),
            pltpu.VMEM((ROWS, QUARTER), F32),
            pltpu.VMEM((D, ROWS), BF16),
            jax.ShapeDtypeStruct((1, 128), F32),
        ],
        compiler_params=params(7),
        cost_estimate=cost(4 * ROWS * QUARTER * D, 4, 2 * ROWS * QUARTER),
        name="far_block",
    )(place, same, other, in_vmem(protos))


def mate_piece_kernel(q, xm_ref, protos_ref, mates_ref):
    for j in range(0, QUARTER, 256):
        protos = protos_ref[:, q * QUARTER + j : q * QUARTER + j + 256]
        mates_ref[:, j : j + 256] = jnp.exp(
            jnp.dot(xm_ref[...], protos, preferred_element_type=F32) * (1.0 / code_eps)
        )


def mate_piece(xm, protos, q):
    return pl.pallas_call(
        functools.partial(mate_piece_kernel, q),
        in_specs=[VM, VM],
        out_specs=VM,
        out_shape=pltpu.VMEM((ROWS, QUARTER), F32),
        compiler_params=params(6),
        cost_estimate=cost(2 * ROWS * QUARTER * D, 2, ROWS * QUARTER),
        name="mate_piece",
    )(in_vmem(xm), in_vmem(protos))


def down(row):
    return jnp.broadcast_to(row, (128, ROWS)).T


def embed_grad_kernel(place, *refs):
    mates, refs = refs[2:6], refs[6:]
    col_total_ref, row_total_ref, plain_ref, protos_ref, embed_ref, exps_ref = refs[:6]
    mine, other = refs[6 : 6 + NX], refs[6 + NX : 6 + 2 * NX]
    total, match, soft, hard, grads = refs[6 + 2 * NX :]
    soft[...] = down((1.0 / sharpness_divisor) / plain_ref[...])
    hard[...] = down(1.0 / row_total_ref[...])
    match[...] = jnp.zeros_like(match)
    width = 512
    for t in range(COLS // width):
        for j in range(width // 128):
            first = t * width + j * 128
            inside = first % QUARTER
            weight = 1.0 / col_total_ref[:, first : first + 128]
            targets = mates[first // QUARTER][:, inside : inside + 128] * weight * hard[...]
            exps = exps_ref[:, first : first + 128]
            match[...] += targets * (jnp.log(exps) * sharpness_divisor)
            grads[t % 2, :, j * 128 : (j + 1) * 128] = (
                exps * soft[...] - targets * (1.0 / sharpness_divisor)
            ).astype(BF16)
        part = lax.dot_general(
            grads[t % 2],
            protos_ref[:, t * width : (t + 1) * width],
            (((1,), (1,)), ((), ())),
            preferred_element_type=F32,
        )
        if t == 0:
            total[...] = part
        else:
            total[...] += part

    raw = embed_ref[...].astype(F32)
    term = total[...]
    scale = lax.rsqrt(jnp.sum(raw * raw, axis=1, keepdims=True) + 1e-06)
    inner = jnp.sum(raw * term, axis=1, keepdims=True)
    total[...] = scale * term - (scale * scale * scale * inner) * raw
    matched = jnp.sum(match[...].T, axis=0, keepdims=True)
    for o in range(NX):
        to = lax.rem(place[2] + o, NX) * 2
        for core, ref in ((place[3], mine[o]), (1 - place[3], other[o])):
            at = pl.ds(pl.multiple_of((to + core) * 128, 128), 128)
            ref[:ROWS, :] = total[:, at]
            ref[ROWS:, :] = jnp.zeros((8, 128), F32)
            for t in range(ROWS // 128):
                ref[ROWS + t : ROWS + t + 1, :] = matched[:, t * 128 : (t + 1) * 128]


def embed_grad(place, after, mates, col_total, row_total, plain, protos, embed, exps):
    column = pltpu.VMEM((ROWS, 128), F32)
    return pl.pallas_call(
        embed_grad_kernel,
        in_specs=[pl.BlockSpec(memory_space=pltpu.SMEM)] + [ANY] * 2 + [VM] * 10,
        out_specs=[VM] * (2 * NX),
        scratch_shapes=[
            pltpu.VMEM((ROWS, D), F32),
            column,
            column,
            column,
            pltpu.VMEM((2, ROWS, 512), BF16),
        ],
        out_shape=[jax.ShapeDtypeStruct((ROWS + 8, 128), F32)] * (2 * NX),
        compiler_params=params(12),
        cost_estimate=cost(ROWS * COLS * D // 4, 1, ROWS * COLS // 8),
        name="embed_grad",
    )(
        place,
        *after,
        *[in_vmem(m) for m in mates],
        col_total,
        row_total,
        plain,
        in_vmem(protos),
        embed,
        in_vmem(exps),
    )


def first_chunk_kernel(place, own_exps, *refs):
    own_mates, exps, mates, scals = refs[0:4], refs[4:7], refs[7:10], refs[10:14]
    turned, col_total_ref = refs[14:18], refs[18]
    grads, chunk_a, chunk_b = refs[19:22]
    at = pl.ds(pl.multiple_of(place[0] * QUARTER, QUARTER), QUARTER)
    weight = (1.0 / sharpness_divisor) / col_total_ref[:, at]

    def fill(b, exps_ref, first, mates_ref):
        soft = down((1.0 / sharpness_divisor) / scals[b][1:2, :])
        hard = down(1.0 / scals[b][0:1, :])
        for j in range(QUARTER // 128):
            lanes = slice(j * 128, (j + 1) * 128)
            e = exps_ref[:, first + j * 128 : first + (j + 1) * 128]
            grads[b * ROWS : (b + 1) * ROWS, lanes] = (
                e * soft - mates_ref[:, lanes] * weight[:, lanes] * hard
            ).astype(BF16)

    for q in range(NY):

        @pl.when(place[0] == q)
        def _():
            fill(0, own_exps, q * QUARTER, own_mates[q])

    total = None
    for b in range(NY):
        if b:
            fill(b, exps[b - 1], 0, mates[b - 1])
        part = jnp.dot(
            turned[b][4 * 128 : 5 * 128, :],
            grads[b * ROWS : (b + 1) * ROWS, :],
            preferred_element_type=F32,
        )
        total = part if total is None else total + part
    chunk_a[...] = total[:, : QUARTER // 2]
    chunk_b[...] = total[:, QUARTER // 2 :]


def first_chunk(place, own_exps, own_mates, far_blocks, scals, turned, col_total):
    half = jax.ShapeDtypeStruct((128, QUARTER // 2), F32)
    return pl.pallas_call(
        first_chunk_kernel,
        in_specs=[pl.BlockSpec(memory_space=pltpu.SMEM)] + [VM] * 20,
        out_specs=[VM] * 3,
        out_shape=[pltpu.VMEM((WIDE, QUARTER), BF16), half, half],
        compiler_params=params(6),
        cost_estimate=cost(2 * 128 * WIDE * QUARTER + 6 * WIDE * QUARTER, 2),
        name="first_chunk",
    )(
        place,
        in_vmem(own_exps),
        *[in_vmem(v) for v in own_mates],
        *[in_vmem(b[0]) for b in far_blocks],
        *[in_vmem(b[1]) for b in far_blocks],
        *scals,
        *[in_vmem(v) for v in turned],
        col_total,
    )


def chunks_kernel(offsets, t0, t1, t2, t3, grads, *outs):
    for o, out in zip(offsets, outs[-len(offsets) :]):
        total = None
        for b, turned in enumerate((t0, t1, t2, t3)):
            part = jnp.dot(
                turned[o * 128 : (o + 1) * 128, :],
                grads[b * ROWS : (b + 1) * ROWS, :],
                preferred_element_type=F32,
            )
            total = part if total is None else total + part
        out[...] = total


def chunks(turned, grads, offsets):
    return pl.pallas_call(
        functools.partial(chunks_kernel, offsets),
        in_specs=[VM] * 5,
        out_specs=[VM] * len(offsets),
        out_shape=[jax.ShapeDtypeStruct((128, QUARTER), F32)] * len(offsets),
        compiler_params=params(5),
        cost_estimate=cost(2 * 128 * WIDE * QUARTER * len(offsets) // 4, 1),
        name="chunks",
    )(*[in_vmem(v) for v in turned], in_vmem(grads))


def gather_kernel(place, r0, r1, r2, r3, out_ref, flag_ref):
    flag_ref[...] = jnp.zeros_like(flag_ref)
    for o, ref in enumerate((r0, r1, r2, r3)):
        quarter = lax.rem(place[0] + NY - o, NY)
        out_ref[:, pl.ds(pl.multiple_of(quarter * QUARTER, QUARTER), QUARTER)] = ref[...]


def gather_quarters(place, quarters):
    return pl.pallas_call(
        gather_kernel,
        in_specs=[pl.BlockSpec(memory_space=pltpu.SMEM)] + [VM] * 4,
        out_specs=[VM, VM],
        out_shape=[
            jax.ShapeDtypeStruct((32, COLS), F32),
            jax.ShapeDtypeStruct((1, 128), F32),
        ],
        compiler_params=params(8),
        cost_estimate=cost(0, 1),
        name="gather_quarters",
    )(place, *quarters)


def finish_kernel(s0, s1, s2, s3, plain_ref, grad_ref, cost_ref):
    share = (s0[...] + s2[...]) + (s1[...] + s3[...])
    grad_ref[...] = share[:ROWS, :]
    for t in range(ROWS // 128):
        lanes = slice(t * 128, (t + 1) * 128)
        matched = share[ROWS + t : ROWS + t + 1, :]
        cost_ref[:, lanes] = jnp.log(plain_ref[:, lanes]) - matched * (1.0 / sharpness_divisor)


def finish_ordered(s0, s1, s2, s3, plain, after):
    def kernel(a, b, c, d, e, unread, grad_ref, cost_ref):
        finish_kernel(a, b, c, d, e, grad_ref, cost_ref)

    return pl.pallas_call(
        kernel,
        in_specs=[VM] * 5 + [ANY],
        out_specs=[VM, VM],
        out_shape=[
            jax.ShapeDtypeStruct((ROWS, 128), F32),
            jax.ShapeDtypeStruct((1, ROWS), F32),
        ],
        compiler_params=params(6),
        cost_estimate=cost(4 * ROWS * 128, 1),
        name="finish",
    )(s0, s1, s2, s3, plain, after)


def local(embed, prototypes, partner):
    dp, proto = lax.axis_index("dp"), lax.axis_index("proto")
    place = jnp.stack([dp // NZ, dp % NZ, proto // 2, proto % 2]).astype(jnp.int32)
    mate = (partner - dp * ROWS).astype(F32).reshape(1, ROWS)
    unit, pay = unit_rows(place, embed, mate)
    exps, col_part, protos = first_scores(unit, prototypes)

    from_left, from_right = move_y(pay, 1), move_y(pay, -1)

    col_total = sum_dp(col_part, [from_left, from_right])
    low, high = second_hop(from_left, from_right, [col_total])
    far = jnp.concatenate([move_y(low, 1), move_y(high, -1)], axis=0)
    same = [from_left, far, from_right]
    crossed = [move_core(v) for v in same]
    row_total = sum_proto(row_sums(exps, col_total, True, []))
    plain = row_total[1:2]
    own_turned, xm = own_block(place, unit, mate)
    far_blocks = [far_block(place, v, w, protos) for v, w in zip(same, crossed)]
    mates = [mate_piece(xm, protos, q) for q in range(NY)]

    col_total = sum_dp(col_sums(exps, row_total, [], []), [], [far])
    row_total = sum_proto(row_sums(exps, col_total, False, [crossed[0], crossed[2]]))
    col_total = sum_dp(col_sums(exps, row_total, mates, []), [far_blocks[2][3]], [far_blocks[0][3]])
    row_total = sum_proto(mate_row_sums(mates, col_total, [far_blocks[1][3]]))

    scal = jnp.concatenate([row_total, plain], axis=0)
    scals = [scal, move_y(scal, 1), move_y(scal, 2), move_y(scal, -1)]

    turned = [own_turned] + [b[2] for b in far_blocks]
    grads, up, back = first_chunk(
        place, exps, mates, far_blocks, scals, turned, col_total
    )
    half = QUARTER // 2
    up, back = move_z(up, 1), move_z(back, -1)
    c3, c5 = chunks(turned, grads, (3, 5))
    parts = embed_grad(
        place, (up, back), mates, col_total, row_total, plain, protos, embed, exps
    )
    up = jnp.concatenate([c3[:, :half] + up, c3[:, half:]], axis=1)
    back = jnp.concatenate([c5[:, :half], c5[:, half:] + back], axis=1)
    up, back = move_z(up, 1), move_z(back, -1)
    c2, c6 = chunks(turned, grads, (2, 6))
    up, back = add([up, c2], parts[:1]), add([back, c6], parts[:1])
    up, back = move_z(up, 1), move_z(back, -1)
    c1, c7 = chunks(turned, grads, (1, 7))
    up, back = up + c1, back + c7
    up, back = move_z(up, 1), move_z(back, -1)
    shares = [parts[o] + move_core(parts[NX + o]) for o in range(NX)]
    moved = [move_x(shares[o], o) for o in (1, 2, 3)]
    (c0,) = chunks(turned, grads, (0,))
    done = add([c0, up, back], [*shares, moved[0]])
    quarters = [done[:32]] + [move_y(done[32 * o : 32 * o + 32], o) for o in (1, 2, 3)]
    grad_protos, flag = gather_quarters(place, quarters)

    grad_embed, view_swapped_cost = finish_ordered(shares[0], *moved, plain, flag)
    return (grad_embed, grad_protos, view_swapped_cost.reshape(ROWS))


def solution(mesh):
    placed = (P("dp", None), P(None, "proto"), P("dp"))
    return jax.shard_map(
        local,
        mesh=mesh,
        in_specs=placed,
        out_specs=(P("dp", "proto"), P("dp", "proto"), P("dp")),
        check_vma=False,
    )
```

```python
import functools

import jax
import jax.numpy as jnp
from jax import lax
from jax.experimental import pallas as pl
from jax.experimental.pallas import tpu as pltpu
from jax.sharding import PartitionSpec as P

NY, NZ, NX = 4, 8, 4
ROWS, COLS, D = 512, 4096, 1024
WIDE, QUARTER, PAY = 2048, 1024, 264
F32, BF16 = jnp.float32, jnp.bfloat16
MIB = 1 << 20


code_eps = 0.05
sharpness_divisor = 0.1


def dp_pairs(f):
    pairs = []
    for y in range(NY):
        for z in range(NZ):
            to_y, to_z = f(y, z)
            pairs.append((y * NZ + z, (to_y % NY) * NZ + to_z % NZ))
    return pairs


def proto_pairs(f):
    pairs = []
    for x in range(NX):
        for core in range(2):
            to_x, to_core = f(x, core)
            pairs.append((x * 2 + core, (to_x % NX) * 2 + to_core % 2))
    return pairs


def move_y(v, off):
    return lax.ppermute(v, "dp", dp_pairs(lambda y, z: (y + off, z)))


def move_z(v, off):
    return lax.ppermute(v, "dp", dp_pairs(lambda y, z: (y, z + off)))


def move_x(v, off):
    return lax.ppermute(v, "proto", proto_pairs(lambda x, c: (x + off, c)))


def move_core(v):
    return lax.ppermute(v, "proto", proto_pairs(lambda x, c: (x, c + 1)))


def sum_y(v):
    return (v + move_y(v, 2)) + (move_y(v, 1) + move_y(v, -1))


def sum_z(v, after=(), early=()):
    left, right = move_z(v, 1), move_z(v, -1)
    two = add([v, right], early) if early else v + right
    three = left + two
    terms = [three, move_z(three, -3), move_z(two, 3)]
    if after:
        return add(terms, after)
    return terms[0] + (terms[1] + terms[2])


def sum_x(v):
    return (v + move_x(v, 2)) + (move_x(v, 1) + move_x(v, -1))


def sum_core(v):
    return v + move_core(v)


def sum_dp(v, after=(), early=()):
    return sum_y(sum_z(v, after, early))


def sum_proto(v):
    return sum_x(sum_core(v))


def in_vmem(v):
    return pltpu.with_memory_space_constraint(v, pltpu.VMEM)


def in_hbm(v):
    return pltpu.with_memory_space_constraint(v, pltpu.HBM)


VM = pl.BlockSpec(memory_space=pltpu.VMEM)
ANY = pl.BlockSpec(memory_space=pl.ANY)


def params(mib):
    return pltpu.CompilerParams(vmem_limit_bytes=mib * MIB)


def cost(flops, mib, exps=0):
    return pl.CostEstimate(flops=flops, bytes_accessed=mib * MIB, transcendentals=exps)


def unit_kernel(place, embed_ref, mate_ref, unit_ref, pay_ref):
    raw = embed_ref[...].astype(F32)
    scale = lax.rsqrt(jnp.sum(raw * raw, axis=1, keepdims=True) + 1e-06)
    unit_ref[...] = (raw * scale).astype(BF16)
    half = pl.ds(pl.multiple_of(place[3] * (ROWS // 2), ROWS // 2), ROWS // 2)
    pay_ref[: ROWS // 2, :] = unit_ref[half, :].astype(F32)
    pay_ref[ROWS // 2 :, :ROWS] = jnp.broadcast_to(mate_ref[...], (8, ROWS))
    pay_ref[ROWS // 2 :, ROWS:] = jnp.zeros((8, D - ROWS), F32)


def unit_rows(place, embed, mate):
    return pl.pallas_call(
        unit_kernel,
        in_specs=[pl.BlockSpec(memory_space=pltpu.SMEM), VM, VM],
        out_specs=[VM, VM],
        out_shape=[pltpu.VMEM((ROWS, D), BF16), jax.ShapeDtypeStruct((PAY, D), F32)],
        compiler_params=params(12),
        cost_estimate=cost(4 * ROWS * D, 3),
        name="unit_rows",
    )(place, embed, mate)


def scores_kernel(unit_ref, protos_ref, exps_ref, scores_ref, col_ref, protos_out):
    raw = protos_ref[...].astype(F32)
    scale = lax.rsqrt(jnp.sum(raw * raw, axis=0, keepdims=True) + 1e-06)
    unit_protos = (raw * scale).astype(BF16)
    scores = jnp.dot(unit_ref[...], unit_protos, preferred_element_type=F32)
    exps = jnp.exp(scores * (1.0 / sharpness_divisor))
    scores_ref[...] = scores
    width = scores.shape[1]
    at = pl.ds(pl.multiple_of(pl.program_id(0) * width, width), width)
    protos_out[:, at] = unit_protos
    exps_ref[:, at] = exps
    col_ref[:, at] = jnp.sum(exps * exps, axis=0, keepdims=True)


def first_scores(unit, prototypes, block=1024):
    return pl.pallas_call(
        scores_kernel,
        grid=(COLS // block,),
        in_specs=[VM, pl.BlockSpec((D, block), lambda j: (0, j))],
        out_specs=[VM, pl.BlockSpec((ROWS, block), lambda j: (0, j)), VM, VM],
        out_shape=[
            pltpu.VMEM((ROWS, COLS), F32),
            pltpu.HBM((ROWS, COLS), F32),
            jax.ShapeDtypeStruct((1, COLS), F32),
            pltpu.VMEM((D, COLS), BF16),
        ],
        compiler_params=params(24),
        cost_estimate=cost(2 * ROWS * COLS * D, 8, ROWS * COLS),
        name="first_scores",
    )(in_vmem(unit), in_hbm(prototypes))


def add_kernel(n, *refs):
    total = refs[0][...]
    for ref in refs[1:n]:
        total += ref[...]
    refs[-1][...] = total


def add(terms, after):
    return pl.pallas_call(
        functools.partial(add_kernel, len(terms)),
        in_specs=[VM] * len(terms) + [ANY] * len(after),
        out_specs=VM,
        out_shape=jax.ShapeDtypeStruct(terms[0].shape, F32),
        compiler_params=params(6),
        cost_estimate=cost(terms[0].size * len(terms), 1),
        name="add",
    )(*terms, *after)


def hop_kernel(left_ref, right_ref, *refs):
    low_ref, high_ref = refs[-2:]
    low_ref[...] = left_ref[:128, :]
    high_ref[...] = right_ref[128:, :]


def second_hop(left, right, after):
    return pl.pallas_call(
        hop_kernel,
        in_specs=[VM, VM] + [ANY] * len(after),
        out_specs=[VM, VM],
        out_shape=[
            jax.ShapeDtypeStruct((128, D), F32),
            jax.ShapeDtypeStruct((PAY - 128, D), F32),
        ],
        compiler_params=params(8),
        cost_estimate=cost(ROWS * D, 2),
        name="second_hop",
    )(left, right, *after)


def lanes_to_row(parts):
    return jnp.sum(jnp.concatenate(parts, axis=0).T, axis=0, keepdims=True)


def row_kernel(with_plain, exps_ref, col_total_ref, *refs):
    row_ref = refs[-1]
    weight = 1.0 / col_total_ref[...]
    rows = 64
    parts, plain_parts = [], []
    for i in range(ROWS // rows):
        total = jnp.zeros((rows, 128), F32)
        plain = jnp.zeros((rows, 128), F32)
        for j in range(COLS // 128):
            e = exps_ref[i * rows : (i + 1) * rows, j * 128 : (j + 1) * 128]
            total += (e * e) * weight[:, j * 128 : (j + 1) * 128]
            if with_plain:
                plain += e
        parts.append(total)
        plain_parts.append(plain)
    row_ref[0:1, :] = lanes_to_row(parts)
    if with_plain:
        row_ref[1:2, :] = lanes_to_row(plain_parts)


def row_sums(exps, col_total, with_plain, after):
    return pl.pallas_call(
        functools.partial(row_kernel, with_plain),
        in_specs=[VM, VM] + [ANY] * len(after),
        out_specs=VM,
        out_shape=jax.ShapeDtypeStruct((2 if with_plain else 1, ROWS), F32),
        compiler_params=params(6),
        cost_estimate=cost(3 * ROWS * COLS, 1),
        name="row_sums",
    )(in_vmem(exps), col_total, *after)


def mate_row_kernel(a0, a1, a2, a3, col_total_ref, *refs):
    row_ref = refs[-1]
    weight = 1.0 / col_total_ref[...]
    rows = 64
    parts = []
    for i in range(ROWS // rows):
        total = jnp.zeros((rows, 128), F32)
        for q, a in enumerate((a0, a1, a2, a3)):
            for j in range(QUARTER // 128):
                at = q * QUARTER + j * 128
                total += (
                    a[i * rows : (i + 1) * rows, j * 128 : (j + 1) * 128] * weight[:, at : at + 128]
                )
        parts.append(total)
    row_ref[...] = lanes_to_row(parts)


def mate_row_sums(mates, col_total, after):
    return pl.pallas_call(
        mate_row_kernel,
        in_specs=[VM] * 5 + [ANY] * len(after),
        out_specs=VM,
        out_shape=jax.ShapeDtypeStruct((1, ROWS), F32),
        compiler_params=params(6),
        cost_estimate=cost(2 * ROWS * COLS, 1),
        name="mate_row_sums",
    )(*[in_vmem(m) for m in mates], col_total, *after)


def col_kernel(exps_ref, row_total_ref, *refs):
    col_ref, weight_ref = refs[-2:]
    weight = 1.0 / row_total_ref[0:1, :]
    weight_ref[...] = jnp.broadcast_to(weight, (128, ROWS)).T
    for j in range(COLS // 128):
        e = exps_ref[:, j * 128 : (j + 1) * 128]
        col_ref[:, j * 128 : (j + 1) * 128] = jnp.sum(
            (e * e) * weight_ref[...], axis=0, keepdims=True
        )


def col_sums(exps, row_total, early, after):
    return pl.pallas_call(
        col_kernel,
        in_specs=[VM, VM] + [VM] * len(early) + [ANY] * len(after),
        out_specs=VM,
        out_shape=jax.ShapeDtypeStruct((1, COLS), F32),
        scratch_shapes=[pltpu.VMEM((ROWS, 128), F32)],
        compiler_params=params(6),
        cost_estimate=cost(3 * ROWS * COLS, 1),
        name="col_sums",
    )(in_vmem(exps), row_total, *[in_vmem(v) for v in early], *after)


def mate_rows(x, mate):
    pick = (lax.broadcasted_iota(jnp.int32, (ROWS, ROWS), 0).astype(F32) == mate).astype(BF16)
    return jnp.dot(pick, x, preferred_element_type=F32).astype(BF16)


def turn_rows(place, x, turned_ref, turn):
    turn[...] = x.T
    for o in range(NZ):
        for p in range(NY):
            to = lax.rem(place[0] + p, NY) * NZ + lax.rem(place[1] + o, NZ)
            at = o * 128 + p * 32
            turned_ref[at : at + 32, :] = turn[pl.ds(pl.multiple_of(to * 32, 32), 32), :]


def own_block_kernel(place, unit_ref, mate_ref, exps_ref, turned_ref, xm_ref, quarter_ref, turn):
    at = pl.ds(pl.multiple_of(place[0] * QUARTER, QUARTER), QUARTER)
    quarter_ref[...] = exps_ref[:, at]
    xm_ref[...] = mate_rows(unit_ref[...], mate_ref[...])
    turn_rows(place, unit_ref[...], turned_ref, turn)


def own_block(place, unit, mate, exps):
    return pl.pallas_call(
        own_block_kernel,
        in_specs=[pl.BlockSpec(memory_space=pltpu.SMEM), VM, VM, VM],
        out_specs=[VM, VM, VM],
        scratch_shapes=[pltpu.VMEM((D, ROWS), BF16)],
        out_shape=[
            pltpu.VMEM((D, ROWS), BF16),
            pltpu.VMEM((ROWS, D), BF16),
            pltpu.VMEM((ROWS, QUARTER), F32),
        ],
        compiler_params=params(7),
        cost_estimate=cost(2 * ROWS * ROWS * D, 4),
        name="own_block",
    )(place, in_vmem(unit), mate, in_vmem(exps))


def far_block_kernel(
    place, same_ref, other_ref, protos_ref, exps_ref, mates_ref, turned_ref, flag_ref, turn, held
):
    flag_ref[...] = jnp.zeros_like(flag_ref)
    half = ROWS // 2
    core = place[3]
    held[pl.ds(pl.multiple_of(core * half, half), half), :] = same_ref[:half, :].astype(BF16)
    held[pl.ds(pl.multiple_of((1 - core) * half, half), half), :] = other_ref[:half, :].astype(BF16)
    x = held[...]
    xm = mate_rows(x, same_ref[half : half + 1, :ROWS])
    for j in range(0, QUARTER, 256):
        at = pl.ds(pl.multiple_of(place[0] * QUARTER + j, 256), 256)
        protos = protos_ref[:, at]
        exps_ref[:, j : j + 256] = jnp.exp(
            jnp.dot(x, protos, preferred_element_type=F32) * (1.0 / sharpness_divisor)
        )
        mates_ref[:, j : j + 256] = jnp.exp(
            jnp.dot(xm, protos, preferred_element_type=F32) * (1.0 / code_eps)
        )
    turn_rows(place, x, turned_ref, turn)


def far_block(place, same, other, protos):
    return pl.pallas_call(
        far_block_kernel,
        in_specs=[pl.BlockSpec(memory_space=pltpu.SMEM), VM, VM, VM],
        out_specs=[VM] * 4,
        scratch_shapes=[pltpu.VMEM((D, ROWS), BF16), pltpu.VMEM((ROWS, D), BF16)],
        out_shape=[
            pltpu.VMEM((ROWS, QUARTER), F32),
            pltpu.VMEM((ROWS, QUARTER), F32),
            pltpu.VMEM((D, ROWS), BF16),
            jax.ShapeDtypeStruct((1, 128), F32),
        ],
        compiler_params=params(7),
        cost_estimate=cost(4 * ROWS * QUARTER * D, 4, 2 * ROWS * QUARTER),
        name="far_block",
    )(place, same, other, in_vmem(protos))


def mate_piece_kernel(q, xm_ref, protos_ref, mates_ref):
    for j in range(0, QUARTER, 256):
        protos = protos_ref[:, q * QUARTER + j : q * QUARTER + j + 256]
        mates_ref[:, j : j + 256] = jnp.exp(
            jnp.dot(xm_ref[...], protos, preferred_element_type=F32) * (1.0 / code_eps)
        )


def mate_piece(xm, protos, q):
    return pl.pallas_call(
        functools.partial(mate_piece_kernel, q),
        in_specs=[VM, VM],
        out_specs=VM,
        out_shape=pltpu.VMEM((ROWS, QUARTER), F32),
        compiler_params=params(6),
        cost_estimate=cost(2 * ROWS * QUARTER * D, 2, ROWS * QUARTER),
        name="mate_piece",
    )(in_vmem(xm), in_vmem(protos))


def down(row):
    return jnp.broadcast_to(row, (128, ROWS)).T


def embed_grad_kernel(place, *refs):
    mates, refs = refs[2:6], refs[6:]
    col_total_ref, row_total_ref, plain_ref, protos_ref, embed_ref, scores_ref = refs[:6]
    mine, other = refs[6 : 6 + NX], refs[6 + NX : 6 + 2 * NX]
    total, match, soft, hard, grads = refs[6 + 2 * NX :]
    soft[...] = down((1.0 / sharpness_divisor) / plain_ref[...])
    hard[...] = down(1.0 / row_total_ref[...])
    match[...] = jnp.zeros_like(match)
    width = 512
    for t in range(COLS // width):
        for j in range(width // 128):
            first = t * width + j * 128
            inside = first % QUARTER
            weight = 1.0 / col_total_ref[:, first : first + 128]
            targets = mates[first // QUARTER][:, inside : inside + 128] * weight * hard[...]
            scores = scores_ref[:, first : first + 128]
            match[...] += targets * scores
            grads[t % 2, :, j * 128 : (j + 1) * 128] = (
                jnp.exp(scores * (1.0 / sharpness_divisor)) * soft[...]
                - targets * (1.0 / sharpness_divisor)
            ).astype(BF16)
        part = lax.dot_general(
            grads[t % 2],
            protos_ref[:, t * width : (t + 1) * width],
            (((1,), (1,)), ((), ())),
            preferred_element_type=F32,
        )
        if t == 0:
            total[...] = part
        else:
            total[...] += part

    raw = embed_ref[...].astype(F32)
    term = total[...]
    scale = lax.rsqrt(jnp.sum(raw * raw, axis=1, keepdims=True) + 1e-06)
    inner = jnp.sum(raw * term, axis=1, keepdims=True)
    total[...] = scale * term - (scale * scale * scale * inner) * raw
    matched = jnp.sum(match[...].T, axis=0, keepdims=True)
    for o in range(NX):
        to = lax.rem(place[2] + o, NX) * 2
        for core, ref in ((place[3], mine[o]), (1 - place[3], other[o])):
            at = pl.ds(pl.multiple_of((to + core) * 128, 128), 128)
            ref[:ROWS, :] = total[:, at]
            ref[ROWS:, :] = jnp.zeros((8, 128), F32)
            for t in range(ROWS // 128):
                ref[ROWS + t : ROWS + t + 1, :] = matched[:, t * 128 : (t + 1) * 128]


def embed_grad(place, after, mates, col_total, row_total, plain, protos, embed, scores):
    column = pltpu.VMEM((ROWS, 128), F32)
    return pl.pallas_call(
        embed_grad_kernel,
        in_specs=[pl.BlockSpec(memory_space=pltpu.SMEM)] + [ANY] * 2 + [VM] * 10,
        out_specs=[VM] * (2 * NX),
        scratch_shapes=[
            pltpu.VMEM((ROWS, D), F32),
            column,
            column,
            column,
            pltpu.VMEM((2, ROWS, 512), BF16),
        ],
        out_shape=[jax.ShapeDtypeStruct((ROWS + 8, 128), F32)] * (2 * NX),
        compiler_params=params(12),
        cost_estimate=cost(ROWS * COLS * D // 4, 1, ROWS * COLS // 8),
        name="embed_grad",
    )(
        place,
        *after,
        *[in_vmem(m) for m in mates],
        col_total,
        row_total,
        plain,
        in_vmem(protos),
        embed,
        in_vmem(scores),
    )


def first_chunk_kernel(place, own_exps, *refs):
    own_mates, exps, mates, scals = refs[0:4], refs[4:7], refs[7:10], refs[10:14]
    turned, col_total_ref = refs[14:18], refs[18]
    grads, chunk_a, chunk_b = refs[19:22]
    at = pl.ds(pl.multiple_of(place[0] * QUARTER, QUARTER), QUARTER)
    weight = (1.0 / sharpness_divisor) / col_total_ref[:, at]

    def fill(b, exps_ref, mates_ref):
        soft = down((1.0 / sharpness_divisor) / scals[b][1:2, :])
        hard = down(1.0 / scals[b][0:1, :])
        for j in range(QUARTER // 128):
            lanes = slice(j * 128, (j + 1) * 128)
            e = exps_ref[:, lanes]
            grads[b * ROWS : (b + 1) * ROWS, lanes] = (
                e * soft - mates_ref[:, lanes] * weight[:, lanes] * hard
            ).astype(BF16)

    for q in range(NY):

        @pl.when(place[0] == q)
        def _():
            fill(0, own_exps, own_mates[q])

    total = None
    for b in range(NY):
        if b:
            fill(b, exps[b - 1], mates[b - 1])
        part = jnp.dot(
            turned[b][4 * 128 : 5 * 128, :],
            grads[b * ROWS : (b + 1) * ROWS, :],
            preferred_element_type=F32,
        )
        total = part if total is None else total + part
    chunk_a[...] = total[:, : QUARTER // 2]
    chunk_b[...] = total[:, QUARTER // 2 :]


def first_chunk(place, own_exps, own_mates, far_blocks, scals, turned, col_total):
    half = jax.ShapeDtypeStruct((128, QUARTER // 2), F32)
    return pl.pallas_call(
        first_chunk_kernel,
        in_specs=[pl.BlockSpec(memory_space=pltpu.SMEM)] + [VM] * 20,
        out_specs=[VM] * 3,
        out_shape=[pltpu.VMEM((WIDE, QUARTER), BF16), half, half],
        compiler_params=params(6),
        cost_estimate=cost(2 * 128 * WIDE * QUARTER + 6 * WIDE * QUARTER, 2),
        name="first_chunk",
    )(
        place,
        in_vmem(own_exps),
        *[in_vmem(v) for v in own_mates],
        *[in_vmem(b[0]) for b in far_blocks],
        *[in_vmem(b[1]) for b in far_blocks],
        *scals,
        *[in_vmem(v) for v in turned],
        col_total,
    )


def chunks_kernel(offsets, t0, t1, t2, t3, grads, *outs):
    for o, out in zip(offsets, outs[-len(offsets) :]):
        total = None
        for b, turned in enumerate((t0, t1, t2, t3)):
            part = jnp.dot(
                turned[o * 128 : (o + 1) * 128, :],
                grads[b * ROWS : (b + 1) * ROWS, :],
                preferred_element_type=F32,
            )
            total = part if total is None else total + part
        out[...] = total


def chunks(turned, grads, offsets):
    return pl.pallas_call(
        functools.partial(chunks_kernel, offsets),
        in_specs=[VM] * 5,
        out_specs=[VM] * len(offsets),
        out_shape=[jax.ShapeDtypeStruct((128, QUARTER), F32)] * len(offsets),
        compiler_params=params(5),
        cost_estimate=cost(2 * 128 * WIDE * QUARTER * len(offsets) // 4, 1),
        name="chunks",
    )(*[in_vmem(v) for v in turned], in_vmem(grads))


def gather_kernel(place, r0, r1, r2, r3, out_ref, flag_ref):
    flag_ref[...] = jnp.zeros_like(flag_ref)
    for o, ref in enumerate((r0, r1, r2, r3)):
        quarter = lax.rem(place[0] + NY - o, NY)
        out_ref[:, pl.ds(pl.multiple_of(quarter * QUARTER, QUARTER), QUARTER)] = ref[...]


def gather_quarters(place, quarters):
    return pl.pallas_call(
        gather_kernel,
        in_specs=[pl.BlockSpec(memory_space=pltpu.SMEM)] + [VM] * 4,
        out_specs=[VM, VM],
        out_shape=[
            jax.ShapeDtypeStruct((32, COLS), F32),
            jax.ShapeDtypeStruct((1, 128), F32),
        ],
        compiler_params=params(8),
        cost_estimate=cost(0, 1),
        name="gather_quarters",
    )(place, *quarters)


def finish_kernel(s0, s1, s2, s3, plain_ref, grad_ref, cost_ref):
    share = (s0[...] + s2[...]) + (s1[...] + s3[...])
    grad_ref[...] = share[:ROWS, :]
    for t in range(ROWS // 128):
        lanes = slice(t * 128, (t + 1) * 128)
        matched = share[ROWS + t : ROWS + t + 1, :]
        cost_ref[:, lanes] = jnp.log(plain_ref[:, lanes]) - matched * (1.0 / sharpness_divisor)


def finish_ordered(s0, s1, s2, s3, plain, after):
    def kernel(a, b, c, d, e, unread, grad_ref, cost_ref):
        finish_kernel(a, b, c, d, e, grad_ref, cost_ref)

    return pl.pallas_call(
        kernel,
        in_specs=[VM] * 5 + [ANY],
        out_specs=[VM, VM],
        out_shape=[
            jax.ShapeDtypeStruct((ROWS, 128), F32),
            jax.ShapeDtypeStruct((1, ROWS), F32),
        ],
        compiler_params=params(6),
        cost_estimate=cost(4 * ROWS * 128, 1),
        name="finish",
    )(s0, s1, s2, s3, plain, after)


def local(embed, prototypes, partner):
    dp, proto = lax.axis_index("dp"), lax.axis_index("proto")
    place = jnp.stack([dp // NZ, dp % NZ, proto // 2, proto % 2]).astype(jnp.int32)
    mate = (partner - dp * ROWS).astype(F32).reshape(1, ROWS)
    unit, pay = unit_rows(place, embed, mate)
    exps, scores, col_part, protos = first_scores(unit, prototypes)

    from_left, from_right = move_y(pay, 1), move_y(pay, -1)

    col_total = sum_dp(col_part, [from_left, from_right])
    low, high = second_hop(from_left, from_right, [col_total])
    far = jnp.concatenate([move_y(low, 1), move_y(high, -1)], axis=0)
    same = [from_left, far, from_right]
    crossed = [move_core(v) for v in same]
    row_total = sum_proto(row_sums(exps, col_total, True, []))
    plain = row_total[1:2]
    own_turned, xm, own_exps = own_block(place, unit, mate, exps)
    far_blocks = [far_block(place, v, w, protos) for v, w in zip(same, crossed)]
    mates = [mate_piece(xm, protos, q) for q in range(NY)]

    col_total = sum_dp(col_sums(exps, row_total, [], []), [], [far])
    row_total = sum_proto(row_sums(exps, col_total, False, crossed))
    col_total = sum_dp(col_sums(exps, row_total, mates, []), [far_blocks[2][3]], [far_blocks[0][3]])
    row_total = sum_proto(mate_row_sums(mates, col_total, [far_blocks[1][3]]))

    scal = jnp.concatenate([row_total, plain], axis=0)
    scals = [scal, move_y(scal, 1), move_y(scal, 2), move_y(scal, -1)]

    turned = [own_turned] + [b[2] for b in far_blocks]
    grads, up, back = first_chunk(
        place, own_exps, mates, far_blocks, scals, turned, col_total
    )
    half = QUARTER // 2
    up, back = move_z(up, 1), move_z(back, -1)
    c3, c5 = chunks(turned, grads, (3, 5))
    parts = embed_grad(
        place, (up, back), mates, col_total, row_total, plain, protos, embed, scores
    )
    up = jnp.concatenate([c3[:, :half] + up, c3[:, half:]], axis=1)
    back = jnp.concatenate([c5[:, :half], c5[:, half:] + back], axis=1)
    up, back = move_z(up, 1), move_z(back, -1)
    c2, c6 = chunks(turned, grads, (2, 6))
    up, back = add([up, c2], parts[:1]), add([back, c6], parts[:1])
    up, back = move_z(up, 1), move_z(back, -1)
    c1, c7 = chunks(turned, grads, (1, 7))
    up, back = up + c1, back + c7
    up, back = move_z(up, 1), move_z(back, -1)
    shares = [parts[o] + move_core(parts[NX + o]) for o in range(NX)]
    moved = [move_x(shares[o], o) for o in (1, 2, 3)]
    (c0,) = chunks(turned, grads, (0,))
    done = add([c0, up, back], [*shares, moved[0]])
    quarters = [done[:32]] + [move_y(done[32 * o : 32 * o + 32], o) for o in (1, 2, 3)]
    grad_protos, flag = gather_quarters(place, quarters)

    grad_embed, view_swapped_cost = finish_ordered(shares[0], *moved, plain, flag)
    return (grad_embed, grad_protos, view_swapped_cost.reshape(ROWS))


def solution(mesh):
    placed = (P("dp", None), P(None, "proto"), P("dp"))
    return jax.shard_map(
        local,
        mesh=mesh,
        in_specs=placed,
        out_specs=(P("dp", "proto"), P("dp", "proto"), P("dp")),
        check_vma=False,
    )
```

```python
import functools

import jax
import jax.numpy as jnp
from jax import lax
from jax.experimental import pallas as pl
from jax.experimental.pallas import tpu as pltpu
from jax.sharding import PartitionSpec as P

NY, NZ, NX = 4, 8, 4
ROWS, COLS, D = 512, 4096, 1024
WIDE, QUARTER, PAY = 2048, 1024, 264
F32, BF16 = jnp.float32, jnp.bfloat16
MIB = 1 << 20


code_eps = 0.05
sharpness_divisor = 0.1


def dp_pairs(f):
    pairs = []
    for y in range(NY):
        for z in range(NZ):
            to_y, to_z = f(y, z)
            pairs.append((y * NZ + z, (to_y % NY) * NZ + to_z % NZ))
    return pairs


def proto_pairs(f):
    pairs = []
    for x in range(NX):
        for core in range(2):
            to_x, to_core = f(x, core)
            pairs.append((x * 2 + core, (to_x % NX) * 2 + to_core % 2))
    return pairs


def move_y(v, off):
    return lax.ppermute(v, "dp", dp_pairs(lambda y, z: (y + off, z)))


def move_z(v, off):
    return lax.ppermute(v, "dp", dp_pairs(lambda y, z: (y, z + off)))


def move_x(v, off):
    return lax.ppermute(v, "proto", proto_pairs(lambda x, c: (x + off, c)))


def move_core(v):
    return lax.ppermute(v, "proto", proto_pairs(lambda x, c: (x, c + 1)))


def sum_y(v):
    return (v + move_y(v, 2)) + (move_y(v, 1) + move_y(v, -1))


def sum_z(v, after=(), early=()):
    left, right = move_z(v, 1), move_z(v, -1)
    two = add([v, right], early) if early else v + right
    three = left + two
    terms = [three, move_z(three, -3), move_z(two, 3)]
    if after:
        return add(terms, after)
    return terms[0] + (terms[1] + terms[2])


def sum_x(v):
    return (v + move_x(v, 2)) + (move_x(v, 1) + move_x(v, -1))


def sum_core(v):
    return v + move_core(v)


def sum_dp(v, after=(), early=()):
    return sum_y(sum_z(v, after, early))


def sum_proto(v):
    return sum_x(sum_core(v))


def in_vmem(v):
    return pltpu.with_memory_space_constraint(v, pltpu.VMEM)


def in_hbm(v):
    return pltpu.with_memory_space_constraint(v, pltpu.HBM)


VM = pl.BlockSpec(memory_space=pltpu.VMEM)
ANY = pl.BlockSpec(memory_space=pl.ANY)


def params(mib):
    return pltpu.CompilerParams(vmem_limit_bytes=mib * MIB)


def cost(flops, mib, exps=0):
    return pl.CostEstimate(flops=flops, bytes_accessed=mib * MIB, transcendentals=exps)


def unit_kernel(place, embed_ref, mate_ref, unit_ref, pay_ref):
    raw = embed_ref[...].astype(F32)
    scale = lax.rsqrt(jnp.sum(raw * raw, axis=1, keepdims=True) + 1e-06)
    unit_ref[...] = (raw * scale).astype(BF16)
    half = pl.ds(pl.multiple_of(place[3] * (ROWS // 2), ROWS // 2), ROWS // 2)
    pay_ref[: ROWS // 2, :] = unit_ref[half, :].astype(F32)
    pay_ref[ROWS // 2 :, :ROWS] = jnp.broadcast_to(mate_ref[...], (8, ROWS))
    pay_ref[ROWS // 2 :, ROWS:] = jnp.zeros((8, D - ROWS), F32)


def unit_rows(place, embed, mate):
    return pl.pallas_call(
        unit_kernel,
        in_specs=[pl.BlockSpec(memory_space=pltpu.SMEM), VM, VM],
        out_specs=[VM, VM],
        out_shape=[pltpu.VMEM((ROWS, D), BF16), jax.ShapeDtypeStruct((PAY, D), F32)],
        compiler_params=params(12),
        cost_estimate=cost(4 * ROWS * D, 3),
        name="unit_rows",
    )(place, embed, mate)


def scores_kernel(unit_ref, protos_ref, exps_ref, scores_ref, col_ref, protos_out):
    raw = protos_ref[...].astype(F32)
    scale = lax.rsqrt(jnp.sum(raw * raw, axis=0, keepdims=True) + 1e-06)
    unit_protos = (raw * scale).astype(BF16)
    scores = jnp.dot(unit_ref[...], unit_protos, preferred_element_type=F32)
    exps = jnp.exp(scores * (1.0 / sharpness_divisor))
    scores_ref[...] = scores
    width = scores.shape[1]
    at = pl.ds(pl.multiple_of(pl.program_id(0) * width, width), width)
    protos_out[:, at] = unit_protos
    exps_ref[:, at] = exps
    col_ref[:, at] = jnp.sum(exps * exps, axis=0, keepdims=True)


def first_scores(unit, prototypes, block=1024):
    return pl.pallas_call(
        scores_kernel,
        grid=(COLS // block,),
        in_specs=[VM, pl.BlockSpec((D, block), lambda j: (0, j))],
        out_specs=[VM, pl.BlockSpec((ROWS, block), lambda j: (0, j)), VM, VM],
        out_shape=[
            pltpu.VMEM((ROWS, COLS), F32),
            pltpu.HBM((ROWS, COLS), F32),
            jax.ShapeDtypeStruct((1, COLS), F32),
            pltpu.VMEM((D, COLS), BF16),
        ],
        compiler_params=params(24),
        cost_estimate=cost(2 * ROWS * COLS * D, 8, ROWS * COLS),
        name="first_scores",
    )(in_vmem(unit), in_hbm(prototypes))


def add_kernel(n, *refs):
    total = refs[0][...]
    for ref in refs[1:n]:
        total += ref[...]
    refs[-1][...] = total


def add(terms, after):
    return pl.pallas_call(
        functools.partial(add_kernel, len(terms)),
        in_specs=[VM] * len(terms) + [ANY] * len(after),
        out_specs=VM,
        out_shape=jax.ShapeDtypeStruct(terms[0].shape, F32),
        compiler_params=params(6),
        cost_estimate=cost(terms[0].size * len(terms), 1),
        name="add",
    )(*terms, *after)


def hop_kernel(left_ref, right_ref, *refs):
    low_ref, high_ref = refs[-2:]
    low_ref[...] = left_ref[:128, :]
    high_ref[...] = right_ref[128:, :]


def second_hop(left, right, after):
    return pl.pallas_call(
        hop_kernel,
        in_specs=[VM, VM] + [ANY] * len(after),
        out_specs=[VM, VM],
        out_shape=[
            jax.ShapeDtypeStruct((128, D), F32),
            jax.ShapeDtypeStruct((PAY - 128, D), F32),
        ],
        compiler_params=params(8),
        cost_estimate=cost(ROWS * D, 2),
        name="second_hop",
    )(left, right, *after)


def lanes_to_row(parts):
    return jnp.sum(jnp.concatenate(parts, axis=0).T, axis=0, keepdims=True)


def row_kernel(with_plain, exps_ref, col_total_ref, *refs):
    row_ref = refs[-1]
    weight = 1.0 / col_total_ref[...]
    rows = 64
    parts, plain_parts = [], []
    for i in range(ROWS // rows):
        total = jnp.zeros((rows, 128), F32)
        plain = jnp.zeros((rows, 128), F32)
        for j in range(COLS // 128):
            e = exps_ref[i * rows : (i + 1) * rows, j * 128 : (j + 1) * 128]
            total += (e * e) * weight[:, j * 128 : (j + 1) * 128]
            if with_plain:
                plain += e
        parts.append(total)
        plain_parts.append(plain)
    row_ref[0:1, :] = lanes_to_row(parts)
    if with_plain:
        row_ref[1:2, :] = lanes_to_row(plain_parts)


def row_sums(exps, col_total, with_plain, after):
    return pl.pallas_call(
        functools.partial(row_kernel, with_plain),
        in_specs=[VM, VM] + [ANY] * len(after),
        out_specs=VM,
        out_shape=jax.ShapeDtypeStruct((2 if with_plain else 1, ROWS), F32),
        compiler_params=params(6),
        cost_estimate=cost(3 * ROWS * COLS, 1),
        name="row_sums",
    )(in_vmem(exps), col_total, *after)


def mate_row_kernel(a0, a1, a2, a3, col_total_ref, *refs):
    row_ref = refs[-1]
    weight = 1.0 / col_total_ref[...]
    rows = 64
    parts = []
    for i in range(ROWS // rows):
        total = jnp.zeros((rows, 128), F32)
        for q, a in enumerate((a0, a1, a2, a3)):
            for j in range(QUARTER // 128):
                at = q * QUARTER + j * 128
                total += (
                    a[i * rows : (i + 1) * rows, j * 128 : (j + 1) * 128] * weight[:, at : at + 128]
                )
        parts.append(total)
    row_ref[...] = lanes_to_row(parts)


def mate_row_sums(mates, col_total, after):
    return pl.pallas_call(
        mate_row_kernel,
        in_specs=[VM] * 5 + [ANY] * len(after),
        out_specs=VM,
        out_shape=jax.ShapeDtypeStruct((1, ROWS), F32),
        compiler_params=params(6),
        cost_estimate=cost(2 * ROWS * COLS, 1),
        name="mate_row_sums",
    )(*[in_vmem(m) for m in mates], col_total, *after)


def col_kernel(exps_ref, row_total_ref, *refs):
    col_ref, weight_ref = refs[-2:]
    weight = 1.0 / row_total_ref[0:1, :]
    weight_ref[...] = jnp.broadcast_to(weight, (128, ROWS)).T
    for j in range(COLS // 128):
        e = exps_ref[:, j * 128 : (j + 1) * 128]
        col_ref[:, j * 128 : (j + 1) * 128] = jnp.sum(
            (e * e) * weight_ref[...], axis=0, keepdims=True
        )


def col_sums(exps, row_total, early, after):
    return pl.pallas_call(
        col_kernel,
        in_specs=[VM, VM] + [VM] * len(early) + [ANY] * len(after),
        out_specs=VM,
        out_shape=jax.ShapeDtypeStruct((1, COLS), F32),
        scratch_shapes=[pltpu.VMEM((ROWS, 128), F32)],
        compiler_params=params(6),
        cost_estimate=cost(3 * ROWS * COLS, 1),
        name="col_sums",
    )(in_vmem(exps), row_total, *[in_vmem(v) for v in early], *after)


def mate_rows(x, mate):
    pick = (lax.broadcasted_iota(jnp.int32, (ROWS, ROWS), 0).astype(F32) == mate).astype(BF16)
    return jnp.dot(pick, x, preferred_element_type=F32).astype(BF16)


def turn_rows(place, x, turned_ref, turn):
    turn[...] = x.T
    for o in range(NZ):
        for p in range(NY):
            to = lax.rem(place[0] + p, NY) * NZ + lax.rem(place[1] + o, NZ)
            at = o * 128 + p * 32
            turned_ref[at : at + 32, :] = turn[pl.ds(pl.multiple_of(to * 32, 32), 32), :]


def own_block_kernel(place, unit_ref, mate_ref, exps_ref, turned_ref, xm_ref, quarter_ref, turn):
    at = pl.ds(pl.multiple_of(place[0] * QUARTER, QUARTER), QUARTER)
    quarter_ref[...] = exps_ref[:, at]
    xm_ref[...] = mate_rows(unit_ref[...], mate_ref[...])
    turn_rows(place, unit_ref[...], turned_ref, turn)


def own_block(place, unit, mate, exps):
    return pl.pallas_call(
        own_block_kernel,
        in_specs=[pl.BlockSpec(memory_space=pltpu.SMEM), VM, VM, VM],
        out_specs=[VM, VM, VM],
        scratch_shapes=[pltpu.VMEM((D, ROWS), BF16)],
        out_shape=[
            pltpu.VMEM((D, ROWS), BF16),
            pltpu.VMEM((ROWS, D), BF16),
            pltpu.VMEM((ROWS, QUARTER), F32),
        ],
        compiler_params=params(7),
        cost_estimate=cost(2 * ROWS * ROWS * D, 4),
        name="own_block",
    )(place, in_vmem(unit), mate, in_vmem(exps))


def far_block_kernel(
    place, same_ref, other_ref, protos_ref, exps_ref, mates_ref, turned_ref, flag_ref, turn, held
):
    flag_ref[...] = jnp.zeros_like(flag_ref)
    half = ROWS // 2
    core = place[3]
    held[pl.ds(pl.multiple_of(core * half, half), half), :] = same_ref[:half, :].astype(BF16)
    held[pl.ds(pl.multiple_of((1 - core) * half, half), half), :] = other_ref[:half, :].astype(BF16)
    x = held[...]
    xm = mate_rows(x, same_ref[half : half + 1, :ROWS])
    for j in range(0, QUARTER, 256):
        at = pl.ds(pl.multiple_of(place[0] * QUARTER + j, 256), 256)
        protos = protos_ref[:, at]
        exps_ref[:, j : j + 256] = jnp.exp(
            jnp.dot(x, protos, preferred_element_type=F32) * (1.0 / sharpness_divisor)
        )
        mates_ref[:, j : j + 256] = jnp.exp(
            jnp.dot(xm, protos, preferred_element_type=F32) * (1.0 / code_eps)
        )
    turn_rows(place, x, turned_ref, turn)


def far_block(place, same, other, protos):
    return pl.pallas_call(
        far_block_kernel,
        in_specs=[pl.BlockSpec(memory_space=pltpu.SMEM), VM, VM, VM],
        out_specs=[VM] * 4,
        scratch_shapes=[pltpu.VMEM((D, ROWS), BF16), pltpu.VMEM((ROWS, D), BF16)],
        out_shape=[
            pltpu.VMEM((ROWS, QUARTER), F32),
            pltpu.VMEM((ROWS, QUARTER), F32),
            pltpu.VMEM((D, ROWS), BF16),
            jax.ShapeDtypeStruct((1, 128), F32),
        ],
        compiler_params=params(7),
        cost_estimate=cost(4 * ROWS * QUARTER * D, 4, 2 * ROWS * QUARTER),
        name="far_block",
    )(place, same, other, in_vmem(protos))


def mate_piece_kernel(q, xm_ref, protos_ref, mates_ref):
    for j in range(0, QUARTER, 256):
        protos = protos_ref[:, q * QUARTER + j : q * QUARTER + j + 256]
        mates_ref[:, j : j + 256] = jnp.exp(
            jnp.dot(xm_ref[...], protos, preferred_element_type=F32) * (1.0 / code_eps)
        )


def mate_piece(xm, protos, q):
    return pl.pallas_call(
        functools.partial(mate_piece_kernel, q),
        in_specs=[VM, VM],
        out_specs=VM,
        out_shape=pltpu.VMEM((ROWS, QUARTER), F32),
        compiler_params=params(6),
        cost_estimate=cost(2 * ROWS * QUARTER * D, 2, ROWS * QUARTER),
        name="mate_piece",
    )(in_vmem(xm), in_vmem(protos))


def down(row):
    return jnp.broadcast_to(row, (128, ROWS)).T


def embed_grad_kernel(place, *refs):
    mates, refs = refs[2:6], refs[6:]
    col_total_ref, row_total_ref, plain_ref, protos_ref, embed_ref, scores_ref = refs[:6]
    mine, other = refs[6 : 6 + NX], refs[6 + NX : 6 + 2 * NX]
    total, match, soft, hard, grads = refs[6 + 2 * NX :]
    soft[...] = down((1.0 / sharpness_divisor) / plain_ref[...])
    hard[...] = down(1.0 / row_total_ref[...])
    match[...] = jnp.zeros_like(match)
    width = 512
    for t in range(COLS // width):
        for j in range(width // 128):
            first = t * width + j * 128
            inside = first % QUARTER
            weight = 1.0 / col_total_ref[:, first : first + 128]
            targets = mates[first // QUARTER][:, inside : inside + 128] * weight * hard[...]
            scores = scores_ref[:, first : first + 128]
            match[...] += targets * scores
            grads[t % 2, :, j * 128 : (j + 1) * 128] = (
                jnp.exp(scores * (1.0 / sharpness_divisor)) * soft[...]
                - targets * (1.0 / sharpness_divisor)
            ).astype(BF16)
        part = lax.dot_general(
            grads[t % 2],
            protos_ref[:, t * width : (t + 1) * width],
            (((1,), (1,)), ((), ())),
            preferred_element_type=F32,
        )
        if t == 0:
            total[...] = part
        else:
            total[...] += part

    raw = embed_ref[...].astype(F32)
    term = total[...]
    scale = lax.rsqrt(jnp.sum(raw * raw, axis=1, keepdims=True) + 1e-06)
    inner = jnp.sum(raw * term, axis=1, keepdims=True)
    total[...] = scale * term - (scale * scale * scale * inner) * raw
    matched = jnp.sum(match[...].T, axis=0, keepdims=True)
    for o in range(NX):
        to = lax.rem(place[2] + o, NX) * 2
        for core, ref in ((place[3], mine[o]), (1 - place[3], other[o])):
            at = pl.ds(pl.multiple_of((to + core) * 128, 128), 128)
            ref[:ROWS, :] = total[:, at]
            ref[ROWS:, :] = jnp.zeros((8, 128), F32)
            for t in range(ROWS // 128):
                ref[ROWS + t : ROWS + t + 1, :] = matched[:, t * 128 : (t + 1) * 128]


def embed_grad(place, after, mates, col_total, row_total, plain, protos, embed, scores):
    column = pltpu.VMEM((ROWS, 128), F32)
    return pl.pallas_call(
        embed_grad_kernel,
        in_specs=[pl.BlockSpec(memory_space=pltpu.SMEM)] + [ANY] * 2 + [VM] * 10,
        out_specs=[VM] * (2 * NX),
        scratch_shapes=[
            pltpu.VMEM((ROWS, D), F32),
            column,
            column,
            column,
            pltpu.VMEM((2, ROWS, 512), BF16),
        ],
        out_shape=[jax.ShapeDtypeStruct((ROWS + 8, 128), F32)] * (2 * NX),
        compiler_params=params(12),
        cost_estimate=cost(ROWS * COLS * D // 4, 1, ROWS * COLS // 8),
        name="embed_grad",
    )(
        place,
        *after,
        *[in_vmem(m) for m in mates],
        col_total,
        row_total,
        plain,
        in_vmem(protos),
        embed,
        in_vmem(scores),
    )


def fill(exps, mates, scal_ref, weight, grads, row):
    soft = down((1.0 / sharpness_divisor) / scal_ref[1:2, :])
    hard = down(1.0 / scal_ref[0:1, :])
    for j in range(QUARTER // 128):
        lanes = slice(j * 128, (j + 1) * 128)
        grads[row : row + ROWS, lanes] = (
            exps[:, lanes] * soft - mates[:, lanes] * weight[:, lanes] * hard
        ).astype(BF16)


def own_weight(place, col_total_ref):
    at = pl.ds(pl.multiple_of(place[0] * QUARTER, QUARTER), QUARTER)
    return (1.0 / sharpness_divisor) / col_total_ref[:, at]


def own_chunk_kernel(place, exps, m0, m1, m2, m3, scal, turned, col_total_ref, grads, part):
    weight = own_weight(place, col_total_ref)
    for q, mates in enumerate((m0, m1, m2, m3)):

        @pl.when(place[0] == q)
        def _():
            fill(exps, mates, scal, weight, grads, 0)

    part[...] = jnp.dot(
        turned[4 * 128 : 5 * 128, :], grads[...], preferred_element_type=F32
    )


def own_chunk(place, own_exps, own_mates, scal, turned, col_total):
    return pl.pallas_call(
        own_chunk_kernel,
        in_specs=[pl.BlockSpec(memory_space=pltpu.SMEM)] + [VM] * 8,
        out_specs=[VM] * 2,
        out_shape=[
            pltpu.VMEM((ROWS, QUARTER), BF16),
            jax.ShapeDtypeStruct((128, QUARTER), F32),
        ],
        compiler_params=params(5),
        cost_estimate=cost(2 * 128 * ROWS * QUARTER, 1),
        name="own_chunk",
    )(
        place,
        in_vmem(own_exps),
        *[in_vmem(v) for v in own_mates],
        scal,
        in_vmem(turned),
        col_total,
    )


def first_chunk_kernel(place, *refs):
    exps, mates, scals, turned = refs[0:3], refs[3:6], refs[6:9], refs[9:12]
    col_total_ref, own_part, grads, chunk_a, chunk_b = refs[12:]
    weight = own_weight(place, col_total_ref)
    total = own_part[...]
    for b in range(NY - 1):
        fill(exps[b], mates[b], scals[b], weight, grads, b * ROWS)
        total += jnp.dot(
            turned[b][4 * 128 : 5 * 128, :],
            grads[b * ROWS : (b + 1) * ROWS, :],
            preferred_element_type=F32,
        )
    chunk_a[...] = total[:, : QUARTER // 2]
    chunk_b[...] = total[:, QUARTER // 2 :]


def first_chunk(place, far_blocks, scals, turned, col_total, own_part):
    half = jax.ShapeDtypeStruct((128, QUARTER // 2), F32)
    return pl.pallas_call(
        first_chunk_kernel,
        in_specs=[pl.BlockSpec(memory_space=pltpu.SMEM)] + [VM] * 14,
        out_specs=[VM] * 3,
        out_shape=[pltpu.VMEM((WIDE - ROWS, QUARTER), BF16), half, half],
        compiler_params=params(6),
        cost_estimate=cost(2 * 128 * WIDE * QUARTER + 6 * WIDE * QUARTER, 2),
        name="first_chunk",
    )(
        place,
        *[in_vmem(b[0]) for b in far_blocks],
        *[in_vmem(b[1]) for b in far_blocks],
        *scals,
        *[in_vmem(v) for v in turned],
        col_total,
        own_part,
    )


def chunks_kernel(offsets, t0, t1, t2, t3, own_grads, grads, *outs):
    for o, out in zip(offsets, outs[-len(offsets) :]):
        total = None
        for b, turned in enumerate((t0, t1, t2, t3)):
            part = jnp.dot(
                turned[o * 128 : (o + 1) * 128, :],
                grads[(b - 1) * ROWS : b * ROWS, :] if b else own_grads[...],
                preferred_element_type=F32,
            )
            total = part if total is None else total + part
        out[...] = total


def chunks(turned, grads, offsets):
    return pl.pallas_call(
        functools.partial(chunks_kernel, offsets),
        in_specs=[VM] * 6,
        out_specs=[VM] * len(offsets),
        out_shape=[jax.ShapeDtypeStruct((128, QUARTER), F32)] * len(offsets),
        compiler_params=params(5),
        cost_estimate=cost(2 * 128 * WIDE * QUARTER * len(offsets) // 4, 1),
        name="chunks",
    )(*[in_vmem(v) for v in turned], in_vmem(grads[0]), in_vmem(grads[1]))


def finish_kernel(place, r0, r1, r2, r3, s0, s1, s2, s3, plain_ref, protos_ref, grad_ref, cost_ref):
    for o, ref in enumerate((r0, r1, r2, r3)):
        quarter = lax.rem(place[0] + NY - o, NY)
        protos_ref[:, pl.ds(pl.multiple_of(quarter * QUARTER, QUARTER), QUARTER)] = ref[...]
    share = (s0[...] + s2[...]) + (s1[...] + s3[...])
    grad_ref[...] = share[:ROWS, :]
    for t in range(ROWS // 128):
        lanes = slice(t * 128, (t + 1) * 128)
        matched = share[ROWS + t : ROWS + t + 1, :]
        cost_ref[:, lanes] = jnp.log(plain_ref[:, lanes]) - matched * (1.0 / sharpness_divisor)


def finish(place, quarters, shares, plain):
    return pl.pallas_call(
        finish_kernel,
        in_specs=[pl.BlockSpec(memory_space=pltpu.SMEM)] + [VM] * 9,
        out_specs=[VM] * 3,
        out_shape=[
            jax.ShapeDtypeStruct((32, COLS), F32),
            jax.ShapeDtypeStruct((ROWS, 128), F32),
            jax.ShapeDtypeStruct((1, ROWS), F32),
        ],
        compiler_params=params(8),
        cost_estimate=cost(4 * ROWS * 128, 2),
        name="finish",
    )(place, *quarters, *shares, plain)


def local(embed, prototypes, partner):
    dp, proto = lax.axis_index("dp"), lax.axis_index("proto")
    place = jnp.stack([dp // NZ, dp % NZ, proto // 2, proto % 2]).astype(jnp.int32)
    mate = (partner - dp * ROWS).astype(F32).reshape(1, ROWS)
    unit, pay = unit_rows(place, embed, mate)
    exps, scores, col_part, protos = first_scores(unit, prototypes)

    from_left, from_right = move_y(pay, 1), move_y(pay, -1)

    col_total = sum_dp(col_part, [from_left, from_right])
    low, high = second_hop(from_left, from_right, [col_total])
    far = jnp.concatenate([move_y(low, 1), move_y(high, -1)], axis=0)
    same = [from_left, far, from_right]
    crossed = [move_core(v) for v in same]
    row_total = sum_proto(row_sums(exps, col_total, True, []))
    plain = row_total[1:2]
    own_turned, xm, own_exps = own_block(place, unit, mate, exps)
    far_blocks = [far_block(place, v, w, protos) for v, w in zip(same, crossed)]
    mates = [mate_piece(xm, protos, q) for q in range(NY)]

    col_total = sum_dp(col_sums(exps, row_total, [], []), [], [far])
    row_total = sum_proto(row_sums(exps, col_total, False, crossed))
    col_total = sum_dp(col_sums(exps, row_total, mates, []), [far_blocks[2][3]], [far_blocks[0][3]])
    row_total = sum_proto(mate_row_sums(mates, col_total, [far_blocks[1][3]]))

    scal = jnp.concatenate([row_total, plain], axis=0)
    scals = [scal, move_y(scal, 1), move_y(scal, 2), move_y(scal, -1)]

    turned = [own_turned] + [b[2] for b in far_blocks]
    own_grads, own_part = own_chunk(place, own_exps, mates, scal, own_turned, col_total)
    far_grads, up, back = first_chunk(
        place, far_blocks, scals[1:], turned[1:], col_total, own_part
    )
    grads = (own_grads, far_grads)
    half = QUARTER // 2
    up, back = move_z(up, 1), move_z(back, -1)
    c3, c5 = chunks(turned, grads, (3, 5))
    parts = embed_grad(
        place, (up, back), mates, col_total, row_total, plain, protos, embed, scores
    )
    up = jnp.concatenate([c3[:, :half] + up, c3[:, half:]], axis=1)
    back = jnp.concatenate([c5[:, :half], c5[:, half:] + back], axis=1)
    up, back = move_z(up, 1), move_z(back, -1)
    c2, c6 = chunks(turned, grads, (2, 6))
    up, back = add([up, c2], parts[:1]), add([back, c6], parts[:1])
    up, back = move_z(up, 1), move_z(back, -1)
    c1, c7 = chunks(turned, grads, (1, 7))
    up, back = up + c1, back + c7
    up, back = move_z(up, 1), move_z(back, -1)
    shares = [parts[o] + move_core(parts[NX + o]) for o in range(NX)]
    moved = [move_x(shares[o], o) for o in (1, 2, 3)]
    (c0,) = chunks(turned, grads, (0,))
    done = add([c0, up, back], [*shares, moved[0]])
    quarters = [done[:32]] + [move_y(done[32 * o : 32 * o + 32], o) for o in (1, 2, 3)]

    grad_protos, grad_embed, view_swapped_cost = finish(
        place, quarters, [shares[0], *moved], plain
    )
    return (grad_embed, grad_protos, view_swapped_cost.reshape(ROWS))


def solution(mesh):
    placed = (P("dp", None), P(None, "proto"), P("dp"))
    return jax.shard_map(
        local,
        mesh=mesh,
        in_specs=placed,
        out_specs=(P("dp", "proto"), P("dp", "proto"), P("dp")),
        check_vma=False,
    )
```

```python
import functools

import jax
import jax.numpy as jnp
from jax import lax
from jax.experimental import pallas as pl
from jax.experimental.pallas import tpu as pltpu
from jax.sharding import PartitionSpec as P

NY, NZ, NX = 4, 8, 4
ROWS, COLS, D = 512, 4096, 1024
WIDE, QUARTER, PAY = 2048, 1024, 264
F32, BF16 = jnp.float32, jnp.bfloat16
MIB = 1 << 20


code_eps = 0.05
sharpness_divisor = 0.1


def dp_pairs(f):
    pairs = []
    for y in range(NY):
        for z in range(NZ):
            to_y, to_z = f(y, z)
            pairs.append((y * NZ + z, (to_y % NY) * NZ + to_z % NZ))
    return pairs


def proto_pairs(f):
    pairs = []
    for x in range(NX):
        for core in range(2):
            to_x, to_core = f(x, core)
            pairs.append((x * 2 + core, (to_x % NX) * 2 + to_core % 2))
    return pairs


def move_y(v, off):
    return lax.ppermute(v, "dp", dp_pairs(lambda y, z: (y + off, z)))


def move_z(v, off):
    return lax.ppermute(v, "dp", dp_pairs(lambda y, z: (y, z + off)))


def move_x(v, off):
    return lax.ppermute(v, "proto", proto_pairs(lambda x, c: (x + off, c)))


def move_core(v):
    return lax.ppermute(v, "proto", proto_pairs(lambda x, c: (x, c + 1)))


def sum_y(v):
    return (v + move_y(v, 2)) + (move_y(v, 1) + move_y(v, -1))


def sum_z(v, after=(), early=()):
    left, right = move_z(v, 1), move_z(v, -1)
    two = add([v, right], early) if early else v + right
    three = left + two
    terms = [three, move_z(three, -3), move_z(two, 3)]
    if after:
        return add(terms, after)
    return terms[0] + (terms[1] + terms[2])


def sum_x(v):
    return (v + move_x(v, 2)) + (move_x(v, 1) + move_x(v, -1))


def sum_core(v):
    return v + move_core(v)


def sum_dp(v, after=(), early=()):
    return sum_y(sum_z(v, after, early))


def sum_proto(v):
    return sum_x(sum_core(v))


def in_vmem(v):
    return pltpu.with_memory_space_constraint(v, pltpu.VMEM)


def in_hbm(v):
    return pltpu.with_memory_space_constraint(v, pltpu.HBM)


VM = pl.BlockSpec(memory_space=pltpu.VMEM)
ANY = pl.BlockSpec(memory_space=pl.ANY)


def params(mib):
    return pltpu.CompilerParams(vmem_limit_bytes=mib * MIB)


def cost(flops, mib, exps=0):
    return pl.CostEstimate(flops=flops, bytes_accessed=mib * MIB, transcendentals=exps)


def unit_kernel(place, embed_ref, mate_ref, unit_ref, pay_ref):
    raw = embed_ref[...].astype(F32)
    scale = lax.rsqrt(jnp.sum(raw * raw, axis=1, keepdims=True) + 1e-06)
    unit_ref[...] = (raw * scale).astype(BF16)
    half = pl.ds(pl.multiple_of(place[3] * (ROWS // 2), ROWS // 2), ROWS // 2)
    pay_ref[: ROWS // 2, :] = unit_ref[half, :].astype(F32)
    pay_ref[ROWS // 2 :, :ROWS] = jnp.broadcast_to(mate_ref[...], (8, ROWS))
    pay_ref[ROWS // 2 :, ROWS:] = jnp.zeros((8, D - ROWS), F32)


def unit_rows(place, embed, mate):
    return pl.pallas_call(
        unit_kernel,
        in_specs=[pl.BlockSpec(memory_space=pltpu.SMEM), VM, VM],
        out_specs=[VM, VM],
        out_shape=[pltpu.VMEM((ROWS, D), BF16), jax.ShapeDtypeStruct((PAY, D), F32)],
        compiler_params=params(12),
        cost_estimate=cost(4 * ROWS * D, 3),
        name="unit_rows",
    )(place, embed, mate)


def scores_kernel(unit_ref, protos_ref, exps_ref, scores_ref, col_ref, protos_out):
    raw = protos_ref[...].astype(F32)
    scale = lax.rsqrt(jnp.sum(raw * raw, axis=0, keepdims=True) + 1e-06)
    unit_protos = (raw * scale).astype(BF16)
    scores = jnp.dot(unit_ref[...], unit_protos, preferred_element_type=F32)
    exps = jnp.exp(scores * (1.0 / sharpness_divisor))
    scores_ref[...] = scores
    width = scores.shape[1]
    at = pl.ds(pl.multiple_of(pl.program_id(0) * width, width), width)
    protos_out[:, at] = unit_protos
    exps_ref[:, at] = exps
    col_ref[:, at] = jnp.sum(exps * exps, axis=0, keepdims=True)


def first_scores(unit, prototypes, block=1024):
    return pl.pallas_call(
        scores_kernel,
        grid=(COLS // block,),
        in_specs=[VM, pl.BlockSpec((D, block), lambda j: (0, j))],
        out_specs=[VM, pl.BlockSpec((ROWS, block), lambda j: (0, j)), VM, VM],
        out_shape=[
            pltpu.VMEM((ROWS, COLS), F32),
            pltpu.HBM((ROWS, COLS), F32),
            jax.ShapeDtypeStruct((1, COLS), F32),
            pltpu.VMEM((D, COLS), BF16),
        ],
        compiler_params=params(24),
        cost_estimate=cost(2 * ROWS * COLS * D, 8, ROWS * COLS),
        name="first_scores",
    )(in_vmem(unit), in_hbm(prototypes))


def add_kernel(n, *refs):
    total = refs[0][...]
    for ref in refs[1:n]:
        total += ref[...]
    refs[-1][...] = total


def add(terms, after):
    return pl.pallas_call(
        functools.partial(add_kernel, len(terms)),
        in_specs=[VM] * len(terms) + [ANY] * len(after),
        out_specs=VM,
        out_shape=jax.ShapeDtypeStruct(terms[0].shape, F32),
        compiler_params=params(6),
        cost_estimate=cost(terms[0].size * len(terms), 1),
        name="add",
    )(*terms, *after)


def hop_kernel(left_ref, right_ref, *refs):
    low_ref, high_ref = refs[-2:]
    low_ref[...] = left_ref[:128, :]
    high_ref[...] = right_ref[128:, :]


def second_hop(left, right, after):
    return pl.pallas_call(
        hop_kernel,
        in_specs=[VM, VM] + [ANY] * len(after),
        out_specs=[VM, VM],
        out_shape=[
            jax.ShapeDtypeStruct((128, D), F32),
            jax.ShapeDtypeStruct((PAY - 128, D), F32),
        ],
        compiler_params=params(8),
        cost_estimate=cost(ROWS * D, 2),
        name="second_hop",
    )(left, right, *after)


def lanes_to_row(parts):
    return jnp.sum(jnp.concatenate(parts, axis=0).T, axis=0, keepdims=True)


def row_kernel(with_plain, exps_ref, col_total_ref, *refs):
    row_ref = refs[-1]
    weight = 1.0 / col_total_ref[...]
    rows = 64
    parts, plain_parts = [], []
    for i in range(ROWS // rows):
        total = jnp.zeros((rows, 128), F32)
        plain = jnp.zeros((rows, 128), F32)
        for j in range(COLS // 128):
            e = exps_ref[i * rows : (i + 1) * rows, j * 128 : (j + 1) * 128]
            total += (e * e) * weight[:, j * 128 : (j + 1) * 128]
            if with_plain:
                plain += e
        parts.append(total)
        plain_parts.append(plain)
    row_ref[0:1, :] = lanes_to_row(parts)
    if with_plain:
        row_ref[1:2, :] = lanes_to_row(plain_parts)


def row_sums(exps, col_total, with_plain, after):
    return pl.pallas_call(
        functools.partial(row_kernel, with_plain),
        in_specs=[VM, VM] + [ANY] * len(after),
        out_specs=VM,
        out_shape=jax.ShapeDtypeStruct((2 if with_plain else 1, ROWS), F32),
        compiler_params=params(6),
        cost_estimate=cost(3 * ROWS * COLS, 1),
        name="row_sums",
    )(in_vmem(exps), col_total, *after)


def mate_row_kernel(a0, a1, a2, a3, col_total_ref, *refs):
    row_ref = refs[-1]
    weight = 1.0 / col_total_ref[...]
    rows = 64
    parts = []
    for i in range(ROWS // rows):
        total = jnp.zeros((rows, 128), F32)
        for q, a in enumerate((a0, a1, a2, a3)):
            for j in range(QUARTER // 128):
                at = q * QUARTER + j * 128
                total += (
                    a[i * rows : (i + 1) * rows, j * 128 : (j + 1) * 128] * weight[:, at : at + 128]
                )
        parts.append(total)
    row_ref[...] = lanes_to_row(parts)


def mate_row_sums(mates, col_total, after):
    return pl.pallas_call(
        mate_row_kernel,
        in_specs=[VM] * 5 + [ANY] * len(after),
        out_specs=VM,
        out_shape=jax.ShapeDtypeStruct((1, ROWS), F32),
        compiler_params=params(6),
        cost_estimate=cost(2 * ROWS * COLS, 1),
        name="mate_row_sums",
    )(*[in_vmem(m) for m in mates], col_total, *after)


def col_kernel(exps_ref, row_total_ref, *refs):
    col_ref, weight_ref = refs[-2:]
    weight = 1.0 / row_total_ref[0:1, :]
    weight_ref[...] = jnp.broadcast_to(weight, (128, ROWS)).T
    for j in range(COLS // 128):
        e = exps_ref[:, j * 128 : (j + 1) * 128]
        col_ref[:, j * 128 : (j + 1) * 128] = jnp.sum(
            (e * e) * weight_ref[...], axis=0, keepdims=True
        )


def col_sums(exps, row_total, early, after):
    return pl.pallas_call(
        col_kernel,
        in_specs=[VM, VM] + [VM] * len(early) + [ANY] * len(after),
        out_specs=VM,
        out_shape=jax.ShapeDtypeStruct((1, COLS), F32),
        scratch_shapes=[pltpu.VMEM((ROWS, 128), F32)],
        compiler_params=params(6),
        cost_estimate=cost(3 * ROWS * COLS, 1),
        name="col_sums",
    )(in_vmem(exps), row_total, *[in_vmem(v) for v in early], *after)


def mate_rows(x, mate):
    pick = (lax.broadcasted_iota(jnp.int32, (ROWS, ROWS), 0).astype(F32) == mate).astype(BF16)
    return jnp.dot(pick, x, preferred_element_type=F32).astype(BF16)


def turn_rows(place, x, turned_ref, turn):
    turn[...] = x.T
    for o in range(NZ):
        for p in range(NY):
            to = lax.rem(place[0] + p, NY) * NZ + lax.rem(place[1] + o, NZ)
            at = o * 128 + p * 32
            turned_ref[at : at + 32, :] = turn[pl.ds(pl.multiple_of(to * 32, 32), 32), :]


def own_block_kernel(place, unit_ref, mate_ref, exps_ref, turned_ref, xm_ref, quarter_ref, turn):
    at = pl.ds(pl.multiple_of(place[0] * QUARTER, QUARTER), QUARTER)
    quarter_ref[...] = exps_ref[:, at]
    xm_ref[...] = mate_rows(unit_ref[...], mate_ref[...])
    turn_rows(place, unit_ref[...], turned_ref, turn)


def own_block(place, unit, mate, exps):
    return pl.pallas_call(
        own_block_kernel,
        in_specs=[pl.BlockSpec(memory_space=pltpu.SMEM), VM, VM, VM],
        out_specs=[VM, VM, VM],
        scratch_shapes=[pltpu.VMEM((D, ROWS), BF16)],
        out_shape=[
            pltpu.VMEM((D, ROWS), BF16),
            pltpu.VMEM((ROWS, D), BF16),
            pltpu.VMEM((ROWS, QUARTER), F32),
        ],
        compiler_params=params(7),
        cost_estimate=cost(2 * ROWS * ROWS * D, 4),
        name="own_block",
    )(place, in_vmem(unit), mate, in_vmem(exps))


def far_block_kernel(
    place, same_ref, other_ref, protos_ref, exps_ref, mates_ref, turned_ref, flag_ref, turn, held
):
    flag_ref[...] = jnp.zeros_like(flag_ref)
    half = ROWS // 2
    core = place[3]
    held[pl.ds(pl.multiple_of(core * half, half), half), :] = same_ref[:half, :].astype(BF16)
    held[pl.ds(pl.multiple_of((1 - core) * half, half), half), :] = other_ref[:half, :].astype(BF16)
    x = held[...]
    xm = mate_rows(x, same_ref[half : half + 1, :ROWS])
    for j in range(0, QUARTER, 256):
        at = pl.ds(pl.multiple_of(place[0] * QUARTER + j, 256), 256)
        protos = protos_ref[:, at]
        exps_ref[:, j : j + 256] = jnp.exp(
            jnp.dot(x, protos, preferred_element_type=F32) * (1.0 / sharpness_divisor)
        )
        mates_ref[:, j : j + 256] = jnp.exp(
            jnp.dot(xm, protos, preferred_element_type=F32) * (1.0 / code_eps)
        )
    turn_rows(place, x, turned_ref, turn)


def far_block(place, same, other, protos):
    return pl.pallas_call(
        far_block_kernel,
        in_specs=[pl.BlockSpec(memory_space=pltpu.SMEM), VM, VM, VM],
        out_specs=[VM] * 4,
        scratch_shapes=[pltpu.VMEM((D, ROWS), BF16), pltpu.VMEM((ROWS, D), BF16)],
        out_shape=[
            pltpu.VMEM((ROWS, QUARTER), F32),
            pltpu.VMEM((ROWS, QUARTER), F32),
            pltpu.VMEM((D, ROWS), BF16),
            jax.ShapeDtypeStruct((1, 128), F32),
        ],
        compiler_params=params(7),
        cost_estimate=cost(4 * ROWS * QUARTER * D, 4, 2 * ROWS * QUARTER),
        name="far_block",
    )(place, same, other, in_vmem(protos))


def mate_piece_kernel(q, xm_ref, protos_ref, mates_ref):
    for j in range(0, QUARTER, 256):
        protos = protos_ref[:, q * QUARTER + j : q * QUARTER + j + 256]
        mates_ref[:, j : j + 256] = jnp.exp(
            jnp.dot(xm_ref[...], protos, preferred_element_type=F32) * (1.0 / code_eps)
        )


def mate_piece(xm, protos, q):
    return pl.pallas_call(
        functools.partial(mate_piece_kernel, q),
        in_specs=[VM, VM],
        out_specs=VM,
        out_shape=pltpu.VMEM((ROWS, QUARTER), F32),
        compiler_params=params(6),
        cost_estimate=cost(2 * ROWS * QUARTER * D, 2, ROWS * QUARTER),
        name="mate_piece",
    )(in_vmem(xm), in_vmem(protos))


def down(row):
    return jnp.broadcast_to(row, (128, ROWS)).T


def embed_grad_kernel(place, *refs):
    mates, refs = refs[2:6], refs[6:]
    col_total_ref, row_total_ref, plain_ref, protos_ref, embed_ref, scores_ref = refs[:6]
    mine, other = refs[6 : 6 + NX], refs[6 + NX : 6 + 2 * NX]
    total, match, soft, hard, grads = refs[6 + 2 * NX :]
    soft[...] = down((1.0 / sharpness_divisor) / plain_ref[...])
    hard[...] = down(1.0 / row_total_ref[...])
    match[...] = jnp.zeros_like(match)
    width = 512
    for t in range(COLS // width):
        for j in range(width // 128):
            first = t * width + j * 128
            inside = first % QUARTER
            weight = 1.0 / col_total_ref[:, first : first + 128]
            targets = mates[first // QUARTER][:, inside : inside + 128] * weight * hard[...]
            scores = scores_ref[:, first : first + 128]
            match[...] += targets * scores
            grads[t % 2, :, j * 128 : (j + 1) * 128] = (
                jnp.exp(scores * (1.0 / sharpness_divisor)) * soft[...]
                - targets * (1.0 / sharpness_divisor)
            ).astype(BF16)
        part = lax.dot_general(
            grads[t % 2],
            protos_ref[:, t * width : (t + 1) * width],
            (((1,), (1,)), ((), ())),
            preferred_element_type=F32,
        )
        if t == 0:
            total[...] = part
        else:
            total[...] += part

    raw = embed_ref[...].astype(F32)
    term = total[...]
    scale = lax.rsqrt(jnp.sum(raw * raw, axis=1, keepdims=True) + 1e-06)
    inner = jnp.sum(raw * term, axis=1, keepdims=True)
    total[...] = scale * term - (scale * scale * scale * inner) * raw
    matched = jnp.sum(match[...].T, axis=0, keepdims=True)
    for o in range(NX):
        to = lax.rem(place[2] + o, NX) * 2
        for core, ref in ((place[3], mine[o]), (1 - place[3], other[o])):
            at = pl.ds(pl.multiple_of((to + core) * 128, 128), 128)
            ref[:ROWS, :] = total[:, at]
            ref[ROWS:, :] = jnp.zeros((8, 128), F32)
            for t in range(ROWS // 128):
                ref[ROWS + t : ROWS + t + 1, :] = matched[:, t * 128 : (t + 1) * 128]


def embed_grad(place, after, mates, col_total, row_total, plain, protos, embed, scores):
    column = pltpu.VMEM((ROWS, 128), F32)
    return pl.pallas_call(
        embed_grad_kernel,
        in_specs=[pl.BlockSpec(memory_space=pltpu.SMEM)] + [ANY] * 2 + [VM] * 10,
        out_specs=[VM] * (2 * NX),
        scratch_shapes=[
            pltpu.VMEM((ROWS, D), F32),
            column,
            column,
            column,
            pltpu.VMEM((2, ROWS, 512), BF16),
        ],
        out_shape=[jax.ShapeDtypeStruct((ROWS + 8, 128), F32)] * (2 * NX),
        compiler_params=params(12),
        cost_estimate=cost(ROWS * COLS * D // 4, 1, ROWS * COLS // 8),
        name="embed_grad",
    )(
        place,
        *after,
        *[in_vmem(m) for m in mates],
        col_total,
        row_total,
        plain,
        in_vmem(protos),
        embed,
        in_vmem(scores),
    )


def fill(exps, mates, scal_ref, weight, grads, row):
    soft = down((1.0 / sharpness_divisor) / scal_ref[1:2, :])
    hard = down(1.0 / scal_ref[0:1, :])
    for j in range(QUARTER // 128):
        lanes = slice(j * 128, (j + 1) * 128)
        grads[row : row + ROWS, lanes] = (
            exps[:, lanes] * soft - mates[:, lanes] * weight[:, lanes] * hard
        ).astype(BF16)


def own_weight(place, col_total_ref):
    at = pl.ds(pl.multiple_of(place[0] * QUARTER, QUARTER), QUARTER)
    return (1.0 / sharpness_divisor) / col_total_ref[:, at]


def own_chunk_kernel(place, exps, m0, m1, m2, m3, scal, turned, col_total_ref, grads, part):
    weight = own_weight(place, col_total_ref)
    for q, mates in enumerate((m0, m1, m2, m3)):

        @pl.when(place[0] == q)
        def _():
            fill(exps, mates, scal, weight, grads, 0)

    part[...] = jnp.dot(
        turned[4 * 128 : 5 * 128, :], grads[...], preferred_element_type=F32
    )


def own_chunk(place, own_exps, own_mates, scal, turned, col_total):
    return pl.pallas_call(
        own_chunk_kernel,
        in_specs=[pl.BlockSpec(memory_space=pltpu.SMEM)] + [VM] * 8,
        out_specs=[VM] * 2,
        out_shape=[
            pltpu.VMEM((ROWS, QUARTER), BF16),
            jax.ShapeDtypeStruct((128, QUARTER), F32),
        ],
        compiler_params=params(5),
        cost_estimate=cost(2 * 128 * ROWS * QUARTER, 1),
        name="own_chunk",
    )(
        place,
        in_vmem(own_exps),
        *[in_vmem(v) for v in own_mates],
        scal,
        in_vmem(turned),
        col_total,
    )


def first_chunk_kernel(place, *refs):
    exps, mates, scals, turned = refs[0:3], refs[3:6], refs[6:9], refs[9:12]
    col_total_ref, own_part, grads, chunk_a, chunk_b = refs[12:]
    weight = own_weight(place, col_total_ref)
    total = own_part[...]
    for b in range(NY - 1):
        fill(exps[b], mates[b], scals[b], weight, grads, b * ROWS)
        total += jnp.dot(
            turned[b][4 * 128 : 5 * 128, :],
            grads[b * ROWS : (b + 1) * ROWS, :],
            preferred_element_type=F32,
        )
    chunk_a[...] = total[:, : QUARTER // 2]
    chunk_b[...] = total[:, QUARTER // 2 :]


def first_chunk(place, far_blocks, scals, turned, col_total, own_part):
    half = jax.ShapeDtypeStruct((128, QUARTER // 2), F32)
    return pl.pallas_call(
        first_chunk_kernel,
        in_specs=[pl.BlockSpec(memory_space=pltpu.SMEM)] + [VM] * 14,
        out_specs=[VM] * 3,
        out_shape=[pltpu.VMEM((WIDE - ROWS, QUARTER), BF16), half, half],
        compiler_params=params(6),
        cost_estimate=cost(2 * 128 * WIDE * QUARTER + 6 * WIDE * QUARTER, 2),
        name="first_chunk",
    )(
        place,
        *[in_vmem(b[0]) for b in far_blocks],
        *[in_vmem(b[1]) for b in far_blocks],
        *scals,
        *[in_vmem(v) for v in turned],
        col_total,
        own_part,
    )


def chunks_kernel(offsets, t0, t1, t2, t3, own_grads, grads, *outs):
    for o, out in zip(offsets, outs[-len(offsets) :]):
        total = None
        for b, turned in enumerate((t0, t1, t2, t3)):
            part = jnp.dot(
                turned[o * 128 : (o + 1) * 128, :],
                grads[(b - 1) * ROWS : b * ROWS, :] if b else own_grads[...],
                preferred_element_type=F32,
            )
            total = part if total is None else total + part
        out[...] = total


def chunks(turned, grads, offsets):
    return pl.pallas_call(
        functools.partial(chunks_kernel, offsets),
        in_specs=[VM] * 6,
        out_specs=[VM] * len(offsets),
        out_shape=[jax.ShapeDtypeStruct((128, QUARTER), F32)] * len(offsets),
        compiler_params=params(5),
        cost_estimate=cost(2 * 128 * WIDE * QUARTER * len(offsets) // 4, 1),
        name="chunks",
    )(*[in_vmem(v) for v in turned], in_vmem(grads[0]), in_vmem(grads[1]))


def finish_kernel(place, r0, r1, r2, r3, s0, s1, s2, s3, plain_ref, protos_ref, grad_ref, cost_ref):
    for o, ref in enumerate((r0, r1, r2, r3)):
        quarter = lax.rem(place[0] + NY - o, NY)
        protos_ref[:, pl.ds(pl.multiple_of(quarter * QUARTER, QUARTER), QUARTER)] = ref[...]
    share = (s0[...] + s2[...]) + (s1[...] + s3[...])
    grad_ref[...] = share[:ROWS, :]
    for t in range(ROWS // 128):
        lanes = slice(t * 128, (t + 1) * 128)
        matched = share[ROWS + t : ROWS + t + 1, :]
        cost_ref[:, lanes] = jnp.log(plain_ref[:, lanes]) - matched * (1.0 / sharpness_divisor)


def finish(place, quarters, shares, plain):
    return pl.pallas_call(
        finish_kernel,
        in_specs=[pl.BlockSpec(memory_space=pltpu.SMEM)] + [VM] * 9,
        out_specs=[VM] * 3,
        out_shape=[
            jax.ShapeDtypeStruct((32, COLS), F32),
            jax.ShapeDtypeStruct((ROWS, 128), F32),
            jax.ShapeDtypeStruct((1, ROWS), F32),
        ],
        compiler_params=params(8),
        cost_estimate=cost(4 * ROWS * 128, 2),
        name="finish",
    )(place, *quarters, *shares, plain)


def local(embed, prototypes, partner):
    dp, proto = lax.axis_index("dp"), lax.axis_index("proto")
    place = jnp.stack([dp // NZ, dp % NZ, proto // 2, proto % 2]).astype(jnp.int32)
    mate = (partner - dp * ROWS).astype(F32).reshape(1, ROWS)
    unit, pay = unit_rows(place, embed, mate)
    exps, scores, col_part, protos = first_scores(unit, prototypes)

    from_left, from_right = move_y(pay, 1), move_y(pay, -1)

    col_total = sum_dp(col_part, [from_left, from_right])
    row_part = row_sums(exps, col_total, True, [])
    low, high = second_hop(from_left, from_right, [row_part])
    far = jnp.concatenate([move_y(low, 1), move_y(high, -1)], axis=0)
    same = [from_left, far, from_right]
    crossed = [move_core(v) for v in same]
    row_total = sum_proto(row_part)
    plain = row_total[1:2]
    own_turned, xm, own_exps = own_block(place, unit, mate, exps)
    far_blocks = [far_block(place, v, w, protos) for v, w in zip(same, crossed)]
    mates = [mate_piece(xm, protos, q) for q in range(NY)]

    col_total = sum_dp(col_sums(exps, row_total, [], []), [], [far])
    row_total = sum_proto(row_sums(exps, col_total, False, crossed))
    col_total = sum_dp(col_sums(exps, row_total, mates, []), [far_blocks[2][3]], [far_blocks[0][3]])
    row_total = sum_proto(mate_row_sums(mates, col_total, [far_blocks[1][3]]))

    scal = jnp.concatenate([row_total, plain], axis=0)
    scals = [scal, move_y(scal, 1), move_y(scal, 2), move_y(scal, -1)]

    turned = [own_turned] + [b[2] for b in far_blocks]
    own_grads, own_part = own_chunk(place, own_exps, mates, scal, own_turned, col_total)
    far_grads, up, back = first_chunk(
        place, far_blocks, scals[1:], turned[1:], col_total, own_part
    )
    grads = (own_grads, far_grads)
    half = QUARTER // 2
    up, back = move_z(up, 1), move_z(back, -1)
    c3, c5 = chunks(turned, grads, (3, 5))
    parts = embed_grad(
        place, (up, back), mates, col_total, row_total, plain, protos, embed, scores
    )
    up = jnp.concatenate([c3[:, :half] + up, c3[:, half:]], axis=1)
    back = jnp.concatenate([c5[:, :half], c5[:, half:] + back], axis=1)
    up, back = move_z(up, 1), move_z(back, -1)
    c2, c6 = chunks(turned, grads, (2, 6))
    up, back = add([up, c2], parts[:1]), add([back, c6], parts[:1])
    up, back = move_z(up, 1), move_z(back, -1)
    c1, c7 = chunks(turned, grads, (1, 7))
    up, back = up + c1, back + c7
    up, back = move_z(up, 1), move_z(back, -1)
    shares = [parts[o] + move_core(parts[NX + o]) for o in range(NX)]
    moved = [move_x(shares[o], o) for o in (1, 2, 3)]
    (c0,) = chunks(turned, grads, (0,))
    done = add([c0, up, back], [*shares, moved[0]])
    quarters = [done[:32]] + [move_y(done[32 * o : 32 * o + 32], o) for o in (1, 2, 3)]

    grad_protos, grad_embed, view_swapped_cost = finish(
        place, quarters, [shares[0], *moved], plain
    )
    return (grad_embed, grad_protos, view_swapped_cost.reshape(ROWS))


def solution(mesh):
    placed = (P("dp", None), P(None, "proto"), P("dp"))
    return jax.shard_map(
        local,
        mesh=mesh,
        in_specs=placed,
        out_specs=(P("dp", "proto"), P("dp", "proto"), P("dp")),
        check_vma=False,
    )
```
